32 devices in a mesh: groups: 2 (over y), dp: 4 (over z), mp: 2 (over x), pair: 2 (over core).
Axes of the slice: x: 2, y: 2, z: 4, core: 2. Of those that a mesh axis runs over, the one named last changes fastest.
Arguments:
- hidden: bfloat16 [2, 4096, 4096], P('pair', ('groups', 'dp')), parts along dimension 1, may hold values from -16 to 16
- document_labels: int32 [2, 8, 512], P('pair', ('groups', 'dp')), parts along dimension 1, may hold values from 0 to 63, never falling along the last dimension, each value on 1 to 16 neighbouring positions
- frozen_weight: bfloat16 [4096, 4096], P('dp', 'mp'), may hold values from -0.09375 to 0.09375
- adapter_down: bfloat16 [4096, 16], replicated, may hold values from -0.09375 to 0.09375
- adapter_up: bfloat16 [16, 4096], P(None, 'mp'), may hold values from -1.5 to 1.5
- norm_gain_vector: bfloat16 [4096], P('mp'), may hold values from 0.5 to 1.5
- negative_owner: int32 [2, 256, 4], P('pair', 'groups'), parts along dimension 1, may hold values from 0 to 3, as said below
- negative_pool_row: int32 [2, 256, 4], P('pair', 'groups'), parts along dimension 1, may hold values from 0 to 31
Outputs:
- losses: float32 [2, 256], P('pair', ('groups', 'dp')), parts along dimension 1
- doc_grads: float32 [2, 8, 64, 4096], P('pair', ('groups', 'dp'), None, 'mp'), parts along dimension 1
- lora_a_grad: float32 [8192, 16], P(('groups', 'mp')), parts along dimension 0
- lora_b_grad: float32 [32, 4096], P('groups', 'mp'), parts along dimension 0
- gain_grad: float32 [8192], P(('groups', 'mp')), parts along dimension 0
The draws below stay inside these ranges and needn't reach their ends.
There are 2 independent parts, one for each index of `groups`. The reference program is written for one: setup_inputs(seed, part) draws one part's arguments, and reference() takes and returns one part's arrays. A program takes and returns all parts, laid end to end along the dimension named above; an argument that names none is the same for every part. Nothing has to cross between parts.
Inputs may be any that keep to these rules, and one draw needn't show every extreme that they name: `document_labels`: within a shard and side the ids never fall; every document 0 to 63 has 1 to 16 tokens, and one has exactly that many. `negative_owner`: among the 128 requests of the anchors of one shard (the rows of one device), no owner is named more than 32 times and some owner exactly 32 times; the 4 (owner, row) pairs of one anchor are distinct.
All inputs are finite; a program needn't handle non-finite values.
Results may differ from the reference program's by a relative error of at most 0.009.
Values may be sent and summed in bfloat16 or wider, within the bound.
No kernel may reach another device: no remote copies, remote signals or barrier semaphores. Data moves between devices by JAX's collectives and lax.ppermute only.
A program may use at most 128 MiB of HBM per device.

```python
import math
import jax
import jax.numpy as jnp
import numpy as np
from jax import lax

MODEL_WIDTH = 4096
ADAPTER_RANK = 16
TOK = 512
NQ = 32
H = 4
TOKENS = 2048
ANCHORS = 128
CAP = 32
N_DP = 4


def negative_lists(key):
    block_count = 2 * N_DP
    requests = NQ * H
    floor_len = max(1, min(CAP, (requests - CAP + N_DP - 2) // (N_DP - 1)))
    subkeys = jax.random.split(jax.random.fold_in(key, 5), 4)
    lengths = jax.random.randint(subkeys[0], (block_count, N_DP), floor_len, CAP + 1)
    lengths = lengths.at[:, 0].set(CAP)
    bounds = jnp.cumsum(lengths, axis=1)
    starts = bounds - lengths
    positions = jnp.arange(requests, dtype=jnp.int32)
    bucket = jnp.sum((positions[None, :, None] >= bounds[:, None, :]).astype(jnp.int32), axis=2)
    offsets = positions[None, :] - jnp.take_along_axis(starts, bucket, axis=1)
    ranking = jax.vmap(lambda sub: jax.random.permutation(sub, N_DP))(jax.random.split(subkeys[1], block_count))
    owners = jnp.take_along_axis(ranking, bucket, axis=1)
    perm_rows = jax.vmap(lambda sub: jax.random.permutation(sub, NQ))(jax.random.split(subkeys[2], block_count * N_DP)).reshape(block_count, N_DP, NQ)
    chosen = perm_rows[jnp.arange(block_count)[:, None], bucket, offsets]
    shuffle = jax.vmap(lambda sub: jax.random.permutation(sub, requests))(jax.random.split(subkeys[3], block_count))
    owners = jnp.take_along_axis(owners, shuffle, axis=1)
    chosen = jnp.take_along_axis(chosen, shuffle, axis=1)
    target_shape = (2, N_DP * NQ, H)
    return (owners.reshape(target_shape).astype(jnp.int32), chosen.reshape(target_shape).astype(jnp.int32))


def draw_negative_owner(key, part):
    owners, chosen = negative_lists(key)
    return owners


def draw_negative_pool_row(key, part):
    owners, chosen = negative_lists(key)
    return chosen


def draw_hidden(key, part):
    key = jax.random.fold_in(key, 11)
    first, second = jax.random.split(key, 2)
    ramp = jnp.sqrt(1.0 + 2.0 * jnp.arange(MODEL_WIDTH, dtype=jnp.float32) / MODEL_WIDTH)
    spread = jnp.exp(jax.random.uniform(second, (MODEL_WIDTH,), jnp.float32, 0.0, math.log(10.0)))
    columns = 0.3 * spread * ramp
    base = jnp.clip(jax.random.normal(first, (2, TOKENS, MODEL_WIDTH), jnp.float32), -3.0, 3.0)
    values = base * columns
    return values.astype(jnp.bfloat16)


def levels(rng, shape, shards, low, high):
    loudness, own = 1.0, jax.random.fold_in(rng, 6)
    for axis_at, blocks in shards:
        steps = jnp.exp(jax.random.uniform(jax.random.fold_in(own, axis_at), (blocks,), jnp.float32, low / len(shards), high / len(shards)))
        loudness = loudness * jnp.repeat(steps, shape[axis_at] // blocks).reshape([-1 if axis == axis_at else 1 for axis in range(len(shape))])
    return loudness


def length_profile(amount, total, reach, skew):
    loads = [(1 << 20) // math.isqrt(grade ** skew) + 1 for grade in range(2, amount + 1)]
    rest, holding = total - reach - (amount - 1), [1] * (amount - 1)
    while rest > 0:
        movable = [i for i in range(amount - 1) if holding[i] < reach]
        whole, remaining = sum([loads[i] for i in movable]), rest
        for i in movable:
            addition = min(reach - holding[i], max(1, remaining * loads[i] // whole), rest)
            holding[i] = holding[i] + addition
            rest = rest - addition
    return np.array([reach] + holding)


def uneven_parts(own_key, count, total, limit, skew):
    if count == 2:
        one = jax.random.randint(own_key, (), max(1, total - limit), min(limit, total - 1) + 1)
        return jnp.stack([one, total - one])
    sizes = jnp.asarray(length_profile(count, total, limit, skew), jnp.int32)
    couples = (count - 1) // 2
    source_of, taker = sizes[1:1 + 2 * couples:2], sizes[2:2 + 2 * couples:2]
    room = jnp.minimum(source_of - 1, limit - taker)
    passed = jax.random.randint(jax.random.fold_in(own_key, 1), (couples,), 0, 1 << 20) % (room + 1)
    sizes = sizes.at[1:1 + 2 * couples:2].set(source_of - passed).at[2:2 + 2 * couples:2].set(taker + passed)
    return sizes[jax.random.permutation(jax.random.fold_in(own_key, 2), count)]


def centred(key, extent, deviation, most, cuts=(), kind=jnp.bfloat16):
    result = jax.random.normal(key, extent, jnp.float32) * deviation
    if len(cuts) > 0:
        result = levels(key, extent, cuts, -0.22, 0.18) * result
    return jnp.clip(result, min=-most, max=most).astype(kind)


def setup_inputs(seed: int = 0, part: int = 0) -> dict:
    arg_keys = jax.random.split(jax.random.key(seed), 9)
    part_keys = jax.random.split(jax.random.fold_in(arg_keys[8], part), 9)
    hidden = draw_hidden(jax.random.fold_in(jax.random.fold_in(arg_keys[8], part), 71), part)
    document_labels = jax.vmap(lambda own: jnp.searchsorted(jnp.cumsum(uneven_parts(own, 2 * NQ, TOK, TOK // NQ, 2)), jnp.arange(TOK), side="right"))(jax.random.split(part_keys[1], 2 * N_DP)).reshape((2, N_DP, TOK)).astype(jnp.int32)
    frozen_weight = centred(arg_keys[2], (MODEL_WIDTH, MODEL_WIDTH), MODEL_WIDTH ** -0.5, 0.09375, ((0, 4), (1, 2)))
    adapter_down = centred(arg_keys[3], (MODEL_WIDTH, ADAPTER_RANK), MODEL_WIDTH ** -0.5, 0.09375)
    adapter_up = centred(arg_keys[4], (ADAPTER_RANK, MODEL_WIDTH), ADAPTER_RANK ** -0.5, 1.5, ((1, 2),))
    norm_gain_vector = jnp.clip(1.0 + 0.1 * jax.random.normal(arg_keys[5], (MODEL_WIDTH,), jnp.float32), 0.5, 1.5).astype(jnp.bfloat16)
    negative_owner = draw_negative_owner(jax.random.fold_in(jax.random.fold_in(arg_keys[8], part), 71), part)
    negative_pool_row = draw_negative_pool_row(jax.random.fold_in(jax.random.fold_in(arg_keys[8], part), 71), part)
    return dict(hidden=hidden, document_labels=document_labels, frozen_weight=frozen_weight, adapter_down=adapter_down, adapter_up=adapter_up, norm_gain_vector=norm_gain_vector, negative_owner=negative_owner, negative_pool_row=negative_pool_row)


inverse_temp = 50.0

def contrast(unit_rows, cand_side, owners, row_index):
    row_units = unit_rows[1 - cand_side, :, :NQ].reshape(ANCHORS, MODEL_WIDTH)
    cand_units = unit_rows[cand_side, :, :NQ].reshape(ANCHORS, MODEL_WIDTH)
    pool_rows = unit_rows[cand_side, :, NQ:]
    neg_units = pool_rows[owners, row_index]
    batch_scores = jnp.dot(row_units, cand_units.T, preferred_element_type=jnp.float32)
    neg_scores = jnp.einsum('nd,nhd->nh', row_units.astype(jnp.float32), neg_units.astype(jnp.float32), precision=lax.Precision.HIGHEST)
    logits = inverse_temp * jnp.concatenate([batch_scores, neg_scores], axis=1)
    exp_logits = jnp.exp(logits)
    denominator = lax.optimization_barrier(jnp.sum(exp_logits, axis=1))
    target = jnp.arange(ANCHORS + H, dtype=jnp.int32)[None, :] == jnp.arange(ANCHORS, dtype=jnp.int32)[:, None]
    losses = jnp.log(denominator) - lax.optimization_barrier(jnp.sum(jnp.where(target, logits, 0.0), axis=1))
    logit_grad = (inverse_temp * (exp_logits / denominator[:, None] - target.astype(jnp.float32))).astype(jnp.bfloat16)
    grad_batch = logit_grad[:, :ANCHORS]
    grad_neg = logit_grad[:, ANCHORS:].astype(jnp.float32)
    row_grad = jnp.dot(grad_batch, cand_units, preferred_element_type=jnp.float32)
    row_grad = row_grad + jnp.einsum('nh,nhd->nd', grad_neg, neg_units.astype(jnp.float32), precision=lax.Precision.HIGHEST)
    cand_grad = jnp.dot(grad_batch.T, row_units, preferred_element_type=jnp.float32)
    pool_grad = jnp.zeros((N_DP, NQ, MODEL_WIDTH), jnp.float32).at[owners, row_index].add(grad_neg[:, :, None] * row_units.astype(jnp.float32)[:, None, :])
    return (losses, row_grad, cand_grad, pool_grad)

def reference(hidden, document_labels, frozen_weight, adapter_down, adapter_up, norm_gain_vector, negative_owner, negative_pool_row):
    gain_f = norm_gain_vector.astype(jnp.float32)
    incoming_blocks = hidden.reshape(2 * N_DP, TOK, MODEL_WIDTH)
    index_lookup = document_labels.reshape(2 * N_DP, TOK)

    def encode_tokens(pair_in):
        input_tokens, doc_index = pair_in
        projected_states = jnp.dot(input_tokens, frozen_weight, preferred_element_type=jnp.float32)
        adapter_middle = jnp.dot(input_tokens, adapter_down, preferred_element_type=jnp.float32).astype(jnp.bfloat16)
        hidden_states = input_tokens.astype(jnp.float32) + projected_states + jnp.dot(adapter_middle, adapter_up, preferred_element_type=jnp.float32)
        inverse_root_mean = lax.rsqrt(lax.optimization_barrier(jnp.sum(hidden_states * hidden_states, axis=1)) / MODEL_WIDTH + 1e-05)
        normed = (hidden_states * inverse_root_mean[:, None] * gain_f).astype(jnp.bfloat16)
        member = doc_index[None, :] == jnp.arange(2 * NQ, dtype=jnp.int32)[:, None]
        token_counts = lax.optimization_barrier(jnp.sum(member.astype(jnp.float32), axis=1))
        mean_pooled = (jnp.dot(member.astype(jnp.bfloat16), normed, preferred_element_type=jnp.float32) / token_counts[:, None]).astype(jnp.bfloat16)
        return (hidden_states, inverse_root_mean, adapter_middle, mean_pooled, token_counts)
    hidden_states, inverse_root_mean, adapter_middle, mean_pooled, token_counts = lax.map(encode_tokens, (incoming_blocks, index_lookup))
    pooled_f = mean_pooled.astype(jnp.float32)
    document_norm = jnp.sqrt(lax.optimization_barrier(jnp.sum(pooled_f * pooled_f, axis=2)) + 1e-06)
    unit_embedding = pooled_f / document_norm[:, :, None]
    unit_rows = unit_embedding.astype(jnp.bfloat16).reshape(2, N_DP, 2 * NQ, MODEL_WIDTH)
    results = [contrast(unit_rows, side_c, negative_owner[side_c], negative_pool_row[side_c]) for side_c in (0, 1)]
    losses = jnp.stack([results[0][0], results[1][0]])
    grads = []
    for side_s in (0, 1):
        anchor_part = results[side_s][2].reshape(N_DP, NQ, MODEL_WIDTH) + results[1 - side_s][1].reshape(N_DP, NQ, MODEL_WIDTH)
        grads.append(jnp.concatenate([anchor_part, results[side_s][3]], axis=1))
    doc_grads = jnp.stack(grads)
    gradient_blocks = doc_grads.reshape(2 * N_DP, 2 * NQ, MODEL_WIDTH)
    adapter_up_wide32 = adapter_up.astype(jnp.float32)

    def reverse_pass(carry, items):
        a_acc, b_acc, g_acc = carry
        input_tokens, doc_index, state_blk, rms_blk, mid_blk, grad_blk, unit_blk, norm_blk, count_blk = items
        member_f = (doc_index[None, :] == jnp.arange(2 * NQ, dtype=jnp.int32)[:, None]).astype(jnp.float32)
        unit_dots = lax.optimization_barrier(jnp.sum(unit_blk * grad_blk, axis=1))
        per_doc = (grad_blk - unit_blk * unit_dots[:, None]) / (norm_blk * count_blk)[:, None]
        tok_grad = jnp.dot(member_f.T, per_doc, precision=lax.Precision.HIGHEST)
        gained = tok_grad * gain_f
        tok_dots = lax.optimization_barrier(jnp.sum(gained * state_blk, axis=1))
        state_gradient = rms_blk[:, None] * gained - state_blk * (rms_blk * rms_blk * rms_blk * tok_dots / MODEL_WIDTH)[:, None]
        middle_gradient = jnp.dot(state_gradient, adapter_up_wide32.T, precision=lax.Precision.HIGHEST).astype(jnp.bfloat16)
        a_acc = a_acc + jnp.dot(input_tokens.T, middle_gradient, preferred_element_type=jnp.float32)
        b_acc = b_acc + jnp.dot(mid_blk.astype(jnp.float32).T, state_gradient, precision=lax.Precision.HIGHEST)
        g_acc = g_acc + lax.optimization_barrier(jnp.sum(tok_grad * state_blk * rms_blk[:, None], axis=0))
        return ((a_acc, b_acc, g_acc), None)
    start_offset = (jnp.zeros((MODEL_WIDTH, ADAPTER_RANK), jnp.float32), jnp.zeros((ADAPTER_RANK, MODEL_WIDTH), jnp.float32), jnp.zeros((MODEL_WIDTH,), jnp.float32))
    final_states, unused_value = lax.scan(reverse_pass, start_offset, (incoming_blocks, index_lookup, hidden_states, inverse_root_mean, adapter_middle, gradient_blocks, unit_embedding, document_norm, token_counts))
    return (losses, doc_grads, final_states[0], final_states[1], final_states[2])
```

```python
import jax
import jax.numpy as jnp
from jax import lax
from jax.sharding import PartitionSpec as P

inverse_temp = 50.0


def body(
    hidden,
    document_labels,
    frozen_weight,
    adapter_down,
    adapter_up,
    norm_gain_vector,
    negative_owner,
    negative_pool_row,
):
    input_tokens = hidden[0]
    width = input_tokens.shape[1]
    column_total = adapter_up.shape[1]
    dp_count = lax.axis_size("dp")
    side_idx = lax.axis_index("pair")
    shard_idx = lax.axis_index("dp")
    column = lax.axis_index("mp")
    other_side = 1 - side_idx
    anchors = negative_owner.shape[1]
    per_shard = anchors // dp_count
    fanout = negative_owner.shape[2]
    slot_cap = min(per_shard, max(fanout, 2 * -(-(per_shard * fanout) // dp_count)))
    requests = per_shard * fanout
    highest_precision = lax.Precision.HIGHEST
    copies = lax.axis_size("groups") * lax.axis_size("pair")
    copy_rows = frozen_weight.shape[0] // copies
    copy_idx = lax.axis_index("groups") * lax.axis_size("pair") + side_idx
    weight_piece = lax.dynamic_slice_in_dim(frozen_weight, copy_idx * copy_rows, copy_rows, 0)
    projected_states = jnp.dot(
        input_tokens,
        lax.all_gather(weight_piece, ("dp", "groups", "pair"), axis=0, tiled=True),
        preferred_element_type=jnp.float32,
    )
    adapter_middle = jnp.dot(input_tokens, adapter_down, preferred_element_type=jnp.float32).astype(
        jnp.bfloat16
    )
    own_cols = lax.dynamic_slice_in_dim(input_tokens, column * column_total, column_total, 1)
    hidden_states = (
        own_cols.astype(jnp.float32)
        + projected_states
        + jnp.dot(adapter_middle, adapter_up, preferred_element_type=jnp.float32)
    )
    squares = lax.psum(jnp.sum(hidden_states * hidden_states, axis=1), "mp")
    inverse_root_mean = lax.rsqrt(squares / width + 1e-05)
    gain_f = norm_gain_vector.astype(jnp.float32)
    normed = (hidden_states * inverse_root_mean[:, None] * gain_f).astype(jnp.bfloat16)
    doc_index = document_labels[0, 0]
    doc_count = 2 * per_shard
    member = doc_index[None, :] == jnp.arange(doc_count, dtype=jnp.int32)[:, None]
    member_f = member.astype(jnp.float32)
    token_counts = jnp.sum(member_f, axis=1)
    mean_pooled = (
        jnp.dot(member.astype(jnp.bfloat16), normed, preferred_element_type=jnp.float32)
        / token_counts[:, None]
    ).astype(jnp.bfloat16)
    pooled_f = mean_pooled.astype(jnp.float32)
    doc_sq = lax.psum(jnp.sum(pooled_f * pooled_f, axis=1), "mp")
    document_norm = jnp.sqrt(doc_sq + 1e-06)
    unit_embedding = pooled_f / document_norm[:, None]
    unit_rows = unit_embedding.astype(jnp.bfloat16)
    owner_lists = negative_owner[0].reshape(dp_count, requests)
    row_lists = negative_pool_row[0].reshape(dp_count, requests)
    mine_owner = lax.dynamic_index_in_dim(owner_lists, shard_idx, 0, keepdims=False)
    pool_units = unit_rows[per_shard:]
    matched = owner_lists == shard_idx
    ranking = jnp.cumsum(matched.astype(jnp.int32), axis=1) - 1
    picked = (
        matched[:, :, None, None]
        & (ranking[:, :, None, None] == jnp.arange(slot_cap, dtype=jnp.int32)[None, None, :, None])
        & (
            row_lists[:, :, None, None]
            == jnp.arange(per_shard, dtype=jnp.int32)[None, None, None, :]
        )
    )
    selector = jnp.sum(picked.astype(jnp.float32), axis=1)
    outgoing = jnp.einsum(
        "bcr,rd->bcd", selector.astype(jnp.bfloat16), pool_units, preferred_element_type=jnp.float32
    ).astype(jnp.bfloat16)
    arrived = lax.all_to_all(outgoing, "dp", split_axis=0, concat_axis=0, tiled=True)
    arrived_flat = arrived.reshape(dp_count * slot_cap, column_total)
    request_ids = jnp.arange(requests, dtype=jnp.int32)
    earlier = (mine_owner[None, :] == mine_owner[:, None]) & (
        request_ids[None, :] < request_ids[:, None]
    )
    position = (mine_owner * slot_cap + jnp.sum(earlier.astype(jnp.int32), axis=1)).reshape(
        per_shard, fanout
    )
    gathered = lax.all_gather(unit_rows[:per_shard], ("dp", "pair"), axis=0, tiled=True)
    anchor_blocks = gathered.reshape(dp_count, 2, per_shard, column_total)
    row_units = lax.dynamic_index_in_dim(
        lax.dynamic_index_in_dim(anchor_blocks, shard_idx, 0, keepdims=False),
        other_side,
        0,
        keepdims=False,
    )
    cand_units = lax.dynamic_index_in_dim(anchor_blocks, side_idx, 1, keepdims=False).reshape(
        anchors, column_total
    )
    batch_part = jnp.dot(row_units, cand_units.T, preferred_element_type=jnp.float32)
    neg_part = jnp.dot(row_units, arrived_flat.T, preferred_element_type=jnp.float32)
    batch_sums, neg_sums = lax.psum((batch_part, neg_part), "mp")
    neg_pick = jnp.take_along_axis(neg_sums, position, axis=1)
    logits = inverse_temp * jnp.concatenate([batch_sums, neg_pick], axis=1)
    exp_logits = jnp.exp(logits)
    denominator = jnp.sum(exp_logits, axis=1)
    target_col = shard_idx * per_shard + jnp.arange(per_shard, dtype=jnp.int32)
    target = jnp.arange(anchors + fanout, dtype=jnp.int32)[None, :] == target_col[:, None]
    losses = (jnp.log(denominator) - jnp.sum(jnp.where(target, logits, 0.0), axis=1))[None, :]
    logit_grad = (
        inverse_temp * (exp_logits / denominator[:, None] - target.astype(jnp.float32))
    ).astype(jnp.bfloat16)
    grad_batch = logit_grad[:, :anchors]
    grad_neg = logit_grad[:, anchors:].astype(jnp.float32)
    slot_total = arrived_flat.shape[0]
    slot_hot = position[:, :, None] == jnp.arange(slot_total, dtype=jnp.int32)[None, None, :]
    grad_slots = jnp.sum(jnp.where(slot_hot, grad_neg[:, :, None], 0.0), axis=1).astype(
        jnp.bfloat16
    )
    rows_grad = jnp.dot(grad_batch, cand_units, preferred_element_type=jnp.float32) + jnp.dot(
        grad_slots, arrived_flat, preferred_element_type=jnp.float32
    )
    cand_grad = jnp.dot(grad_batch.T, row_units, preferred_element_type=jnp.float32)
    slot_grad = jnp.dot(grad_slots.T, row_units, preferred_element_type=jnp.float32)
    side_mask = (jnp.arange(2, dtype=jnp.int32) == side_idx)[None, :, None, None]
    scatter_term = jnp.where(
        side_mask, cand_grad.reshape(dp_count, 1, per_shard, column_total), 0.0
    )
    row_mask = (
        (jnp.arange(dp_count, dtype=jnp.int32) == shard_idx)[:, None]
        & (jnp.arange(2, dtype=jnp.int32) == other_side)[None, :]
    )[:, :, None, None]
    scatter_term = scatter_term + jnp.where(row_mask, rows_grad[None, None], 0.0)
    anchor_grad = lax.psum_scatter(
        scatter_term.reshape(dp_count * 2 * per_shard, column_total),
        ("dp", "pair"),
        scatter_dimension=0,
        tiled=True,
    )
    returned = lax.all_to_all(
        slot_grad.reshape(dp_count, slot_cap, column_total).astype(jnp.bfloat16),
        "dp",
        split_axis=0,
        concat_axis=0,
        tiled=True,
    ).astype(jnp.float32)
    pool_grad = jnp.einsum("bcr,bcd->rd", selector, returned, precision=highest_precision)
    doc_grad = jnp.concatenate([anchor_grad, pool_grad], axis=0)
    adapter_up_wide32 = adapter_up.astype(jnp.float32)
    cube = inverse_root_mean * inverse_root_mean * inverse_root_mean
    unit_dots = lax.psum(jnp.sum(unit_embedding * doc_grad, axis=1), "mp")
    per_doc = (doc_grad - unit_embedding * unit_dots[:, None]) / (document_norm * token_counts)[
        :, None
    ]
    tok_grad = jnp.dot(member_f.T, per_doc, precision=highest_precision)
    gained = tok_grad * gain_f
    tok_dots = lax.psum(jnp.sum(gained * hidden_states, axis=1), "mp")
    state_gradient = (
        inverse_root_mean[:, None] * gained - hidden_states * (cube * tok_dots / width)[:, None]
    )
    middle_piece = jnp.dot(state_gradient, adapter_up_wide32.T, precision=highest_precision)
    middle_gradient = lax.psum(middle_piece, "mp").astype(jnp.bfloat16)
    gain_grad = jnp.sum(tok_grad * hidden_states * inverse_root_mean[:, None], axis=0)
    up_map_gradient = jnp.dot(
        adapter_middle.astype(jnp.float32).T, state_gradient, precision=highest_precision
    )
    a_grad = jnp.dot(own_cols.T, middle_gradient, preferred_element_type=jnp.float32)
    a_grad, up_map_gradient, gain_grad = lax.psum(
        (a_grad, up_map_gradient, gain_grad), ("dp", "pair")
    )
    return (losses, doc_grad[None, None], a_grad, up_map_gradient, gain_grad)


def solution(mesh):
    in_specs = (
        P("pair", ("groups", "dp"), None),
        P("pair", ("groups", "dp"), None),
        P("dp", "mp"),
        P(),
        P(None, "mp"),
        P("mp"),
        P("pair", "groups", None),
        P("pair", "groups", None),
    )
    out_specs = (
        P("pair", ("groups", "dp")),
        P("pair", ("groups", "dp"), None, "mp"),
        P(("groups", "mp"), None),
        P("groups", "mp"),
        P(("groups", "mp")),
    )
    return jax.shard_map(body, mesh=mesh, in_specs=in_specs, out_specs=out_specs, check_vma=False)
```

```python
import jax
import jax.numpy as jnp
from jax import lax
from jax.sharding import PartitionSpec as P

inverse_temp = 50.0
highest = lax.Precision.HIGHEST


def dot_nt(a, b, precision=None):
    return lax.dot_general(
        a, b, (((1,), (1,)), ((), ())), precision=precision, preferred_element_type=jnp.float32
    )


def dot_nn(a, b, precision=None):
    return jnp.dot(a, b, precision=precision, preferred_element_type=jnp.float32)


def swap(x, axis):
    return lax.ppermute(x, axis, [(0, 1), (1, 0)])


def partner(x, axis, flip):
    return lax.ppermute(x, axis, [(i, i ^ flip) for i in range(lax.axis_size(axis))])


def sum_over(x, axis):
    if lax.axis_size(axis) == 2:
        return x + swap(x, axis)
    return lax.psum(x, axis)


def body(
    hidden,
    document_labels,
    frozen_weight,
    adapter_down,
    adapter_up,
    norm_gain_vector,
    negative_owner,
    negative_pool_row,
):
    tokens = hidden[0]
    token_count, width = tokens.shape
    cols = adapter_up.shape[1]
    rank = adapter_up.shape[0]
    dp = lax.axis_size("dp")
    side = lax.axis_index("pair")
    shard = lax.axis_index("dp")
    anchors = negative_owner.shape[1]
    per_shard = anchors // dp
    docs = 2 * per_shard

    block_shard = shard ^ jnp.arange(dp, dtype=jnp.int32)
    list_col = (shard ^ negative_owner[0]) * docs + per_shard + negative_pool_row[0]
    own_list = lax.dynamic_slice_in_dim(list_col, shard * per_shard, per_shard, 0)
    other_own_list = swap(own_list, "pair")
    rel_list = list_col.reshape(dp, per_shard, -1)[block_shard].reshape(anchors, -1)
    col_id = jnp.arange(dp * docs, dtype=jnp.int32)
    anchor_col = (col_id % docs) < per_shard

    def listed(lists):
        hit = lists[:, :, None] == col_id[None, None, :]
        return jnp.any(hit, axis=1) | anchor_col[None, :]

    mask_c = listed(rel_list)
    mask_o = listed(other_own_list)
    rel_row = jnp.arange(anchors, dtype=jnp.int32)
    target_c = col_id[None, :] == (rel_row // per_shard * docs + rel_row % per_shard)[:, None]
    target_o = target_c[:per_shard]

    copies = lax.axis_size("groups") * lax.axis_size("pair")
    copy_rows = frozen_weight.shape[0] // copies
    copy_idx = lax.axis_index("groups") * lax.axis_size("pair") + side
    weight_piece = lax.dynamic_slice_in_dim(frozen_weight, copy_idx * copy_rows, copy_rows, 0)
    weight = lax.all_gather(weight_piece, ("dp", "groups", "pair"), axis=0, tiled=True)
    lora_mid = dot_nn(tokens, adapter_down).astype(jnp.bfloat16)
    own_cols = lax.dynamic_slice_in_dim(tokens, lax.axis_index("mp") * cols, cols, 1)
    states = own_cols.astype(jnp.float32) + dot_nn(tokens, weight) + dot_nn(lora_mid, adapter_up)
    states_b = states.astype(jnp.bfloat16)
    squares = sum_over(jnp.sum(states * states, axis=1), "mp")
    inv_rms = lax.rsqrt(squares / width + 1e-05)

    gain = norm_gain_vector.astype(jnp.float32)
    labels = document_labels[0, 0]
    member = labels[None, :] == jnp.arange(docs, dtype=jnp.int32)[:, None]
    member_f = member.astype(jnp.float32)
    counts = jnp.sum(member_f, axis=1)
    normed = (states * inv_rms[:, None] * gain).astype(jnp.bfloat16)
    doc_sums = dot_nn(member.astype(jnp.bfloat16), normed)
    pooled = (doc_sums / counts[:, None]).astype(jnp.bfloat16)

    own_blocks = [pooled] + [partner(pooled, "dp", j) for j in range(1, dp)]
    other_blocks = [swap(block, "pair") for block in own_blocks]
    docs_own = jnp.concatenate(own_blocks, axis=0)
    docs_oth = jnp.concatenate(other_blocks, axis=0)
    anchors_oth = jnp.concatenate([block[:per_shard] for block in other_blocks], axis=0)
    docs_own_f = docs_own.astype(jnp.float32)
    docs_oth_f = docs_oth.astype(jnp.float32)
    sums = sum_over(
        jnp.concatenate(
            [
                dot_nt(anchors_oth, docs_own),
                dot_nt(pooled[:per_shard], docs_oth),
                jnp.sum(docs_own_f * docs_own_f, axis=1)[None],
                jnp.sum(docs_oth_f * docs_oth_f, axis=1)[None],
            ],
            axis=0,
        ),
        "mp",
    )
    inner_c = sums[:anchors]
    inner_o = sums[anchors : anchors + per_shard]
    inv_own = lax.rsqrt(sums[anchors + per_shard] + 1e-06)
    inv_oth = lax.rsqrt(sums[anchors + per_shard + 1] + 1e-06)
    inv_oth_anchor = inv_oth.reshape(dp, docs)[:, :per_shard].reshape(anchors)
    inv_own_doc = inv_own[:docs]

    def softmax_grad(inner, scale_row, scale_col, mask, target):
        logits = inverse_temp * (inner * scale_row[:, None] * scale_col[None, :])
        exp_logits = jnp.where(mask, jnp.exp(logits), 0.0)
        total = jnp.sum(exp_logits, axis=1)
        hit = jnp.sum(jnp.where(target, logits, 0.0), axis=1)
        grad = inverse_temp * (exp_logits / total[:, None] - target.astype(jnp.float32))
        return jnp.log(total) - hit, grad

    losses_c, grad_c = softmax_grad(inner_c, inv_oth_anchor, inv_own, mask_c, target_c)
    _, grad_o = softmax_grad(inner_o, inv_own_doc[:per_shard], inv_oth, mask_o, target_o)
    losses = losses_c[:per_shard][None]

    grad_ct = grad_c[:, :docs].T.reshape(docs, dp, per_shard)
    inner_ct = inner_c[:, :docs].T.reshape(docs, dp, per_shard)
    zero_pool = jnp.zeros((docs, dp, per_shard), jnp.float32)
    zero_rows = jnp.zeros((docs - per_shard, dp * docs), jnp.float32)
    coef = jnp.concatenate([grad_ct, zero_pool], axis=2).reshape(docs, dp * docs)
    coef = coef + jnp.concatenate([grad_o, zero_rows], axis=0)
    inner = jnp.concatenate(
        [
            inner_o,
            jnp.concatenate([inner_ct, zero_pool], axis=2).reshape(docs, dp * docs)[per_shard:],
        ],
        axis=0,
    )
    coef_b = (coef * inv_oth[None, :]).astype(jnp.bfloat16)
    doc_grad = dot_nn(coef_b, docs_oth)
    unit_dots = jnp.sum(coef_b.astype(jnp.float32) * inner, axis=1) * inv_own_doc
    pooled_f = pooled.astype(jnp.float32)
    per_doc = (doc_grad - pooled_f * (inv_own_doc * unit_dots)[:, None]) * (inv_own_doc / counts)[
        :, None
    ]

    gained = per_doc * gain
    up_f = adapter_up.astype(jnp.float32)
    tok_doc = dot_nt(gained.astype(jnp.bfloat16), states_b)
    tok_dots = jnp.sum(jnp.where(member, tok_doc, 0.0), axis=0)[None]
    up_states = dot_nt(adapter_up, states_b)
    up_gained = dot_nt(up_f, gained, highest)
    small = sum_over(
        jnp.concatenate(
            [
                jnp.concatenate([tok_dots, up_states], axis=0),
                jnp.concatenate([jnp.zeros((1, docs), jnp.float32), up_gained], axis=0),
            ],
            axis=1,
        ),
        "mp",
    )
    alpha = inv_rms * inv_rms * inv_rms * small[0, :token_count] / width
    up_states = small[1:, :token_count]
    up_gained = small[1:, token_count:]
    mid_grad = (
        inv_rms * dot_nn(up_gained, member_f, highest) - alpha * up_states
    ).astype(jnp.bfloat16)
    mid_t = lora_mid.astype(jnp.float32).T
    a_grad = dot_nn(mid_grad, own_cols)
    b_grad = dot_nn(dot_nt(mid_t * inv_rms, member_f, highest), gained, highest) - dot_nn(
        (mid_t * alpha).astype(jnp.bfloat16), states_b
    )
    gain_grad = jnp.sum(per_doc * doc_sums, axis=0) / gain

    grads = jnp.concatenate([a_grad, b_grad, gain_grad[None]], axis=0)
    half = cols // 2
    kept = lax.dynamic_slice_in_dim(grads, side * half, half, 1)
    sent = lax.dynamic_slice_in_dim(grads, (1 - side) * half, half, 1)
    kept = kept + swap(sent, "pair")
    level = [kept] + [partner(kept, "dp", j) for j in range(1, dp)]
    while len(level) > 1:
        level = [level[i] + level[i + 1] for i in range(0, len(level), 2)]
    total = level[0]
    received = swap(total, "pair")
    grads = jnp.concatenate(
        [jnp.where(side == 0, total, received), jnp.where(side == 0, received, total)], axis=1
    )
    return (
        losses,
        doc_grad[None, None],
        grads[:rank].T,
        grads[rank : 2 * rank],
        grads[2 * rank],
    )


def solution(mesh):
    in_specs = (
        P("pair", ("groups", "dp"), None),
        P("pair", ("groups", "dp"), None),
        P("dp", "mp"),
        P(),
        P(None, "mp"),
        P("mp"),
        P("pair", "groups", None),
        P("pair", "groups", None),
    )
    out_specs = (
        P("pair", ("groups", "dp")),
        P("pair", ("groups", "dp"), None, "mp"),
        P(("groups", "mp"), None),
        P("groups", "mp"),
        P(("groups", "mp")),
    )
    return jax.shard_map(body, mesh=mesh, in_specs=in_specs, out_specs=out_specs, check_vma=False)
```

```python
import jax
import jax.numpy as jnp
from jax import lax
from jax.sharding import PartitionSpec as P

inverse_temp = 50.0
highest = lax.Precision.HIGHEST
chunk_count = 2


def dot_nt(a, b, precision=None):
    return lax.dot_general(
        a, b, (((1,), (1,)), ((), ())), precision=precision, preferred_element_type=jnp.float32
    )


def dot_nn(a, b, precision=None):
    return jnp.dot(a, b, precision=precision, preferred_element_type=jnp.float32)


def swap(x, axis):
    return lax.ppermute(x, axis, [(0, 1), (1, 0)])


def partner(x, axis, flip):
    return lax.ppermute(x, axis, [(i, i ^ flip) for i in range(lax.axis_size(axis))])


def sum_over(x, axis):
    if lax.axis_size(axis) == 2:
        return x + swap(x, axis)
    return lax.psum(x, axis)


def body(
    hidden,
    document_labels,
    frozen_weight,
    adapter_down,
    adapter_up,
    norm_gain_vector,
    negative_owner,
    negative_pool_row,
):
    tokens = hidden[0]
    token_count, width = tokens.shape
    cols = adapter_up.shape[1]
    rank = adapter_up.shape[0]
    dp = lax.axis_size("dp")
    side = lax.axis_index("pair")
    shard = lax.axis_index("dp")
    anchors = negative_owner.shape[1]
    per_shard = anchors // dp
    docs = 2 * per_shard

    block_shard = shard ^ jnp.arange(dp, dtype=jnp.int32)
    list_col = (shard ^ negative_owner[0]) * docs + per_shard + negative_pool_row[0]
    own_list = lax.dynamic_slice_in_dim(list_col, shard * per_shard, per_shard, 0)
    other_own_list = swap(own_list, "pair")
    rel_list = list_col.reshape(dp, per_shard, -1)[block_shard].reshape(anchors, -1)
    col_id = jnp.arange(dp * docs, dtype=jnp.int32)
    anchor_col = (col_id % docs) < per_shard

    def listed(lists):
        hit = lists[:, :, None] == col_id[None, None, :]
        return jnp.any(hit, axis=1) | anchor_col[None, :]

    mask_c = listed(rel_list)
    mask_o = listed(other_own_list)
    rel_row = jnp.arange(anchors, dtype=jnp.int32)
    target_c = col_id[None, :] == (rel_row // per_shard * docs + rel_row % per_shard)[:, None]
    target_o = target_c[:per_shard]

    group = lax.axis_index("groups")
    quarter = frozen_weight.shape[0] // 4
    shard_rows = frozen_weight.shape[0]
    chunk = cols // chunk_count
    order = list(range(1, dp, 2)) + list(range(dp - 2 + dp % 2, 0, -2))
    order = [0] + order
    hops = [(order[i], order[(i + 1) % dp]) for i in range(dp)]
    place = jnp.array([order.index(i) for i in range(dp)], jnp.int32)[shard]
    order_table = jnp.array(order, jnp.int32)
    quarters = [
        (group * 2 + side),
        ((1 - group) * 2 + side),
        (group * 2 + 1 - side),
        ((1 - group) * 2 + 1 - side),
    ]
    moving = [
        lax.dynamic_slice(frozen_weight, (quarters[0] * quarter, h * chunk), (quarter, chunk))
        for h in range(chunk_count)
    ]
    lora_mid = dot_nn(tokens, adapter_down).astype(jnp.bfloat16)
    own_cols = lax.dynamic_slice_in_dim(tokens, lax.axis_index("mp") * cols, cols, 1)
    own_tokens = lax.dynamic_slice_in_dim(tokens, shard * shard_rows, shard_rows, 1)
    states = []
    for h in range(chunk_count):
        part = slice(h * chunk, (h + 1) * chunk)
        states.append(
            own_cols[:, part].astype(jnp.float32)
            + dot_nn(own_tokens, frozen_weight[:, part])
            + dot_nn(lora_mid, adapter_up[:, part])
        )
    for step in range(1, dp):
        origin = order_table[(place - step) % dp]
        step_tokens = jnp.concatenate(
            [
                lax.dynamic_slice_in_dim(tokens, origin * shard_rows + q * quarter, quarter, 1)
                for q in quarters
            ],
            axis=1,
        )
        for h in range(chunk_count):
            moving[h] = lax.ppermute(moving[h], "dp", hops)
            across = swap(moving[h], "groups")
            rows = [moving[h], across, swap(moving[h], "pair"), swap(across, "pair")]
            states[h] = states[h] + dot_nn(step_tokens, jnp.concatenate(rows, axis=0))
    states_b = [x.astype(jnp.bfloat16) for x in states]
    squares = sum_over(sum(jnp.sum(x * x, axis=1) for x in states), "mp")
    inv_rms = lax.rsqrt(squares / width + 1e-05)

    gain = norm_gain_vector.astype(jnp.float32)
    labels = document_labels[0, 0]
    member = labels[None, :] == jnp.arange(docs, dtype=jnp.int32)[:, None]
    member_f = member.astype(jnp.float32)
    counts = jnp.sum(member_f, axis=1)
    member_b = member.astype(jnp.bfloat16)
    doc_sums = jnp.concatenate(
        [
            dot_nn(member_b, (x * inv_rms[:, None] * g[None, :]).astype(jnp.bfloat16))
            for x, g in zip(states, jnp.split(gain, chunk_count))
        ],
        axis=1,
    )
    pooled = (doc_sums / counts[:, None]).astype(jnp.bfloat16)

    own_blocks = [pooled] + [partner(pooled, "dp", j) for j in range(1, dp)]
    other_blocks = [swap(block, "pair") for block in own_blocks]
    docs_own = jnp.concatenate(own_blocks, axis=0)
    docs_oth = jnp.concatenate(other_blocks, axis=0)
    anchors_oth = jnp.concatenate([block[:per_shard] for block in other_blocks], axis=0)
    docs_own_f = docs_own.astype(jnp.float32)
    docs_oth_f = docs_oth.astype(jnp.float32)
    sums = sum_over(
        jnp.concatenate(
            [
                dot_nt(anchors_oth, docs_own),
                dot_nt(pooled[:per_shard], docs_oth),
                jnp.sum(docs_own_f * docs_own_f, axis=1)[None],
                jnp.sum(docs_oth_f * docs_oth_f, axis=1)[None],
            ],
            axis=0,
        ),
        "mp",
    )
    inner_c = sums[:anchors]
    inner_o = sums[anchors : anchors + per_shard]
    inv_own = lax.rsqrt(sums[anchors + per_shard] + 1e-06)
    inv_oth = lax.rsqrt(sums[anchors + per_shard + 1] + 1e-06)
    inv_oth_anchor = inv_oth.reshape(dp, docs)[:, :per_shard].reshape(anchors)
    inv_own_doc = inv_own[:docs]

    def softmax_grad(inner, scale_row, scale_col, mask, target):
        logits = inverse_temp * (inner * scale_row[:, None] * scale_col[None, :])
        exp_logits = jnp.where(mask, jnp.exp(logits), 0.0)
        total = jnp.sum(exp_logits, axis=1)
        hit = jnp.sum(jnp.where(target, logits, 0.0), axis=1)
        grad = inverse_temp * (exp_logits / total[:, None] - target.astype(jnp.float32))
        return jnp.log(total) - hit, grad

    losses_c, grad_c = softmax_grad(inner_c, inv_oth_anchor, inv_own, mask_c, target_c)
    _, grad_o = softmax_grad(inner_o, inv_own_doc[:per_shard], inv_oth, mask_o, target_o)
    losses = losses_c[:per_shard][None]

    grad_ct = grad_c[:, :docs].T.reshape(docs, dp, per_shard)
    inner_ct = inner_c[:, :docs].T.reshape(docs, dp, per_shard)
    zero_pool = jnp.zeros((docs, dp, per_shard), jnp.float32)
    zero_rows = jnp.zeros((docs - per_shard, dp * docs), jnp.float32)
    coef = jnp.concatenate([grad_ct, zero_pool], axis=2).reshape(docs, dp * docs)
    coef = coef + jnp.concatenate([grad_o, zero_rows], axis=0)
    inner = jnp.concatenate(
        [
            inner_o,
            jnp.concatenate([inner_ct, zero_pool], axis=2).reshape(docs, dp * docs)[per_shard:],
        ],
        axis=0,
    )
    coef_b = (coef * inv_oth[None, :]).astype(jnp.bfloat16)
    doc_grad = dot_nn(coef_b, docs_oth)
    unit_dots = jnp.sum(coef_b.astype(jnp.float32) * inner, axis=1) * inv_own_doc
    pooled_f = pooled.astype(jnp.float32)
    per_doc = (doc_grad - pooled_f * (inv_own_doc * unit_dots)[:, None]) * (inv_own_doc / counts)[
        :, None
    ]

    gained = per_doc * gain
    up_f = adapter_up.astype(jnp.float32)
    gained_b = jnp.split(gained.astype(jnp.bfloat16), chunk_count, axis=1)
    tok_doc = sum(dot_nt(g, x) for g, x in zip(gained_b, states_b))
    tok_dots = jnp.sum(jnp.where(member, tok_doc, 0.0), axis=0)[None]
    up_parts = jnp.split(adapter_up, chunk_count, axis=1)
    up_states = sum(dot_nt(u, x) for u, x in zip(up_parts, states_b))
    up_gained = dot_nt(up_f, gained, highest)
    small = sum_over(
        jnp.concatenate(
            [
                jnp.concatenate([tok_dots, up_states], axis=0),
                jnp.concatenate([jnp.zeros((1, docs), jnp.float32), up_gained], axis=0),
            ],
            axis=1,
        ),
        "mp",
    )
    alpha = inv_rms * inv_rms * inv_rms * small[0, :token_count] / width
    up_states = small[1:, :token_count]
    up_gained = small[1:, token_count:]
    mid_grad = (
        inv_rms * dot_nn(up_gained, member_f, highest) - alpha * up_states
    ).astype(jnp.bfloat16)
    mid_t = lora_mid.astype(jnp.float32).T
    a_grad = dot_nn(mid_grad, own_cols)
    mid_alpha = (mid_t * alpha).astype(jnp.bfloat16)
    b_grad = dot_nn(dot_nt(mid_t * inv_rms, member_f, highest), gained, highest) - jnp.concatenate(
        [dot_nn(mid_alpha, x) for x in states_b], axis=1
    )
    gain_grad = jnp.sum(per_doc * doc_sums, axis=0) / gain

    grads = jnp.concatenate([a_grad, b_grad, gain_grad[None]], axis=0)
    half = cols // 2
    kept = lax.dynamic_slice_in_dim(grads, side * half, half, 1)
    sent = lax.dynamic_slice_in_dim(grads, (1 - side) * half, half, 1)
    kept = kept + swap(sent, "pair")
    level = [kept] + [partner(kept, "dp", j) for j in range(1, dp)]
    while len(level) > 1:
        level = [level[i] + level[i + 1] for i in range(0, len(level), 2)]
    total = level[0]
    received = swap(total, "pair")
    grads = jnp.concatenate(
        [jnp.where(side == 0, total, received), jnp.where(side == 0, received, total)], axis=1
    )
    return (
        losses,
        doc_grad[None, None],
        grads[:rank].T,
        grads[rank : 2 * rank],
        grads[2 * rank],
    )


def solution(mesh):
    in_specs = (
        P("pair", ("groups", "dp"), None),
        P("pair", ("groups", "dp"), None),
        P("dp", "mp"),
        P(),
        P(None, "mp"),
        P("mp"),
        P("pair", "groups", None),
        P("pair", "groups", None),
    )
    out_specs = (
        P("pair", ("groups", "dp")),
        P("pair", ("groups", "dp"), None, "mp"),
        P(("groups", "mp"), None),
        P("groups", "mp"),
        P(("groups", "mp")),
    )
    return jax.shard_map(body, mesh=mesh, in_specs=in_specs, out_specs=out_specs, check_vma=False)
```

```python
import functools

import jax
import jax.numpy as jnp
from jax import lax
from jax.experimental import pallas as pl
from jax.experimental.pallas import tpu as pltpu
from jax.sharding import PartitionSpec as P

inverse_temp = 50.0
highest = lax.Precision.HIGHEST
chunk_count = 2


def dot_nt(a, b, precision=None):
    return lax.dot_general(
        a, b, (((1,), (1,)), ((), ())), precision=precision, preferred_element_type=jnp.float32
    )


def dot_nn(a, b, precision=None):
    return jnp.dot(a, b, precision=precision, preferred_element_type=jnp.float32)


def swap(x, axis):
    return lax.ppermute(x, axis, [(0, 1), (1, 0)])


def partner(x, axis, flip):
    return lax.ppermute(x, axis, [(i, i ^ flip) for i in range(lax.axis_size(axis))])


def sum_over(x, axis):
    if lax.axis_size(axis) == 2:
        return x + swap(x, axis)
    return lax.psum(x, axis)


def call(kernel, outs, args, scratch=(), flops=1 << 24):
    size = sum(a.size * a.dtype.itemsize for a in args)
    return pl.pallas_call(
        kernel,
        out_shape=outs,
        scratch_shapes=list(scratch),
        compiler_params=pltpu.CompilerParams(vmem_limit_bytes=48 << 20),
        cost_estimate=pl.CostEstimate(flops=flops, bytes_accessed=size, transcendentals=0),
    )(*args)


def as_row(column):
    size = column.shape[0]
    eye = lax.broadcasted_iota(jnp.int32, (size, size), 0) == lax.broadcasted_iota(
        jnp.int32, (size, size), 1
    )
    return jnp.sum(jnp.where(eye, column, 0.0), axis=0, keepdims=True)


def as_column(row):
    size = row.shape[1]
    eye = lax.broadcasted_iota(jnp.int32, (size, size), 0) == lax.broadcasted_iota(
        jnp.int32, (size, size), 1
    )
    return jnp.sum(jnp.where(eye, row, 0.0), axis=1, keepdims=True)


def gram_kernel(blocks, *refs):
    own, oth = refs[:blocks], refs[blocks : 2 * blocks]
    out_ref, sorted_ref, own_ref = refs[2 * blocks :]
    docs = own[0].shape[0]
    half = docs // 2
    anchors = blocks * half
    for j in range(blocks):
        own_ref[j * docs : (j + 1) * docs] = own[j][...]
        sorted_ref[j * half : (j + 1) * half] = oth[j][:half]
        sorted_ref[anchors + j * half : anchors + (j + 1) * half] = oth[j][half:]
    rows = blocks * docs
    out_ref[:rows] = dot_nt(own_ref[...], sorted_ref[:anchors])
    out_ref[rows : rows + half] = dot_nt(own[0][:half], sorted_ref[anchors:])
    own_f = own_ref[...].astype(jnp.float32)
    oth_f = sorted_ref[...].astype(jnp.float32)
    own_sq = as_row(jnp.sum(own_f * own_f, axis=1, keepdims=True))
    oth_sq = as_row(jnp.sum(oth_f * oth_f, axis=1, keepdims=True))
    tail = jnp.concatenate(
        [
            own_sq[:, :anchors],
            own_sq[:, anchors:],
            oth_sq[:, :anchors],
            oth_sq[:, anchors:],
            jnp.zeros((4, anchors), jnp.float32),
        ],
        axis=0,
    )
    out_ref[rows + half :] = tail


def loss_kernel(blocks, sums_count, chunks, *refs):
    sums_refs = refs[:sums_count]
    list_c, list_o, pooled_ref, oth_ref, counts_ref, gain_ref, doc_sums_ref, up_ref = refs[
        sums_count : sums_count + 8
    ]
    up_states_ref, labels_ref = refs[sums_count + 8 : sums_count + 10]
    state_refs = refs[sums_count + 10 : sums_count + 10 + chunks]
    losses_ref, doc_grad_ref, small_ref, gained_ref, gain_grad_ref = refs[
        sums_count + 10 + chunks :
    ]
    docs = pooled_ref.shape[0]
    half = docs // 2
    anchors = blocks * half
    rows = blocks * docs
    fanout = list_o.shape[1]
    sums = sums_refs[0][...]
    if sums_count == 2:
        sums = sums + sums_refs[1][...]
    inner_c = sums[:rows]
    inner_o = sums[rows : rows + half]
    scales = lax.rsqrt(sums[rows + half :] + 1e-06)
    own_scale = as_column(jnp.concatenate([scales[0:1], scales[1:2]], axis=1))
    oth_scale = scales[2:3]
    pool_scale = scales[3:4]

    row_id = lax.broadcasted_iota(jnp.int32, (rows, anchors), 0)
    col_id = lax.broadcasted_iota(jnp.int32, (rows, anchors), 1)
    mask_c = (row_id % docs) < half
    for h in range(fanout):
        mask_c = mask_c | (row_id == list_c[h : h + 1, :])
    target_c = row_id == (col_id // half) * docs + col_id % half
    logits_c = inverse_temp * (inner_c * own_scale * oth_scale)
    exp_all = jnp.exp(logits_c)
    exp_c = jnp.where(mask_c, exp_all, 0.0)
    total_c = jnp.sum(exp_c, axis=0, keepdims=True)
    losses_ref[...] = jnp.log(total_c) - jnp.sum(
        jnp.where(target_c, logits_c, 0.0), axis=0, keepdims=True
    )
    target_own = target_c[:docs].astype(jnp.float32)
    grad_c = inverse_temp * (exp_c[:docs] / total_c - target_own)

    logits_o = inverse_temp * (inner_o * own_scale[:half] * pool_scale)
    pool_id = lax.broadcasted_iota(jnp.int32, (half, anchors), 1)
    mask_o = pool_id == list_o[:, 0:1]
    for h in range(1, fanout):
        mask_o = mask_o | (pool_id == list_o[:, h : h + 1])
    exp_o = jnp.where(mask_o, jnp.exp(logits_o), 0.0)
    exp_a = exp_all[:half]
    total_o = jnp.sum(exp_a, axis=1, keepdims=True) + jnp.sum(exp_o, axis=1, keepdims=True)
    grad_a = inverse_temp * (exp_a / total_o - target_own[:half])
    grad_o = inverse_temp * (exp_o / total_o)

    zeros = jnp.zeros((docs - half, anchors), jnp.float32)
    coef = jnp.concatenate(
        [
            (grad_c + jnp.concatenate([grad_a, zeros], axis=0)) * oth_scale,
            jnp.concatenate([grad_o * pool_scale, zeros], axis=0),
        ],
        axis=1,
    ).astype(jnp.bfloat16)
    inner = jnp.concatenate(
        [inner_c[:docs], jnp.concatenate([inner_o, zeros], axis=0)], axis=1
    )
    doc_grad = dot_nn(coef, oth_ref[...])
    doc_grad_ref[...] = doc_grad
    scale = own_scale[:docs]
    unit_dots = jnp.sum(coef.astype(jnp.float32) * inner, axis=1, keepdims=True) * scale
    pooled = pooled_ref[...].astype(jnp.float32)
    per_doc = (doc_grad - pooled * (scale * unit_dots)) * (scale / counts_ref[...])
    gain = gain_ref[...]
    gained = per_doc * gain
    gained_ref[...] = gained
    gain_grad_ref[...] = jnp.sum(per_doc * doc_sums_ref[...], axis=0, keepdims=True) / gain

    gained_b = gained.astype(jnp.bfloat16)
    chunk = state_refs[0].shape[1]
    tok_doc = dot_nt(gained_b[:, :chunk], state_refs[0][...])
    for i in range(1, chunks):
        tok_doc = tok_doc + dot_nt(
            gained_b[:, i * chunk : (i + 1) * chunk], state_refs[i][...]
        )
    tokens = tok_doc.shape[1]
    rank = up_ref.shape[0]
    doc_id = lax.broadcasted_iota(jnp.int32, (docs, tokens), 0)
    tok_dots = jnp.sum(
        jnp.where(doc_id == labels_ref[...], tok_doc, 0.0), axis=0, keepdims=True
    )
    up_gained = dot_nt(up_ref[...].astype(jnp.float32), gained, highest)
    small_ref[...] = jnp.zeros_like(small_ref)
    small_ref[:rank, :tokens] = up_states_ref[...]
    small_ref[:rank, tokens : tokens + docs] = up_gained
    small_ref[rank : rank + 1, :tokens] = tok_dots


def body(
    hidden,
    document_labels,
    frozen_weight,
    adapter_down,
    adapter_up,
    norm_gain_vector,
    negative_owner,
    negative_pool_row,
):
    tokens = hidden[0]
    token_count, width = tokens.shape
    cols = adapter_up.shape[1]
    rank = adapter_up.shape[0]
    dp = lax.axis_size("dp")
    side = lax.axis_index("pair")
    shard = lax.axis_index("dp")
    anchors = negative_owner.shape[1]
    per_shard = anchors // dp
    docs = 2 * per_shard

    block_shard = shard ^ jnp.arange(dp, dtype=jnp.int32)
    owner_block = shard ^ negative_owner[0]
    rel_list = (owner_block * docs + per_shard + negative_pool_row[0]).reshape(dp, per_shard, -1)
    list_c = rel_list[block_shard].reshape(anchors, -1).T
    pool_col = owner_block * per_shard + negative_pool_row[0]
    list_o = swap(
        lax.dynamic_slice_in_dim(pool_col, shard * per_shard, per_shard, 0), "pair"
    )

    group = lax.axis_index("groups")
    quarter = frozen_weight.shape[0] // 4
    shard_rows = frozen_weight.shape[0]
    chunk = cols // chunk_count
    order = list(range(1, dp, 2)) + list(range(dp - 2 + dp % 2, 0, -2))
    order = [0] + order
    hops = [(order[i], order[(i + 1) % dp]) for i in range(dp)]
    place = jnp.array([order.index(i) for i in range(dp)], jnp.int32)[shard]
    order_table = jnp.array(order, jnp.int32)
    quarters = [
        (group * 2 + side),
        ((1 - group) * 2 + side),
        (group * 2 + 1 - side),
        ((1 - group) * 2 + 1 - side),
    ]
    moving = [
        lax.dynamic_slice(frozen_weight, (quarters[0] * quarter, h * chunk), (quarter, chunk))
        for h in range(chunk_count)
    ]
    lora_mid = dot_nn(tokens, adapter_down).astype(jnp.bfloat16)
    own_cols = lax.dynamic_slice_in_dim(tokens, lax.axis_index("mp") * cols, cols, 1)
    own_tokens = lax.dynamic_slice_in_dim(tokens, shard * shard_rows, shard_rows, 1)
    states = []
    for h in range(chunk_count):
        part = slice(h * chunk, (h + 1) * chunk)
        states.append(
            own_cols[:, part].astype(jnp.float32)
            + dot_nn(own_tokens, frozen_weight[:, part])
            + dot_nn(lora_mid, adapter_up[:, part])
        )
    for step in range(1, dp):
        origin = order_table[(place - step) % dp]
        step_tokens = jnp.concatenate(
            [
                lax.dynamic_slice_in_dim(tokens, origin * shard_rows + q * quarter, quarter, 1)
                for q in quarters
            ],
            axis=1,
        )
        for h in range(chunk_count):
            moving[h] = lax.ppermute(moving[h], "dp", hops)
            across = swap(moving[h], "groups")
            rows = [moving[h], across, swap(moving[h], "pair"), swap(across, "pair")]
            states[h] = states[h] + dot_nn(step_tokens, jnp.concatenate(rows, axis=0))
    states_b = [x.astype(jnp.bfloat16) for x in states]
    squares = sum_over(sum(jnp.sum(x * x, axis=1) for x in states), "mp")
    inv_rms = lax.rsqrt(squares / width + 1e-05)

    gain = norm_gain_vector.astype(jnp.float32)
    labels = document_labels[0, 0]
    member = labels[None, :] == jnp.arange(docs, dtype=jnp.int32)[:, None]
    member_f = member.astype(jnp.float32)
    counts = jnp.sum(member_f, axis=1)
    member_b = member.astype(jnp.bfloat16)
    doc_sums = jnp.concatenate(
        [
            dot_nn(member_b, (x * inv_rms[:, None] * g[None, :]).astype(jnp.bfloat16))
            for x, g in zip(states, jnp.split(gain, chunk_count))
        ],
        axis=1,
    )
    pooled = (doc_sums / counts[:, None]).astype(jnp.bfloat16)

    own_blocks = [pooled] + [partner(pooled, "dp", j) for j in range(1, dp)]
    other_blocks = [swap(block, "pair") for block in own_blocks]
    rows = dp * docs
    sums, sorted_oth = call(
        functools.partial(gram_kernel, dp),
        (
            jax.ShapeDtypeStruct((rows + per_shard + 8, anchors), jnp.float32),
            jax.ShapeDtypeStruct((rows, cols), jnp.bfloat16),
        ),
        own_blocks + other_blocks,
        [pltpu.VMEM((rows, cols), jnp.bfloat16)],
    )
    up_parts = jnp.split(adapter_up, chunk_count, axis=1)
    up_states = sum(dot_nt(u, x) for u, x in zip(up_parts, states_b))
    if lax.axis_size("mp") == 2:
        sums = [sums, swap(sums, "mp")]
    else:
        sums = [lax.psum(sums, "mp")]
    losses, doc_grad, small, gained, gain_grad = call(
        functools.partial(loss_kernel, dp, len(sums), chunk_count),
        (
            jax.ShapeDtypeStruct((1, anchors), jnp.float32),
            jax.ShapeDtypeStruct((docs, cols), jnp.float32),
            jax.ShapeDtypeStruct((rank + 8, token_count + 128), jnp.float32),
            jax.ShapeDtypeStruct((docs, cols), jnp.float32),
            jax.ShapeDtypeStruct((1, cols), jnp.float32),
        ),
        sums
        + [
            list_c,
            list_o,
            pooled,
            sorted_oth,
            counts[:, None],
            gain[None],
            doc_sums,
            adapter_up,
            up_states,
            labels[None],
        ]
        + states_b,
    )
    losses = losses[:, :per_shard]
    small = sum_over(small, "mp")
    alpha = inv_rms * inv_rms * inv_rms * small[rank, :token_count] / width
    up_states = small[:rank, :token_count]
    up_gained = small[:rank, token_count : token_count + docs]
    mid_grad = (
        inv_rms * dot_nn(up_gained, member_f, highest) - alpha * up_states
    ).astype(jnp.bfloat16)
    mid_t = lora_mid.astype(jnp.float32).T
    a_grad = dot_nn(mid_grad, own_cols)
    mid_alpha = (mid_t * alpha).astype(jnp.bfloat16)
    b_grad = dot_nn(dot_nt(mid_t * inv_rms, member_f, highest), gained, highest) - jnp.concatenate(
        [dot_nn(mid_alpha, x) for x in states_b], axis=1
    )

    grads = jnp.concatenate([a_grad, b_grad, gain_grad], axis=0)
    half = cols // 2
    kept = lax.dynamic_slice_in_dim(grads, side * half, half, 1)
    sent = lax.dynamic_slice_in_dim(grads, (1 - side) * half, half, 1)
    kept = kept + swap(sent, "pair")
    level = [kept] + [partner(kept, "dp", j) for j in range(1, dp)]
    while len(level) > 1:
        level = [level[i] + level[i + 1] for i in range(0, len(level), 2)]
    total = level[0]
    received = swap(total, "pair")
    grads = jnp.concatenate(
        [jnp.where(side == 0, total, received), jnp.where(side == 0, received, total)], axis=1
    )
    return (
        losses,
        doc_grad[None, None],
        grads[:rank].T,
        grads[rank : 2 * rank],
        grads[2 * rank],
    )


def solution(mesh):
    in_specs = (
        P("pair", ("groups", "dp"), None),
        P("pair", ("groups", "dp"), None),
        P("dp", "mp"),
        P(),
        P(None, "mp"),
        P("mp"),
        P("pair", "groups", None),
        P("pair", "groups", None),
    )
    out_specs = (
        P("pair", ("groups", "dp")),
        P("pair", ("groups", "dp"), None, "mp"),
        P(("groups", "mp"), None),
        P("groups", "mp"),
        P(("groups", "mp")),
    )
    return jax.shard_map(body, mesh=mesh, in_specs=in_specs, out_specs=out_specs, check_vma=False)
```

```python
import functools

import jax
import jax.numpy as jnp
from jax import lax
from jax.experimental import pallas as pl
from jax.experimental.pallas import tpu as pltpu
from jax.sharding import PartitionSpec as P

inverse_temp = 50.0
highest = lax.Precision.HIGHEST
chunk_count = 2


def dot_nt(a, b, precision=None):
    return lax.dot_general(
        a, b, (((1,), (1,)), ((), ())), precision=precision, preferred_element_type=jnp.float32
    )


def dot_nn(a, b, precision=None):
    return jnp.dot(a, b, precision=precision, preferred_element_type=jnp.float32)


def swap(x, axis):
    return lax.ppermute(x, axis, [(0, 1), (1, 0)])


def partner(x, axis, flip):
    return lax.ppermute(x, axis, [(i, i ^ flip) for i in range(lax.axis_size(axis))])


def sum_over(x, axis):
    if lax.axis_size(axis) == 2:
        return x + swap(x, axis)
    return lax.psum(x, axis)


def call(kernel, outs, args, scratch=(), flops=1 << 24):
    size = sum(a.size * a.dtype.itemsize for a in args)
    return pl.pallas_call(
        kernel,
        out_shape=outs,
        scratch_shapes=list(scratch),
        compiler_params=pltpu.CompilerParams(vmem_limit_bytes=48 << 20),
        cost_estimate=pl.CostEstimate(flops=flops, bytes_accessed=size, transcendentals=0),
    )(*args)


def as_row(column):
    size = column.shape[0]
    eye = lax.broadcasted_iota(jnp.int32, (size, size), 0) == lax.broadcasted_iota(
        jnp.int32, (size, size), 1
    )
    return jnp.sum(jnp.where(eye, column, 0.0), axis=0, keepdims=True)


def as_column(row):
    size = row.shape[1]
    eye = lax.broadcasted_iota(jnp.int32, (size, size), 0) == lax.broadcasted_iota(
        jnp.int32, (size, size), 1
    )
    return jnp.sum(jnp.where(eye, row, 0.0), axis=1, keepdims=True)


def gram_kernel(blocks, *refs):
    own, oth = refs[:blocks], refs[blocks : 2 * blocks]
    out_ref, sorted_ref, own_ref = refs[2 * blocks :]
    docs = own[0].shape[0]
    half = docs // 2
    anchors = blocks * half
    for j in range(blocks):
        own_ref[j * docs : (j + 1) * docs] = own[j][...]
        sorted_ref[j * half : (j + 1) * half] = oth[j][:half]
        sorted_ref[anchors + j * half : anchors + (j + 1) * half] = oth[j][half:]
    rows = blocks * docs
    out_ref[:rows] = dot_nt(own_ref[...], sorted_ref[:anchors])
    out_ref[rows : rows + half] = dot_nt(own[0][:half], sorted_ref[anchors:])
    own_f = own_ref[...].astype(jnp.float32)
    oth_f = sorted_ref[...].astype(jnp.float32)
    own_sq = as_row(jnp.sum(own_f * own_f, axis=1, keepdims=True))
    oth_sq = as_row(jnp.sum(oth_f * oth_f, axis=1, keepdims=True))
    tail = jnp.concatenate(
        [
            own_sq[:, :anchors],
            own_sq[:, anchors:],
            oth_sq[:, :anchors],
            oth_sq[:, anchors:],
            jnp.zeros((4, anchors), jnp.float32),
        ],
        axis=0,
    )
    out_ref[rows + half :] = tail


def loss_kernel(blocks, sums_count, chunks, *refs):
    sums_refs = refs[:sums_count]
    list_c, list_o, pooled_ref, oth_ref, counts_ref, gain_ref, doc_sums_ref, up_ref = refs[
        sums_count : sums_count + 8
    ]
    up_states_ref, labels_ref = refs[sums_count + 8 : sums_count + 10]
    state_refs = refs[sums_count + 10 : sums_count + 10 + chunks]
    losses_ref, doc_grad_ref, small_ref, gained_ref, gain_grad_ref = refs[
        sums_count + 10 + chunks :
    ]
    docs = pooled_ref.shape[0]
    half = docs // 2
    anchors = blocks * half
    rows = blocks * docs
    fanout = list_o.shape[1]
    sums = sums_refs[0][...]
    if sums_count == 2:
        sums = sums + sums_refs[1][...]
    inner_c = sums[:rows]
    inner_o = sums[rows : rows + half]
    scales = lax.rsqrt(sums[rows + half :] + 1e-06)
    own_scale = as_column(jnp.concatenate([scales[0:1], scales[1:2]], axis=1))
    oth_scale = scales[2:3]
    pool_scale = scales[3:4]

    row_id = lax.broadcasted_iota(jnp.int32, (rows, anchors), 0)
    col_id = lax.broadcasted_iota(jnp.int32, (rows, anchors), 1)
    mask_c = (row_id % docs) < half
    for h in range(fanout):
        mask_c = mask_c | (row_id == list_c[h : h + 1, :])
    target_c = row_id == (col_id // half) * docs + col_id % half
    logits_c = inverse_temp * (inner_c * own_scale * oth_scale)
    exp_all = jnp.exp(logits_c)
    exp_c = jnp.where(mask_c, exp_all, 0.0)
    total_c = jnp.sum(exp_c, axis=0, keepdims=True)
    losses_ref[...] = jnp.log(total_c) - jnp.sum(
        jnp.where(target_c, logits_c, 0.0), axis=0, keepdims=True
    )
    target_own = target_c[:docs].astype(jnp.float32)
    grad_c = inverse_temp * (exp_c[:docs] / total_c - target_own)

    logits_o = inverse_temp * (inner_o * own_scale[:half] * pool_scale)
    pool_id = lax.broadcasted_iota(jnp.int32, (half, anchors), 1)
    mask_o = pool_id == list_o[:, 0:1]
    for h in range(1, fanout):
        mask_o = mask_o | (pool_id == list_o[:, h : h + 1])
    exp_o = jnp.where(mask_o, jnp.exp(logits_o), 0.0)
    exp_a = exp_all[:half]
    total_o = jnp.sum(exp_a, axis=1, keepdims=True) + jnp.sum(exp_o, axis=1, keepdims=True)
    grad_a = inverse_temp * (exp_a / total_o - target_own[:half])
    grad_o = inverse_temp * (exp_o / total_o)

    zeros = jnp.zeros((docs - half, anchors), jnp.float32)
    coef = jnp.concatenate(
        [
            (grad_c + jnp.concatenate([grad_a, zeros], axis=0)) * oth_scale,
            jnp.concatenate([grad_o * pool_scale, zeros], axis=0),
        ],
        axis=1,
    ).astype(jnp.bfloat16)
    inner = jnp.concatenate(
        [inner_c[:docs], jnp.concatenate([inner_o, zeros], axis=0)], axis=1
    )
    doc_grad = dot_nn(coef, oth_ref[...])
    doc_grad_ref[...] = doc_grad
    scale = own_scale[:docs]
    unit_dots = jnp.sum(coef.astype(jnp.float32) * inner, axis=1, keepdims=True) * scale
    pooled = pooled_ref[...].astype(jnp.float32)
    per_doc = (doc_grad - pooled * (scale * unit_dots)) * (scale / counts_ref[...])
    gain = gain_ref[...]
    gained = per_doc * gain
    gained_ref[...] = gained
    gain_grad_ref[...] = jnp.sum(per_doc * doc_sums_ref[...], axis=0, keepdims=True) / gain

    gained_b = gained.astype(jnp.bfloat16)
    chunk = state_refs[0].shape[1]
    tok_doc = dot_nt(gained_b[:, :chunk], state_refs[0][...])
    for i in range(1, chunks):
        tok_doc = tok_doc + dot_nt(
            gained_b[:, i * chunk : (i + 1) * chunk], state_refs[i][...]
        )
    tokens = tok_doc.shape[1]
    rank = up_ref.shape[0]
    doc_id = lax.broadcasted_iota(jnp.int32, (docs, tokens), 0)
    tok_dots = jnp.sum(
        jnp.where(doc_id == labels_ref[...], tok_doc, 0.0), axis=0, keepdims=True
    )
    up_gained = dot_nt(up_ref[...].astype(jnp.float32), gained, highest)
    small_ref[...] = jnp.zeros_like(small_ref)
    small_ref[:rank, :tokens] = up_states_ref[...]
    small_ref[:rank, tokens : tokens + docs] = up_gained
    small_ref[rank : rank + 1, :tokens] = tok_dots


def body(
    hidden,
    document_labels,
    frozen_weight,
    adapter_down,
    adapter_up,
    norm_gain_vector,
    negative_owner,
    negative_pool_row,
):
    tokens = hidden[0]
    token_count, width = tokens.shape
    cols = adapter_up.shape[1]
    rank = adapter_up.shape[0]
    dp = lax.axis_size("dp")
    side = lax.axis_index("pair")
    shard = lax.axis_index("dp")
    anchors = negative_owner.shape[1]
    per_shard = anchors // dp
    docs = 2 * per_shard

    order = [0] + list(range(1, dp, 2)) + list(range(dp - 2 + dp % 2, 0, -2))
    hops = [(order[i], order[(i + 1) % dp]) for i in range(dp)]
    order_table = jnp.array(order, jnp.int32)
    place_table = jnp.array([order.index(i) for i in range(dp)], jnp.int32)
    place = place_table[shard]

    block_shard = order_table[(place - jnp.arange(dp, dtype=jnp.int32)) % dp]
    owner_block = (place - place_table[negative_owner[0]]) % dp
    rel_list = (owner_block * docs + per_shard + negative_pool_row[0]).reshape(dp, per_shard, -1)
    list_c = rel_list[block_shard].reshape(anchors, -1).T
    pool_col = owner_block * per_shard + negative_pool_row[0]
    list_o = swap(
        lax.dynamic_slice_in_dim(pool_col, shard * per_shard, per_shard, 0), "pair"
    )

    group = lax.axis_index("groups")
    quarter = frozen_weight.shape[0] // 4
    shard_rows = frozen_weight.shape[0]
    chunk = cols // chunk_count
    quarters = [
        (group * 2 + side),
        ((1 - group) * 2 + side),
        (group * 2 + 1 - side),
        ((1 - group) * 2 + 1 - side),
    ]
    moving = [
        lax.dynamic_slice(frozen_weight, (quarters[0] * quarter, h * chunk), (quarter, chunk))
        for h in range(chunk_count)
    ]
    lora_mid = dot_nn(tokens, adapter_down).astype(jnp.bfloat16)
    own_cols = lax.dynamic_slice_in_dim(tokens, lax.axis_index("mp") * cols, cols, 1)
    own_tokens = lax.dynamic_slice_in_dim(tokens, shard * shard_rows, shard_rows, 1)
    states = [None] * chunk_count
    for step in range(1, dp):
        origin = order_table[(place - step) % dp]
        step_tokens = jnp.concatenate(
            [
                lax.dynamic_slice_in_dim(tokens, origin * shard_rows + q * quarter, quarter, 1)
                for q in quarters
            ],
            axis=1,
        )
        for h in range(chunk_count):
            part = slice(h * chunk, (h + 1) * chunk)
            moving[h] = lax.ppermute(moving[h], "dp", hops)
            if step == 1:
                own_first, mid_first, _ = lax.optimization_barrier((own_tokens, lora_mid, moving[h]))
                states[h] = (
                    own_cols[:, part].astype(jnp.float32)
                    + dot_nn(own_first, frozen_weight[:, part])
                    + dot_nn(mid_first, adapter_up[:, part])
                )
            across = swap(moving[h], "groups")
            rows = [moving[h], across, swap(moving[h], "pair"), swap(across, "pair")]
            states[h] = states[h] + dot_nn(step_tokens, jnp.concatenate(rows, axis=0))
    states_b = [x.astype(jnp.bfloat16) for x in states]
    squares = sum_over(sum(jnp.sum(x * x, axis=1) for x in states), "mp")
    inv_rms = lax.rsqrt(squares / width + 1e-05)

    gain = norm_gain_vector.astype(jnp.float32)
    labels = document_labels[0, 0]
    member = labels[None, :] == jnp.arange(docs, dtype=jnp.int32)[:, None]
    member_f = member.astype(jnp.float32)
    counts = jnp.sum(member_f, axis=1)
    member_b = member.astype(jnp.bfloat16)
    doc_sums = jnp.concatenate(
        [
            dot_nn(member_b, (x * inv_rms[:, None] * g[None, :]).astype(jnp.bfloat16))
            for x, g in zip(states, jnp.split(gain, chunk_count))
        ],
        axis=1,
    )
    pooled = (doc_sums / counts[:, None]).astype(jnp.bfloat16)

    own_blocks = [pooled]
    for _ in range(1, dp):
        own_blocks.append(lax.ppermute(own_blocks[-1], "dp", hops))
    other_blocks = [swap(block, "pair") for block in own_blocks]
    rows = dp * docs
    sums, sorted_oth = call(
        functools.partial(gram_kernel, dp),
        (
            jax.ShapeDtypeStruct((rows + per_shard + 8, anchors), jnp.float32),
            jax.ShapeDtypeStruct((rows, cols), jnp.bfloat16),
        ),
        own_blocks + other_blocks,
        [pltpu.VMEM((rows, cols), jnp.bfloat16)],
    )
    up_parts = jnp.split(adapter_up, chunk_count, axis=1)
    up_states = sum(dot_nt(u, x) for u, x in zip(up_parts, states_b))
    if lax.axis_size("mp") == 2:
        sums = [sums, swap(sums, "mp")]
    else:
        sums = [lax.psum(sums, "mp")]
    losses, doc_grad, small, gained, gain_grad = call(
        functools.partial(loss_kernel, dp, len(sums), chunk_count),
        (
            jax.ShapeDtypeStruct((1, anchors), jnp.float32),
            jax.ShapeDtypeStruct((docs, cols), jnp.float32),
            jax.ShapeDtypeStruct((rank + 8, token_count + 128), jnp.float32),
            jax.ShapeDtypeStruct((docs, cols), jnp.float32),
            jax.ShapeDtypeStruct((1, cols), jnp.float32),
        ),
        sums
        + [
            list_c,
            list_o,
            pooled,
            sorted_oth,
            counts[:, None],
            gain[None],
            doc_sums,
            adapter_up,
            up_states,
            labels[None],
        ]
        + states_b,
    )
    losses = losses[:, :per_shard]
    small = sum_over(small, "mp")
    alpha = inv_rms * inv_rms * inv_rms * small[rank, :token_count] / width
    up_states = small[:rank, :token_count]
    up_gained = small[:rank, token_count : token_count + docs]
    mid_grad = (
        inv_rms * dot_nn(up_gained, member_f, highest) - alpha * up_states
    ).astype(jnp.bfloat16)
    mid_t = lora_mid.astype(jnp.float32).T
    a_grad = dot_nn(mid_grad, own_cols)
    mid_alpha = (mid_t * alpha).astype(jnp.bfloat16)
    b_grad = dot_nn(dot_nt(mid_t * inv_rms, member_f, highest), gained, highest) - jnp.concatenate(
        [dot_nn(mid_alpha, x) for x in states_b], axis=1
    )

    grads = jnp.concatenate([a_grad, b_grad, gain_grad], axis=0)
    half = cols // 2
    kept = lax.dynamic_slice_in_dim(grads, side * half, half, 1)
    sent = lax.dynamic_slice_in_dim(grads, (1 - side) * half, half, 1)
    kept = kept + swap(sent, "pair")
    piece = half // dp
    parts = kept.reshape(-1, dp, piece)

    def part_of(owner):
        return lax.dynamic_index_in_dim(parts, owner, 1, keepdims=False)

    total = part_of(shard)
    for j in range(1, dp):
        total = total + partner(part_of(shard ^ j), "dp", j)
    gathered = jnp.stack([total] + [partner(total, "dp", j) for j in range(1, dp)], axis=1)
    total = jnp.concatenate(
        [
            lax.dynamic_index_in_dim(gathered, shard ^ j, 1, keepdims=False)
            for j in range(dp)
        ],
        axis=1,
    )
    received = swap(total, "pair")
    grads = jnp.concatenate(
        [jnp.where(side == 0, total, received), jnp.where(side == 0, received, total)], axis=1
    )
    return (
        losses,
        doc_grad[None, None],
        grads[:rank].T,
        grads[rank : 2 * rank],
        grads[2 * rank],
    )


def solution(mesh):
    in_specs = (
        P("pair", ("groups", "dp"), None),
        P("pair", ("groups", "dp"), None),
        P("dp", "mp"),
        P(),
        P(None, "mp"),
        P("mp"),
        P("pair", "groups", None),
        P("pair", "groups", None),
    )
    out_specs = (
        P("pair", ("groups", "dp")),
        P("pair", ("groups", "dp"), None, "mp"),
        P(("groups", "mp"), None),
        P("groups", "mp"),
        P(("groups", "mp")),
    )
    return jax.shard_map(body, mesh=mesh, in_specs=in_specs, out_specs=out_specs, check_vma=False)
```

```python
import functools

import jax
import jax.numpy as jnp
from jax import lax
from jax.experimental import pallas as pl
from jax.experimental.pallas import tpu as pltpu
from jax.sharding import PartitionSpec as P

inverse_temp = 50.0
highest = lax.Precision.HIGHEST
chunk_count = 2


def dot_nt(a, b, precision=None):
    return lax.dot_general(
        a, b, (((1,), (1,)), ((), ())), precision=precision, preferred_element_type=jnp.float32
    )


def dot_nn(a, b, precision=None):
    return jnp.dot(a, b, precision=precision, preferred_element_type=jnp.float32)


def swap(x, axis):
    return lax.ppermute(x, axis, [(0, 1), (1, 0)])


def partner(x, axis, flip):
    return lax.ppermute(x, axis, [(i, i ^ flip) for i in range(lax.axis_size(axis))])


def sum_over(x, axis):
    if lax.axis_size(axis) == 2:
        return x + swap(x, axis)
    return lax.psum(x, axis)


def widths(cols):
    tiles = cols // 128
    base, more = divmod(tiles, chunk_count)
    return [128 * (base + (i >= chunk_count - more)) for i in range(chunk_count)]


def spans(cols):
    out, at = [], 0
    for width in widths(cols):
        out.append((at, at + width))
        at += width
    return out


def after(x, *deps):
    return lax.optimization_barrier((x, *deps))[0]


def call(kernel, outs, args, scratch=(), flops=1 << 24, vmem=16):
    size = sum(a.size * a.dtype.itemsize for a in args)
    return pl.pallas_call(
        kernel,
        out_shape=outs,
        scratch_shapes=list(scratch),
        compiler_params=pltpu.CompilerParams(vmem_limit_bytes=vmem << 20),
        cost_estimate=pl.CostEstimate(flops=flops, bytes_accessed=size, transcendentals=0),
    )(*args)


def as_row(column):
    size = column.shape[0]
    eye = lax.broadcasted_iota(jnp.int32, (size, size), 0) == lax.broadcasted_iota(
        jnp.int32, (size, size), 1
    )
    return jnp.sum(jnp.where(eye, column, 0.0), axis=0, keepdims=True)


def as_column(row):
    size = row.shape[1]
    eye = lax.broadcasted_iota(jnp.int32, (size, size), 0) == lax.broadcasted_iota(
        jnp.int32, (size, size), 1
    )
    return jnp.sum(jnp.where(eye, row, 0.0), axis=1, keepdims=True)


def gram_kernel(blocks, *refs):
    own, oth = refs[: 2 * blocks], refs[2 * blocks : 4 * blocks]
    out_ref, sorted_ref, own_ref = refs[4 * blocks :]
    half = own[0].shape[0]
    docs = 2 * half
    anchors = blocks * half
    for j in range(blocks):
        own_ref[j * docs : j * docs + half] = own[j][...]
        own_ref[j * docs + half : (j + 1) * docs] = own[blocks + j][...]
        sorted_ref[j * half : (j + 1) * half] = oth[j][...]
        sorted_ref[anchors + j * half : anchors + (j + 1) * half] = oth[blocks + j][...]
    rows = blocks * docs
    out_ref[:rows] = dot_nt(own_ref[...], sorted_ref[:anchors])
    out_ref[rows : rows + half] = dot_nt(own[0][...], sorted_ref[anchors:])
    own_f = own_ref[...].astype(jnp.float32)
    oth_f = sorted_ref[...].astype(jnp.float32)
    own_sq = as_row(jnp.sum(own_f * own_f, axis=1, keepdims=True))
    oth_sq = as_row(jnp.sum(oth_f * oth_f, axis=1, keepdims=True))
    tail = jnp.concatenate(
        [
            own_sq[:, :anchors],
            own_sq[:, anchors:],
            oth_sq[:, :anchors],
            oth_sq[:, anchors:],
            jnp.zeros((4, anchors), jnp.float32),
        ],
        axis=0,
    )
    out_ref[rows + half :] = tail


def loss_kernel(blocks, sums_count, chunks, *refs):
    sums_refs = refs[:sums_count]
    list_c, list_o, pooled_ref, oth_ref, counts_ref, gain_ref, doc_sums_ref, up_ref = refs[
        sums_count : sums_count + 8
    ]
    up_states_ref, labels_ref = refs[sums_count + 8 : sums_count + 10]
    state_refs = refs[sums_count + 10 : sums_count + 10 + chunks]
    losses_ref, doc_grad_ref, small_ref, gained_ref, gain_grad_ref = refs[
        sums_count + 10 + chunks :
    ]
    docs = pooled_ref.shape[0]
    half = docs // 2
    anchors = blocks * half
    rows = blocks * docs
    fanout = list_o.shape[1]
    sums = sums_refs[0][...]
    if sums_count == 2:
        sums = sums + sums_refs[1][...]
    inner_c = sums[:rows]
    inner_o = sums[rows : rows + half]
    scales = lax.rsqrt(sums[rows + half :] + 1e-06)
    own_scale = as_column(jnp.concatenate([scales[0:1], scales[1:2]], axis=1))
    oth_scale = scales[2:3]
    pool_scale = scales[3:4]

    row_id = lax.broadcasted_iota(jnp.int32, (rows, anchors), 0)
    col_id = lax.broadcasted_iota(jnp.int32, (rows, anchors), 1)
    mask_c = (row_id % docs) < half
    for h in range(fanout):
        mask_c = mask_c | (row_id == list_c[h : h + 1, :])
    target_c = row_id == (col_id // half) * docs + col_id % half
    logits_c = inverse_temp * (inner_c * own_scale * oth_scale)
    exp_all = jnp.exp(logits_c)
    exp_c = jnp.where(mask_c, exp_all, 0.0)
    total_c = jnp.sum(exp_c, axis=0, keepdims=True)
    losses_ref[...] = jnp.log(total_c) - jnp.sum(
        jnp.where(target_c, logits_c, 0.0), axis=0, keepdims=True
    )
    target_own = target_c[:docs].astype(jnp.float32)
    grad_c = inverse_temp * (exp_c[:docs] / total_c - target_own)

    logits_o = inverse_temp * (inner_o * own_scale[:half] * pool_scale)
    pool_id = lax.broadcasted_iota(jnp.int32, (half, anchors), 1)
    mask_o = pool_id == list_o[:, 0:1]
    for h in range(1, fanout):
        mask_o = mask_o | (pool_id == list_o[:, h : h + 1])
    exp_o = jnp.where(mask_o, jnp.exp(logits_o), 0.0)
    exp_a = exp_all[:half]
    total_o = jnp.sum(exp_a, axis=1, keepdims=True) + jnp.sum(exp_o, axis=1, keepdims=True)
    grad_a = inverse_temp * (exp_a / total_o - target_own[:half])
    grad_o = inverse_temp * (exp_o / total_o)

    zeros = jnp.zeros((docs - half, anchors), jnp.float32)
    coef = jnp.concatenate(
        [
            (grad_c + jnp.concatenate([grad_a, zeros], axis=0)) * oth_scale,
            jnp.concatenate([grad_o * pool_scale, zeros], axis=0),
        ],
        axis=1,
    ).astype(jnp.bfloat16)
    inner = jnp.concatenate(
        [inner_c[:docs], jnp.concatenate([inner_o, zeros], axis=0)], axis=1
    )
    doc_grad = dot_nn(coef, oth_ref[...])
    doc_grad_ref[...] = doc_grad
    scale = own_scale[:docs]
    unit_dots = jnp.sum(coef.astype(jnp.float32) * inner, axis=1, keepdims=True) * scale
    pooled = pooled_ref[...].astype(jnp.float32)
    per_doc = (doc_grad - pooled * (scale * unit_dots)) * (scale / counts_ref[...])
    gain = gain_ref[...]
    gained = per_doc * gain
    gained_ref[...] = gained
    gain_grad_ref[...] = jnp.sum(per_doc * doc_sums_ref[...], axis=0, keepdims=True) / gain

    gained_b = gained.astype(jnp.bfloat16)
    tok_doc = 0.0
    for (low, high), state_ref in zip(spans(gained_b.shape[1]), state_refs):
        tok_doc = tok_doc + dot_nt(gained_b[:, low:high], state_ref[...])
    tokens = tok_doc.shape[1]
    rank = up_ref.shape[0]
    doc_id = lax.broadcasted_iota(jnp.int32, (docs, tokens), 0)
    tok_dots = jnp.sum(
        jnp.where(doc_id == labels_ref[...], tok_doc, 0.0), axis=0, keepdims=True
    )
    up_gained = dot_nt(up_ref[...].astype(jnp.float32), gained, highest)
    small_ref[...] = jnp.zeros_like(small_ref)
    small_ref[:rank, :tokens] = up_states_ref[...]
    small_ref[:rank, tokens : tokens + docs] = up_gained
    small_ref[rank : rank + 1, :tokens] = tok_dots


def body(
    hidden,
    document_labels,
    frozen_weight,
    adapter_down,
    adapter_up,
    norm_gain_vector,
    negative_owner,
    negative_pool_row,
):
    tokens = hidden[0]
    token_count, width = tokens.shape
    cols = adapter_up.shape[1]
    rank = adapter_up.shape[0]
    dp = lax.axis_size("dp")
    side = lax.axis_index("pair")
    shard = lax.axis_index("dp")
    anchors = negative_owner.shape[1]
    per_shard = anchors // dp
    docs = 2 * per_shard

    order = [0] + list(range(1, dp, 2)) + list(range(dp - 2 + dp % 2, 0, -2))
    hops = [(order[i], order[(i + 1) % dp]) for i in range(dp)]
    order_table = jnp.array(order, jnp.int32)
    place_table = jnp.array([order.index(i) for i in range(dp)], jnp.int32)
    place = place_table[shard]

    block_shard = order_table[(place - jnp.arange(dp, dtype=jnp.int32)) % dp]
    owner_block = (place - place_table[negative_owner[0]]) % dp
    rel_list = (owner_block * docs + per_shard + negative_pool_row[0]).reshape(dp, per_shard, -1)
    list_c = rel_list[block_shard].reshape(anchors, -1).T
    pool_col = owner_block * per_shard + negative_pool_row[0]
    list_o = swap(
        lax.dynamic_slice_in_dim(pool_col, shard * per_shard, per_shard, 0), "pair"
    )

    group = lax.axis_index("groups")
    quarter = frozen_weight.shape[0] // 4
    shard_rows = frozen_weight.shape[0]
    parts = spans(cols)
    quarters = [
        (group * 2 + side),
        ((1 - group) * 2 + side),
        (group * 2 + 1 - side),
        ((1 - group) * 2 + 1 - side),
    ]
    moving = []
    for low, high in parts:
        corner = quarters[0] * quarter
        moving.append(lax.dynamic_slice(frozen_weight, (corner, low), (quarter, high - low)))
    lora_mid = dot_nn(tokens, adapter_down).astype(jnp.bfloat16)
    own_cols = lax.dynamic_slice_in_dim(tokens, lax.axis_index("mp") * cols, cols, 1)
    own_tokens = lax.dynamic_slice_in_dim(tokens, shard * shard_rows, shard_rows, 1)
    states = [None] * chunk_count
    ringed = []
    for step in range(1, dp):
        for h in range(chunk_count):
            ringed.append(lax.ppermute(ringed[-chunk_count] if step > 1 else moving[h], "dp", hops))
    event = 0
    for step in range(1, dp):
        origin = order_table[(place - step) % dp]
        step_tokens = jnp.concatenate(
            [
                lax.dynamic_slice_in_dim(tokens, origin * shard_rows + q * quarter, quarter, 1)
                for q in quarters
            ],
            axis=1,
        )
        for h, (low, high) in enumerate(parts):
            moved = ringed[event]
            if step == 1:
                own_first, mid_first = own_tokens, lora_mid
                own_first, mid_first = after((own_first, mid_first), moved)
                states[h] = (
                    own_cols[:, low:high].astype(jnp.float32)
                    + dot_nn(own_first, frozen_weight[:, low:high])
                    + dot_nn(mid_first, adapter_up[:, low:high])
                )
            across = swap(moved, "groups")
            lhs = step_tokens
            rows = [moved, across, swap(moved, "pair"), swap(across, "pair")]
            states[h] = states[h] + dot_nn(lhs, jnp.concatenate(rows, axis=0))
            event += 1
    states_b = [x.astype(jnp.bfloat16) for x in states]
    squares = sum_over(sum(jnp.sum(x * x, axis=1) for x in states), "mp")
    inv_rms = lax.rsqrt(squares / width + 1e-05)

    gain = norm_gain_vector.astype(jnp.float32)
    labels = document_labels[0, 0]
    member = labels[None, :] == jnp.arange(docs, dtype=jnp.int32)[:, None]
    member_f = member.astype(jnp.float32)
    counts = jnp.sum(member_f, axis=1)
    member_b = member.astype(jnp.bfloat16)
    doc_sums = jnp.concatenate(
        [
            dot_nn(member_b, (x * inv_rms[:, None] * g[None, :]).astype(jnp.bfloat16))
            for x, g in zip(states, [gain[low:high] for low, high in parts])
        ],
        axis=1,
    )
    pooled = (doc_sums / counts[:, None]).astype(jnp.bfloat16)

    own_anchors, own_pools = [pooled[:per_shard]], [pooled[per_shard:]]
    for _ in range(1, dp):
        own_anchors.append(lax.ppermute(own_anchors[-1], "dp", hops))
        own_pools.append(lax.ppermute(own_pools[-1], "dp", hops))
    own_blocks = own_anchors + own_pools
    other_blocks = [swap(block, "pair") for block in own_blocks]
    rows = dp * docs
    sums, sorted_oth = call(
        functools.partial(gram_kernel, dp),
        (
            jax.ShapeDtypeStruct((rows + per_shard + 8, anchors), jnp.float32),
            jax.ShapeDtypeStruct((rows, cols), jnp.bfloat16),
        ),
        own_blocks + other_blocks,
        [pltpu.VMEM((rows, cols), jnp.bfloat16)],
        vmem=16 if dp <= 4 else 48,
    )
    up_parts = [adapter_up[:, low:high] for low, high in parts]
    up_states = sum(dot_nt(u, x) for u, x in zip(up_parts, states_b))
    if lax.axis_size("mp") == 2:
        sums = [sums, swap(sums, "mp")]
    else:
        sums = [lax.psum(sums, "mp")]
    losses, doc_grad, small, gained, gain_grad = call(
        functools.partial(loss_kernel, dp, len(sums), chunk_count),
        (
            jax.ShapeDtypeStruct((1, anchors), jnp.float32),
            jax.ShapeDtypeStruct((docs, cols), jnp.float32),
            jax.ShapeDtypeStruct((rank + 8, token_count + 128), jnp.float32),
            jax.ShapeDtypeStruct((docs, cols), jnp.float32),
            jax.ShapeDtypeStruct((1, cols), jnp.float32),
        ),
        sums
        + [
            list_c,
            list_o,
            pooled,
            sorted_oth,
            counts[:, None],
            gain[None],
            doc_sums,
            adapter_up,
            up_states,
            labels[None],
        ]
        + states_b,
        vmem=16 if dp <= 4 else 48,
    )
    losses = losses[:, :per_shard]
    small = sum_over(small, "mp")
    alpha = inv_rms * inv_rms * inv_rms * small[rank, :token_count] / width
    up_states = small[:rank, :token_count]
    up_gained = small[:rank, token_count : token_count + docs]
    mid_grad = (
        inv_rms * dot_nn(up_gained, member_f, highest) - alpha * up_states
    ).astype(jnp.bfloat16)
    mid_t = lora_mid.astype(jnp.float32).T
    a_grad = dot_nn(mid_grad, own_cols)
    mid_alpha = (mid_t * alpha).astype(jnp.bfloat16)
    b_grad = dot_nn(dot_nt(mid_t * inv_rms, member_f, highest), gained, highest) - jnp.concatenate(
        [dot_nn(mid_alpha, x) for x in states_b], axis=1
    )

    grads = jnp.concatenate([a_grad, b_grad, gain_grad], axis=0)
    half = cols // 2
    kept = lax.dynamic_slice_in_dim(grads, side * half, half, 1)
    sent = lax.dynamic_slice_in_dim(grads, (1 - side) * half, half, 1)
    kept = kept + swap(sent, "pair")
    kept = kept.astype(jnp.bfloat16)
    level = [kept] + [partner(kept, "dp", j) for j in range(1, dp)]
    level = [x.astype(jnp.float32) for x in level]
    while len(level) > 1:
        level = [level[i] + level[i + 1] for i in range(0, len(level), 2)]
    total = level[0]
    received = swap(total, "pair")
    grads = jnp.concatenate(
        [jnp.where(side == 0, total, received), jnp.where(side == 0, received, total)], axis=1
    )
    return (
        losses,
        doc_grad[None, None],
        grads[:rank].T,
        grads[rank : 2 * rank],
        grads[2 * rank],
    )


def solution(mesh):
    in_specs = (
        P("pair", ("groups", "dp"), None),
        P("pair", ("groups", "dp"), None),
        P("dp", "mp"),
        P(),
        P(None, "mp"),
        P("mp"),
        P("pair", "groups", None),
        P("pair", "groups", None),
    )
    out_specs = (
        P("pair", ("groups", "dp")),
        P("pair", ("groups", "dp"), None, "mp"),
        P(("groups", "mp"), None),
        P("groups", "mp"),
        P(("groups", "mp")),
    )
    return jax.shard_map(body, mesh=mesh, in_specs=in_specs, out_specs=out_specs, check_vma=False)
```

```python
import functools

import jax
import jax.numpy as jnp
from jax import lax
from jax.experimental import pallas as pl
from jax.experimental.pallas import tpu as pltpu
from jax.sharding import PartitionSpec as P

inverse_temp = 50.0
highest = lax.Precision.HIGHEST
chunk_count = 2


def dot_nt(a, b, precision=None):
    return lax.dot_general(
        a, b, (((1,), (1,)), ((), ())), precision=precision, preferred_element_type=jnp.float32
    )


def dot_nn(a, b, precision=None):
    return jnp.dot(a, b, precision=precision, preferred_element_type=jnp.float32)


def swap(x, axis):
    return lax.ppermute(x, axis, [(0, 1), (1, 0)])


def partner(x, axis, flip):
    return lax.ppermute(x, axis, [(i, i ^ flip) for i in range(lax.axis_size(axis))])


def sum_over(x, axis):
    if lax.axis_size(axis) == 2:
        return x + swap(x, axis)
    return lax.psum(x, axis)


def widths(cols):
    tiles = cols // 128
    base, more = divmod(tiles, chunk_count)
    return [128 * (base + (i >= chunk_count - more)) for i in range(chunk_count)]


def spans(cols):
    out, at = [], 0
    for width in widths(cols):
        out.append((at, at + width))
        at += width
    return out


def after(x, *deps):
    return lax.optimization_barrier((x, *deps))[0]


def call(kernel, outs, args, scratch=(), flops=1 << 24, vmem=16):
    size = sum(a.size * a.dtype.itemsize for a in args)
    return pl.pallas_call(
        kernel,
        out_shape=outs,
        scratch_shapes=list(scratch),
        compiler_params=pltpu.CompilerParams(vmem_limit_bytes=vmem << 20),
        cost_estimate=pl.CostEstimate(flops=flops, bytes_accessed=size, transcendentals=0),
    )(*args)


def as_row(column):
    size = column.shape[0]
    eye = lax.broadcasted_iota(jnp.int32, (size, size), 0) == lax.broadcasted_iota(
        jnp.int32, (size, size), 1
    )
    return jnp.sum(jnp.where(eye, column, 0.0), axis=0, keepdims=True)


def as_column(row):
    size = row.shape[1]
    eye = lax.broadcasted_iota(jnp.int32, (size, size), 0) == lax.broadcasted_iota(
        jnp.int32, (size, size), 1
    )
    return jnp.sum(jnp.where(eye, row, 0.0), axis=1, keepdims=True)


def gram_kernel(blocks, *refs):
    own, oth = refs[:blocks], refs[blocks : 2 * blocks]
    out_ref, sorted_ref, own_ref = refs[2 * blocks :]
    docs = own[0].shape[0]
    half = docs // 2
    anchors = blocks * half
    for j in range(blocks):
        own_ref[j * docs : (j + 1) * docs] = own[j][...]
        sorted_ref[j * half : (j + 1) * half] = oth[j][:half]
        sorted_ref[anchors + j * half : anchors + (j + 1) * half] = oth[j][half:]
    rows = blocks * docs
    out_ref[:rows] = dot_nt(own_ref[...], sorted_ref[:anchors])
    out_ref[rows : rows + half] = dot_nt(own[0][:half], sorted_ref[anchors:])
    own_f = own_ref[...].astype(jnp.float32)
    oth_f = sorted_ref[...].astype(jnp.float32)
    own_sq = as_row(jnp.sum(own_f * own_f, axis=1, keepdims=True))
    oth_sq = as_row(jnp.sum(oth_f * oth_f, axis=1, keepdims=True))
    tail = jnp.concatenate(
        [
            own_sq[:, :anchors],
            own_sq[:, anchors:],
            oth_sq[:, :anchors],
            oth_sq[:, anchors:],
            jnp.zeros((4, anchors), jnp.float32),
        ],
        axis=0,
    )
    out_ref[rows + half :] = tail


def loss_kernel(blocks, sums_count, chunks, *refs):
    sums_refs = refs[:sums_count]
    list_c, list_o, pooled_ref, oth_ref, counts_ref, gain_ref, doc_sums_ref, up_ref = refs[
        sums_count : sums_count + 8
    ]
    up_states_ref, labels_ref = refs[sums_count + 8 : sums_count + 10]
    state_refs = refs[sums_count + 10 : sums_count + 10 + chunks]
    losses_ref, doc_grad_ref, small_ref, gained_ref, gain_grad_ref = refs[
        sums_count + 10 + chunks :
    ]
    docs = pooled_ref.shape[0]
    half = docs // 2
    anchors = blocks * half
    rows = blocks * docs
    fanout = list_o.shape[1]
    sums = sums_refs[0][...]
    if sums_count == 2:
        sums = sums + sums_refs[1][...]
    inner_c = sums[:rows]
    inner_o = sums[rows : rows + half]
    scales = lax.rsqrt(sums[rows + half :] + 1e-06)
    own_scale = as_column(jnp.concatenate([scales[0:1], scales[1:2]], axis=1))
    oth_scale = scales[2:3]
    pool_scale = scales[3:4]

    row_id = lax.broadcasted_iota(jnp.int32, (rows, anchors), 0)
    col_id = lax.broadcasted_iota(jnp.int32, (rows, anchors), 1)
    mask_c = (row_id % docs) < half
    for h in range(fanout):
        mask_c = mask_c | (row_id == list_c[h : h + 1, :])
    target_c = row_id == (col_id // half) * docs + col_id % half
    logits_c = inverse_temp * (inner_c * own_scale * oth_scale)
    exp_all = jnp.exp(logits_c)
    exp_c = jnp.where(mask_c, exp_all, 0.0)
    total_c = jnp.sum(exp_c, axis=0, keepdims=True)
    losses_ref[...] = jnp.log(total_c) - jnp.sum(
        jnp.where(target_c, logits_c, 0.0), axis=0, keepdims=True
    )
    target_own = target_c[:docs].astype(jnp.float32)
    grad_c = inverse_temp * (exp_c[:docs] / total_c - target_own)

    logits_o = inverse_temp * (inner_o * own_scale[:half] * pool_scale)
    pool_id = lax.broadcasted_iota(jnp.int32, (half, anchors), 1)
    mask_o = pool_id == list_o[:, 0:1]
    for h in range(1, fanout):
        mask_o = mask_o | (pool_id == list_o[:, h : h + 1])
    exp_o = jnp.where(mask_o, jnp.exp(logits_o), 0.0)
    exp_a = exp_all[:half]
    total_o = jnp.sum(exp_a, axis=1, keepdims=True) + jnp.sum(exp_o, axis=1, keepdims=True)
    grad_a = inverse_temp * (exp_a / total_o - target_own[:half])
    grad_o = inverse_temp * (exp_o / total_o)

    zeros = jnp.zeros((docs - half, anchors), jnp.float32)
    coef = jnp.concatenate(
        [
            (grad_c + jnp.concatenate([grad_a, zeros], axis=0)) * oth_scale,
            jnp.concatenate([grad_o * pool_scale, zeros], axis=0),
        ],
        axis=1,
    ).astype(jnp.bfloat16)
    inner = jnp.concatenate(
        [inner_c[:docs], jnp.concatenate([inner_o, zeros], axis=0)], axis=1
    )
    doc_grad = dot_nn(coef, oth_ref[...])
    doc_grad_ref[...] = doc_grad
    scale = own_scale[:docs]
    unit_dots = jnp.sum(coef.astype(jnp.float32) * inner, axis=1, keepdims=True) * scale
    pooled = pooled_ref[...].astype(jnp.float32)
    per_doc = (doc_grad - pooled * (scale * unit_dots)) * (scale / counts_ref[...])
    gain = gain_ref[...]
    gained = per_doc * gain
    gained_ref[...] = gained
    gain_grad_ref[...] = jnp.sum(per_doc * doc_sums_ref[...], axis=0, keepdims=True) / gain

    gained_b = gained.astype(jnp.bfloat16)
    tok_doc = 0.0
    for (low, high), state_ref in zip(spans(gained_b.shape[1]), state_refs):
        tok_doc = tok_doc + dot_nt(gained_b[:, low:high], state_ref[...])
    tokens = tok_doc.shape[1]
    rank = up_ref.shape[0]
    doc_id = lax.broadcasted_iota(jnp.int32, (docs, tokens), 0)
    tok_dots = jnp.sum(
        jnp.where(doc_id == labels_ref[...], tok_doc, 0.0), axis=0, keepdims=True
    )
    up_gained = dot_nt(up_ref[...].astype(jnp.float32), gained, highest)
    small_ref[...] = jnp.zeros_like(small_ref)
    small_ref[:rank, :tokens] = up_states_ref[...]
    small_ref[:rank, tokens : tokens + docs] = up_gained
    small_ref[rank : rank + 1, :tokens] = tok_dots


def body(
    hidden,
    document_labels,
    frozen_weight,
    adapter_down,
    adapter_up,
    norm_gain_vector,
    negative_owner,
    negative_pool_row,
):
    tokens = hidden[0]
    token_count, width = tokens.shape
    cols = adapter_up.shape[1]
    rank = adapter_up.shape[0]
    dp = lax.axis_size("dp")
    side = lax.axis_index("pair")
    shard = lax.axis_index("dp")
    anchors = negative_owner.shape[1]
    per_shard = anchors // dp
    docs = 2 * per_shard

    order = [0] + list(range(1, dp, 2)) + list(range(dp - 2 + dp % 2, 0, -2))
    hops = [(order[i], order[(i + 1) % dp]) for i in range(dp)]
    back_hops = [(b, a) for a, b in hops]

    def place_of(index):
        return jnp.where(index % 2 == 1, (index + 1) // 2, (dp - index // 2) % dp)

    def shard_at(position):
        return jnp.where(
            position == 0, 0, jnp.where(position <= dp // 2, 2 * position - 1, 2 * (dp - position))
        )

    place = place_of(shard)

    block_shard = shard_at((place - jnp.arange(dp, dtype=jnp.int32)) % dp)
    owner_block = (place - place_of(negative_owner[0])) % dp
    rel_list = (owner_block * docs + per_shard + negative_pool_row[0]).reshape(dp, per_shard, -1)
    list_c = rel_list[block_shard].reshape(anchors, -1).T
    pool_col = owner_block * per_shard + negative_pool_row[0]
    list_o = swap(
        lax.dynamic_slice_in_dim(pool_col, shard * per_shard, per_shard, 0), "pair"
    )

    group = lax.axis_index("groups")
    quarter = frozen_weight.shape[0] // 4
    shard_rows = frozen_weight.shape[0]
    parts = spans(cols)
    quarters = [
        (group * 2 + side),
        ((1 - group) * 2 + side),
        (group * 2 + 1 - side),
        ((1 - group) * 2 + 1 - side),
    ]
    moving = []
    for low, high in parts:
        corner = quarters[0] * quarter
        moving.append(lax.dynamic_slice(frozen_weight, (corner, low), (quarter, high - low)))
    lora_mid = dot_nn(tokens, adapter_down).astype(jnp.bfloat16)
    own_cols = lax.dynamic_slice_in_dim(tokens, lax.axis_index("mp") * cols, cols, 1)
    own_tokens = lax.dynamic_slice_in_dim(tokens, shard * shard_rows, shard_rows, 1)
    states = [None] * chunk_count
    ringed = []
    for step in range(1, dp):
        for h in range(chunk_count):
            ringed.append(lax.ppermute(ringed[-chunk_count] if step > 1 else moving[h], "dp", hops))
    event = 0
    for step in range(1, dp):
        origin = shard_at((place - step) % dp)
        step_tokens = jnp.concatenate(
            [
                lax.dynamic_slice_in_dim(tokens, origin * shard_rows + q * quarter, quarter, 1)
                for q in quarters
            ],
            axis=1,
        )
        for h, (low, high) in enumerate(parts):
            moved = ringed[event]
            if step == 1:
                own_first, mid_first = own_tokens, lora_mid
                own_first, mid_first = after((own_first, mid_first), moved)
                states[h] = (
                    own_cols[:, low:high].astype(jnp.float32)
                    + dot_nn(own_first, frozen_weight[:, low:high])
                    + dot_nn(mid_first, adapter_up[:, low:high])
                )
            across = swap(moved, "groups")
            lhs = step_tokens
            rows = [moved, across, swap(moved, "pair"), swap(across, "pair")]
            states[h] = states[h] + dot_nn(lhs, jnp.concatenate(rows, axis=0))
            event += 1
    states_b = [x.astype(jnp.bfloat16) for x in states]
    squares = sum_over(sum(jnp.sum(x * x, axis=1) for x in states), "mp")
    inv_rms = lax.rsqrt(squares / width + 1e-05)

    gain = norm_gain_vector.astype(jnp.float32)
    labels = document_labels[0, 0]
    member = labels[None, :] == jnp.arange(docs, dtype=jnp.int32)[:, None]
    member_f = member.astype(jnp.float32)
    counts = jnp.sum(member_f, axis=1)
    member_b = member.astype(jnp.bfloat16)
    doc_sums = jnp.concatenate(
        [
            dot_nn(member_b, (x * inv_rms[:, None] * g[None, :]).astype(jnp.bfloat16))
            for x, g in zip(states, [gain[low:high] for low, high in parts])
        ],
        axis=1,
    )
    pooled = (doc_sums / counts[:, None]).astype(jnp.bfloat16)

    own_blocks = [pooled] * dp
    for j in range(1, dp):
        if j <= dp // 2:
            own_blocks[j] = lax.ppermute(own_blocks[j - 1], "dp", hops)
        else:
            own_blocks[dp + dp // 2 - j] = lax.ppermute(
                own_blocks[(dp + dp // 2 - j + 1) % dp], "dp", back_hops
            )
    other_blocks = [swap(block, "pair") for block in own_blocks]
    rows = dp * docs
    sums, sorted_oth = call(
        functools.partial(gram_kernel, dp),
        (
            jax.ShapeDtypeStruct((rows + per_shard + 8, anchors), jnp.float32),
            jax.ShapeDtypeStruct((rows, cols), jnp.bfloat16),
        ),
        own_blocks + other_blocks,
        [pltpu.VMEM((rows, cols), jnp.bfloat16)],
        vmem=16 if dp <= 4 else 48,
    )
    up_parts = [adapter_up[:, low:high] for low, high in parts]
    up_states = sum(dot_nt(u, x) for u, x in zip(up_parts, states_b))
    if lax.axis_size("mp") == 2:
        sums = [sums, swap(sums, "mp")]
    else:
        sums = [lax.psum(sums, "mp")]
    losses, doc_grad, small, gained, gain_grad = call(
        functools.partial(loss_kernel, dp, len(sums), chunk_count),
        (
            jax.ShapeDtypeStruct((1, anchors), jnp.float32),
            jax.ShapeDtypeStruct((docs, cols), jnp.float32),
            jax.ShapeDtypeStruct((rank + 8, token_count + 128), jnp.float32),
            jax.ShapeDtypeStruct((docs, cols), jnp.float32),
            jax.ShapeDtypeStruct((1, cols), jnp.float32),
        ),
        sums
        + [
            list_c,
            list_o,
            pooled,
            sorted_oth,
            counts[:, None],
            gain[None],
            doc_sums,
            adapter_up,
            up_states,
            labels[None],
        ]
        + states_b,
        vmem=16 if dp <= 4 else 48,
    )
    losses = losses[:, :per_shard]
    small = sum_over(small, "mp")
    alpha = inv_rms * inv_rms * inv_rms * small[rank, :token_count] / width
    up_states = small[:rank, :token_count]
    up_gained = small[:rank, token_count : token_count + docs]
    mid_grad = (
        inv_rms * dot_nn(up_gained, member_f, highest) - alpha * up_states
    ).astype(jnp.bfloat16)
    mid_t = lora_mid.astype(jnp.float32).T
    a_grad = dot_nn(mid_grad, own_cols)
    mid_alpha = (mid_t * alpha).astype(jnp.bfloat16)
    b_grad = dot_nn(dot_nt(mid_t * inv_rms, member_f, highest), gained, highest) - jnp.concatenate(
        [dot_nn(mid_alpha, x) for x in states_b], axis=1
    )

    grads = jnp.concatenate([a_grad, b_grad, gain_grad], axis=0)
    half = cols // 2
    kept = lax.dynamic_slice_in_dim(grads, side * half, half, 1)
    sent = lax.dynamic_slice_in_dim(grads, (1 - side) * half, half, 1)
    kept = kept + swap(sent, "pair")
    kept = kept.astype(jnp.bfloat16)
    level = [kept] + [partner(kept, "dp", j) for j in range(1, dp)]
    level = [x.astype(jnp.float32) for x in level]
    while len(level) > 1:
        level = [level[i] + level[i + 1] for i in range(0, len(level), 2)]
    total = level[0]
    received = swap(total, "pair")
    grads = jnp.concatenate(
        [jnp.where(side == 0, total, received), jnp.where(side == 0, received, total)], axis=1
    )
    return (
        losses,
        doc_grad[None, None],
        grads[:rank].T,
        grads[rank : 2 * rank],
        grads[2 * rank],
    )


def solution(mesh):
    in_specs = (
        P("pair", ("groups", "dp"), None),
        P("pair", ("groups", "dp"), None),
        P("dp", "mp"),
        P(),
        P(None, "mp"),
        P("mp"),
        P("pair", "groups", None),
        P("pair", "groups", None),
    )
    out_specs = (
        P("pair", ("groups", "dp")),
        P("pair", ("groups", "dp"), None, "mp"),
        P(("groups", "mp"), None),
        P("groups", "mp"),
        P(("groups", "mp")),
    )
    return jax.shard_map(body, mesh=mesh, in_specs=in_specs, out_specs=out_specs, check_vma=False)
```

```python
import functools

import jax
import jax.numpy as jnp
from jax import lax
from jax.experimental import pallas as pl
from jax.experimental.pallas import tpu as pltpu
from jax.sharding import PartitionSpec as P

inverse_temp = 50.0
highest = lax.Precision.HIGHEST
chunk_count = 2


def dot_nt(a, b, precision=None):
    return lax.dot_general(
        a, b, (((1,), (1,)), ((), ())), precision=precision, preferred_element_type=jnp.float32
    )


def dot_nn(a, b, precision=None):
    return jnp.dot(a, b, precision=precision, preferred_element_type=jnp.float32)


def swap(x, axis):
    return lax.ppermute(x, axis, [(0, 1), (1, 0)])


def partner(x, axis, flip):
    return lax.ppermute(x, axis, [(i, i ^ flip) for i in range(lax.axis_size(axis))])


def sum_over(x, axis):
    if lax.axis_size(axis) == 2:
        return x + swap(x, axis)
    return lax.psum(x, axis)


def widths(cols):
    tiles = cols // 128
    base, more = divmod(tiles, chunk_count)
    return [128 * (base + (i >= chunk_count - more)) for i in range(chunk_count)]


def spans(cols):
    out, at = [], 0
    for width in widths(cols):
        out.append((at, at + width))
        at += width
    return out


def after(x, *deps):
    return lax.optimization_barrier((x, *deps))[0]


def call(kernel, outs, args, scratch=(), flops=1 << 24, vmem=16):
    size = sum(a.size * a.dtype.itemsize for a in args)
    return pl.pallas_call(
        kernel,
        out_shape=outs,
        scratch_shapes=list(scratch),
        compiler_params=pltpu.CompilerParams(vmem_limit_bytes=vmem << 20),
        cost_estimate=pl.CostEstimate(flops=flops, bytes_accessed=size, transcendentals=0),
    )(*args)


def as_row(column):
    size = column.shape[0]
    eye = lax.broadcasted_iota(jnp.int32, (size, size), 0) == lax.broadcasted_iota(
        jnp.int32, (size, size), 1
    )
    return jnp.sum(jnp.where(eye, column, 0.0), axis=0, keepdims=True)


def as_column(row):
    size = row.shape[1]
    eye = lax.broadcasted_iota(jnp.int32, (size, size), 0) == lax.broadcasted_iota(
        jnp.int32, (size, size), 1
    )
    return jnp.sum(jnp.where(eye, row, 0.0), axis=1, keepdims=True)


def gram_kernel(blocks, *refs):
    own, oth = refs[:blocks], refs[blocks : 2 * blocks]
    out_ref, sorted_ref, own_ref = refs[2 * blocks :]
    docs = own[0].shape[0]
    half = docs // 2
    anchors = blocks * half
    for j in range(blocks):
        own_ref[j * docs : (j + 1) * docs] = own[j][...]
        sorted_ref[j * half : (j + 1) * half] = oth[j][:half]
        sorted_ref[anchors + j * half : anchors + (j + 1) * half] = oth[j][half:]
    rows = blocks * docs
    out_ref[:rows] = dot_nt(own_ref[...], sorted_ref[:anchors])
    out_ref[rows : rows + half] = dot_nt(own[0][:half], sorted_ref[anchors:])
    own_f = own_ref[...].astype(jnp.float32)
    oth_f = sorted_ref[...].astype(jnp.float32)
    own_sq = as_row(jnp.sum(own_f * own_f, axis=1, keepdims=True))
    oth_sq = as_row(jnp.sum(oth_f * oth_f, axis=1, keepdims=True))
    tail = jnp.concatenate(
        [
            own_sq[:, :anchors],
            own_sq[:, anchors:],
            oth_sq[:, :anchors],
            oth_sq[:, anchors:],
            jnp.zeros((4, anchors), jnp.float32),
        ],
        axis=0,
    )
    out_ref[rows + half :] = tail


def loss_kernel(blocks, sums_count, chunks, *refs):
    sums_refs = refs[:sums_count]
    list_c, list_o, pooled_ref, oth_ref, counts_ref, gain_ref, doc_sums_ref, up_ref = refs[
        sums_count : sums_count + 8
    ]
    up_states_ref, labels_ref = refs[sums_count + 8 : sums_count + 10]
    state_refs = refs[sums_count + 10 : sums_count + 10 + chunks]
    losses_ref, doc_grad_ref, small_ref, gained_ref, gain_grad_ref = refs[
        sums_count + 10 + chunks :
    ]
    docs = pooled_ref.shape[0]
    half = docs // 2
    anchors = blocks * half
    rows = blocks * docs
    fanout = list_o.shape[1]
    sums = sums_refs[0][...]
    if sums_count == 2:
        sums = sums + sums_refs[1][...]
    inner_c = sums[:rows]
    inner_o = sums[rows : rows + half]
    scales = lax.rsqrt(sums[rows + half :] + 1e-06)
    own_scale = as_column(jnp.concatenate([scales[0:1], scales[1:2]], axis=1))
    oth_scale = scales[2:3]
    pool_scale = scales[3:4]

    row_id = lax.broadcasted_iota(jnp.int32, (rows, anchors), 0)
    col_id = lax.broadcasted_iota(jnp.int32, (rows, anchors), 1)
    mask_c = (row_id % docs) < half
    for h in range(fanout):
        mask_c = mask_c | (row_id == list_c[h : h + 1, :])
    target_c = row_id == (col_id // half) * docs + col_id % half
    logits_c = inverse_temp * (inner_c * own_scale * oth_scale)
    exp_all = jnp.exp(logits_c)
    exp_c = jnp.where(mask_c, exp_all, 0.0)
    total_c = jnp.sum(exp_c, axis=0, keepdims=True)
    losses_ref[...] = jnp.log(total_c) - jnp.sum(
        jnp.where(target_c, logits_c, 0.0), axis=0, keepdims=True
    )
    target_own = target_c[:docs].astype(jnp.float32)
    grad_c = inverse_temp * (exp_c[:docs] / total_c - target_own)

    logits_o = inverse_temp * (inner_o * own_scale[:half] * pool_scale)
    pool_id = lax.broadcasted_iota(jnp.int32, (half, anchors), 1)
    mask_o = pool_id == list_o[:, 0:1]
    for h in range(1, fanout):
        mask_o = mask_o | (pool_id == list_o[:, h : h + 1])
    exp_o = jnp.where(mask_o, jnp.exp(logits_o), 0.0)
    exp_a = exp_all[:half]
    total_o = jnp.sum(exp_a, axis=1, keepdims=True) + jnp.sum(exp_o, axis=1, keepdims=True)
    grad_a = inverse_temp * (exp_a / total_o - target_own[:half])
    grad_o = inverse_temp * (exp_o / total_o)

    zeros = jnp.zeros((docs - half, anchors), jnp.float32)
    coef = jnp.concatenate(
        [
            (grad_c + jnp.concatenate([grad_a, zeros], axis=0)) * oth_scale,
            jnp.concatenate([grad_o * pool_scale, zeros], axis=0),
        ],
        axis=1,
    ).astype(jnp.bfloat16)
    inner = jnp.concatenate(
        [inner_c[:docs], jnp.concatenate([inner_o, zeros], axis=0)], axis=1
    )
    doc_grad = dot_nn(coef, oth_ref[...])
    doc_grad_ref[...] = doc_grad
    scale = own_scale[:docs]
    unit_dots = jnp.sum(coef.astype(jnp.float32) * inner, axis=1, keepdims=True) * scale
    pooled = pooled_ref[...].astype(jnp.float32)
    per_doc = (doc_grad - pooled * (scale * unit_dots)) * (scale / counts_ref[...])
    gain = gain_ref[...]
    gained = per_doc * gain
    gained_ref[...] = gained
    gain_grad_ref[...] = jnp.sum(per_doc * doc_sums_ref[...], axis=0, keepdims=True) / gain

    gained_b = gained.astype(jnp.bfloat16)
    tok_doc = 0.0
    for (low, high), state_ref in zip(spans(gained_b.shape[1]), state_refs):
        tok_doc = tok_doc + dot_nt(gained_b[:, low:high], state_ref[...])
    tokens = tok_doc.shape[1]
    rank = up_ref.shape[0]
    doc_id = lax.broadcasted_iota(jnp.int32, (docs, tokens), 0)
    tok_dots = jnp.sum(
        jnp.where(doc_id == labels_ref[...], tok_doc, 0.0), axis=0, keepdims=True
    )
    up_gained = dot_nt(up_ref[...].astype(jnp.float32), gained, highest)
    small_ref[...] = jnp.zeros_like(small_ref)
    small_ref[:rank, :tokens] = up_states_ref[...]
    small_ref[:rank, tokens : tokens + docs] = up_gained
    small_ref[rank : rank + 1, :tokens] = tok_dots


def body(
    hidden,
    document_labels,
    frozen_weight,
    adapter_down,
    adapter_up,
    norm_gain_vector,
    negative_owner,
    negative_pool_row,
):
    tokens = hidden[0]
    token_count, width = tokens.shape
    cols = adapter_up.shape[1]
    rank = adapter_up.shape[0]
    dp = lax.axis_size("dp")
    side = lax.axis_index("pair")
    shard = lax.axis_index("dp")
    anchors = negative_owner.shape[1]
    per_shard = anchors // dp
    docs = 2 * per_shard

    order = [0] + list(range(1, dp, 2)) + list(range(dp - 2 + dp % 2, 0, -2))
    hops = [(order[i], order[(i + 1) % dp]) for i in range(dp)]
    back_hops = [(b, a) for a, b in hops]

    def place_of(index):
        return jnp.where(index % 2 == 1, (index + 1) // 2, (dp - index // 2) % dp)

    def shard_at(position):
        return jnp.where(
            position == 0, 0, jnp.where(position <= dp // 2, 2 * position - 1, 2 * (dp - position))
        )

    place = place_of(shard)

    block_shard = shard_at((place - jnp.arange(dp, dtype=jnp.int32)) % dp)
    owner_block = (place - place_of(negative_owner[0])) % dp
    rel_list = (owner_block * docs + per_shard + negative_pool_row[0]).reshape(dp, per_shard, -1)
    list_c = rel_list[block_shard].reshape(anchors, -1).T
    pool_col = owner_block * per_shard + negative_pool_row[0]
    list_o = swap(
        lax.dynamic_slice_in_dim(pool_col, shard * per_shard, per_shard, 0), "pair"
    )

    group = lax.axis_index("groups")
    quarter = frozen_weight.shape[0] // 4
    shard_rows = frozen_weight.shape[0]
    parts = spans(cols)
    quarters = [
        (group * 2 + side),
        ((1 - group) * 2 + side),
        (group * 2 + 1 - side),
        ((1 - group) * 2 + 1 - side),
    ]
    moving = []
    for low, high in parts:
        corner = quarters[0] * quarter
        if moving:
            corner = after(corner, moving[0])
        moving.append(lax.dynamic_slice(frozen_weight, (corner, low), (quarter, high - low)))
    lora_mid = dot_nn(tokens, adapter_down).astype(jnp.bfloat16)
    own_cols = lax.dynamic_slice_in_dim(tokens, lax.axis_index("mp") * cols, cols, 1)
    own_tokens = lax.dynamic_slice_in_dim(tokens, shard * shard_rows, shard_rows, 1)
    states = [None] * chunk_count
    ringed = []
    for step in range(1, dp):
        for h in range(chunk_count):
            ringed.append(lax.ppermute(ringed[-chunk_count] if step > 1 else moving[h], "dp", hops))
    event = 0
    for step in range(1, dp):
        origin = shard_at((place - step) % dp)
        step_tokens = jnp.concatenate(
            [
                lax.dynamic_slice_in_dim(tokens, origin * shard_rows + q * quarter, quarter, 1)
                for q in quarters
            ],
            axis=1,
        )
        for h, (low, high) in enumerate(parts):
            moved = ringed[event]
            if step == 1:
                own_first, mid_first = own_tokens, lora_mid
                states[h] = (
                    own_cols[:, low:high].astype(jnp.float32)
                    + dot_nn(own_first, frozen_weight[:, low:high])
                    + dot_nn(mid_first, adapter_up[:, low:high])
                )
                states[h] = lax.optimization_barrier(states[h])
            across = swap(moved, "groups")
            lhs = step_tokens
            late = across
            if step == dp - 1 and h == chunk_count - 1:
                late = after(across, *states)
            rows = [moved, across, swap(moved, "pair"), swap(late, "pair")]
            states[h] = lax.optimization_barrier(
                states[h] + dot_nn(lhs, jnp.concatenate(rows, axis=0))
            )
            event += 1
    states_b = [x.astype(jnp.bfloat16) for x in states]
    squares = sum_over(sum(jnp.sum(x * x, axis=1) for x in states), "mp")
    inv_rms = lax.rsqrt(squares / width + 1e-05)

    gain = norm_gain_vector.astype(jnp.float32)
    labels = document_labels[0, 0]
    member = labels[None, :] == jnp.arange(docs, dtype=jnp.int32)[:, None]
    member_f = member.astype(jnp.float32)
    counts = jnp.sum(member_f, axis=1)
    member_b = member.astype(jnp.bfloat16)
    doc_sums = jnp.concatenate(
        [
            dot_nn(member_b, (x * inv_rms[:, None] * g[None, :]).astype(jnp.bfloat16))
            for x, g in zip(states, [gain[low:high] for low, high in parts])
        ],
        axis=1,
    )
    pooled = (doc_sums / counts[:, None]).astype(jnp.bfloat16)

    own_blocks = [pooled] * dp
    for j in range(1, dp):
        if j <= dp // 2:
            own_blocks[j] = lax.ppermute(own_blocks[j - 1], "dp", hops)
        else:
            own_blocks[dp + dp // 2 - j] = lax.ppermute(
                own_blocks[(dp + dp // 2 - j + 1) % dp], "dp", back_hops
            )
    other_blocks = [swap(block, "pair") for block in own_blocks]
    rows = dp * docs
    sums, sorted_oth = call(
        functools.partial(gram_kernel, dp),
        (
            jax.ShapeDtypeStruct((rows + per_shard + 8, anchors), jnp.float32),
            jax.ShapeDtypeStruct((rows, cols), jnp.bfloat16),
        ),
        own_blocks + other_blocks,
        [pltpu.VMEM((rows, cols), jnp.bfloat16)],
        vmem=16 if dp <= 4 else 48,
    )
    up_parts = [adapter_up[:, low:high] for low, high in parts]
    up_states = sum(dot_nt(u, x) for u, x in zip(up_parts, states_b))
    if lax.axis_size("mp") == 2:
        sums = [sums, swap(sums, "mp")]
    else:
        sums = [lax.psum(sums, "mp")]
    losses, doc_grad, small, gained, gain_grad = call(
        functools.partial(loss_kernel, dp, len(sums), chunk_count),
        (
            jax.ShapeDtypeStruct((1, anchors), jnp.float32),
            jax.ShapeDtypeStruct((docs, cols), jnp.float32),
            jax.ShapeDtypeStruct((rank + 8, token_count + 128), jnp.float32),
            jax.ShapeDtypeStruct((docs, cols), jnp.float32),
            jax.ShapeDtypeStruct((1, cols), jnp.float32),
        ),
        sums
        + [
            list_c,
            list_o,
            pooled,
            sorted_oth,
            counts[:, None],
            gain[None],
            doc_sums,
            adapter_up,
            up_states,
            labels[None],
        ]
        + states_b,
        vmem=16 if dp <= 4 else 48,
    )
    losses = losses[:, :per_shard]
    small = sum_over(small, "mp")
    alpha = inv_rms * inv_rms * inv_rms * small[rank, :token_count] / width
    up_states = small[:rank, :token_count]
    up_gained = small[:rank, token_count : token_count + docs]
    mid_grad = (
        inv_rms * dot_nn(up_gained, member_f, highest) - alpha * up_states
    ).astype(jnp.bfloat16)
    mid_t = lora_mid.astype(jnp.float32).T
    a_grad = dot_nn(mid_grad, own_cols)
    mid_alpha = (mid_t * alpha).astype(jnp.bfloat16)
    b_grad = dot_nn(dot_nt(mid_t * inv_rms, member_f, highest), gained, highest) - jnp.concatenate(
        [dot_nn(mid_alpha, x) for x in states_b], axis=1
    )

    grads = jnp.concatenate([a_grad, b_grad, gain_grad], axis=0)
    half = cols // 2
    kept = lax.dynamic_slice_in_dim(grads, side * half, half, 1)
    sent = lax.dynamic_slice_in_dim(grads, (1 - side) * half, half, 1)
    kept = kept + swap(sent, "pair")
    kept = kept.astype(jnp.bfloat16)
    level = [kept] + [partner(kept, "dp", j) for j in range(1, dp)]
    level = [x.astype(jnp.float32) for x in level]
    while len(level) > 1:
        level = [level[i] + level[i + 1] for i in range(0, len(level), 2)]
    total = level[0]
    received = swap(total, "pair")
    grads = jnp.concatenate(
        [jnp.where(side == 0, total, received), jnp.where(side == 0, received, total)], axis=1
    )
    return (
        losses,
        doc_grad[None, None],
        grads[:rank].T,
        grads[rank : 2 * rank],
        grads[2 * rank],
    )


def solution(mesh):
    in_specs = (
        P("pair", ("groups", "dp"), None),
        P("pair", ("groups", "dp"), None),
        P("dp", "mp"),
        P(),
        P(None, "mp"),
        P("mp"),
        P("pair", "groups", None),
        P("pair", "groups", None),
    )
    out_specs = (
        P("pair", ("groups", "dp")),
        P("pair", ("groups", "dp"), None, "mp"),
        P(("groups", "mp"), None),
        P("groups", "mp"),
        P(("groups", "mp")),
    )
    return jax.shard_map(body, mesh=mesh, in_specs=in_specs, out_specs=out_specs, check_vma=False)
```

```python
import functools

import jax
import jax.numpy as jnp
from jax import lax
from jax.experimental import pallas as pl
from jax.experimental.pallas import tpu as pltpu
from jax.sharding import PartitionSpec as P

inverse_temp = 50.0
highest = lax.Precision.HIGHEST
chunk_count = 2


def dot_nt(a, b, precision=None):
    return lax.dot_general(
        a, b, (((1,), (1,)), ((), ())), precision=precision, preferred_element_type=jnp.float32
    )


def dot_nn(a, b, precision=None):
    return jnp.dot(a, b, precision=precision, preferred_element_type=jnp.float32)


def swap(x, axis):
    return lax.ppermute(x, axis, [(0, 1), (1, 0)])


def partner(x, axis, flip):
    return lax.ppermute(x, axis, [(i, i ^ flip) for i in range(lax.axis_size(axis))])


def sum_over(x, axis):
    if lax.axis_size(axis) == 2:
        return x + swap(x, axis)
    return lax.psum(x, axis)


def widths(cols):
    tiles = cols // 128
    base, more = divmod(tiles, chunk_count)
    return [128 * (base + (i >= chunk_count - more)) for i in range(chunk_count)]


def spans(cols):
    out, at = [], 0
    for width in widths(cols):
        out.append((at, at + width))
        at += width
    return out


def after(x, *deps):
    return lax.optimization_barrier((x, *deps))[0]


def call(kernel, outs, args, scratch=(), flops=1 << 24, vmem=16):
    size = sum(a.size * a.dtype.itemsize for a in args)
    return pl.pallas_call(
        kernel,
        out_shape=outs,
        scratch_shapes=list(scratch),
        compiler_params=pltpu.CompilerParams(vmem_limit_bytes=vmem << 20),
        cost_estimate=pl.CostEstimate(flops=flops, bytes_accessed=size, transcendentals=0),
    )(*args)


def as_row(column):
    size = column.shape[0]
    eye = lax.broadcasted_iota(jnp.int32, (size, size), 0) == lax.broadcasted_iota(
        jnp.int32, (size, size), 1
    )
    return jnp.sum(jnp.where(eye, column, 0.0), axis=0, keepdims=True)


def as_column(row):
    size = row.shape[1]
    eye = lax.broadcasted_iota(jnp.int32, (size, size), 0) == lax.broadcasted_iota(
        jnp.int32, (size, size), 1
    )
    return jnp.sum(jnp.where(eye, row, 0.0), axis=1, keepdims=True)


def gram_kernel(blocks, *refs):
    own, oth = refs[:blocks], refs[blocks : 2 * blocks]
    out_ref, sorted_ref, own_ref = refs[2 * blocks :]
    docs = own[0].shape[0]
    half = docs // 2
    anchors = blocks * half
    for j in range(blocks):
        own_ref[j * docs : (j + 1) * docs] = own[j][...]
        sorted_ref[j * half : (j + 1) * half] = oth[j][:half]
        sorted_ref[anchors + j * half : anchors + (j + 1) * half] = oth[j][half:]
    rows = blocks * docs
    out_ref[:rows] = dot_nt(own_ref[...], sorted_ref[:anchors])
    out_ref[rows : rows + half] = dot_nt(own[0][:half], sorted_ref[anchors:])
    own_f = own_ref[...].astype(jnp.float32)
    oth_f = sorted_ref[...].astype(jnp.float32)
    own_sq = as_row(jnp.sum(own_f * own_f, axis=1, keepdims=True))
    oth_sq = as_row(jnp.sum(oth_f * oth_f, axis=1, keepdims=True))
    tail = jnp.concatenate(
        [
            own_sq[:, :anchors],
            own_sq[:, anchors:],
            oth_sq[:, :anchors],
            oth_sq[:, anchors:],
            jnp.zeros((4, anchors), jnp.float32),
        ],
        axis=0,
    )
    out_ref[rows + half :] = tail


def pool_kernel(squares_count, chunks, width, *refs):
    squares = refs[0][...]
    for ref in refs[1:squares_count]:
        squares = squares + ref[...]
    state_refs = refs[squares_count : squares_count + chunks]
    labels_ref, gain_ref, counts_ref, sums_ref, pooled_ref, inv_rms_ref = refs[
        squares_count + chunks :
    ]
    inv_rms = lax.rsqrt(squares / width + 1e-05)
    inv_rms_ref[...] = inv_rms
    scale = as_column(inv_rms)
    docs, tokens = counts_ref.shape[0], squares.shape[1]
    doc_id = lax.broadcasted_iota(jnp.int32, (docs, tokens), 0)
    member = jnp.where(doc_id == labels_ref[...], 1.0, 0.0).astype(jnp.bfloat16)
    counts = counts_ref[...]
    for (low, high), state_ref in zip(spans(gain_ref.shape[1]), state_refs):
        tile = 256 if (high - low) % 256 == 0 else 128
        for at in range(0, high - low, tile):
            part = slice(low + at, low + at + tile)
            normed = (state_ref[:, at : at + tile] * scale * gain_ref[:, part]).astype(jnp.bfloat16)
            sums = dot_nn(member, normed)
            sums_ref[:, part] = sums
            pooled_ref[:, part] = (sums / counts).astype(jnp.bfloat16)


def loss_kernel(blocks, sums_count, chunks, *refs):
    sums_refs = refs[:sums_count]
    list_c, list_o, pooled_ref, oth_ref, counts_ref, gain_ref, doc_sums_ref, up_ref = refs[
        sums_count : sums_count + 8
    ]
    up_states_ref, labels_ref = refs[sums_count + 8 : sums_count + 10]
    state_refs = refs[sums_count + 10 : sums_count + 10 + chunks]
    losses_ref, doc_grad_ref, small_ref, gained_ref, gain_grad_ref = refs[
        sums_count + 10 + chunks :
    ]
    docs = pooled_ref.shape[0]
    half = docs // 2
    anchors = blocks * half
    rows = blocks * docs
    fanout = list_o.shape[1]
    sums = sums_refs[0][...]
    if sums_count == 2:
        sums = sums + sums_refs[1][...]
    inner_c = sums[:rows]
    inner_o = sums[rows : rows + half]
    scales = lax.rsqrt(sums[rows + half :] + 1e-06)
    own_scale = as_column(jnp.concatenate([scales[0:1], scales[1:2]], axis=1))
    oth_scale = scales[2:3]
    pool_scale = scales[3:4]

    row_id = lax.broadcasted_iota(jnp.int32, (rows, anchors), 0)
    col_id = lax.broadcasted_iota(jnp.int32, (rows, anchors), 1)
    mask_c = (row_id % docs) < half
    for h in range(fanout):
        mask_c = mask_c | (row_id == list_c[h : h + 1, :])
    target_c = row_id == (col_id // half) * docs + col_id % half
    logits_c = inverse_temp * (inner_c * own_scale * oth_scale)
    exp_all = jnp.exp(logits_c)
    exp_c = jnp.where(mask_c, exp_all, 0.0)
    total_c = jnp.sum(exp_c, axis=0, keepdims=True)
    losses_ref[...] = jnp.log(total_c) - jnp.sum(
        jnp.where(target_c, logits_c, 0.0), axis=0, keepdims=True
    )
    target_own = target_c[:docs].astype(jnp.float32)
    grad_c = inverse_temp * (exp_c[:docs] / total_c - target_own)

    logits_o = inverse_temp * (inner_o * own_scale[:half] * pool_scale)
    pool_id = lax.broadcasted_iota(jnp.int32, (half, anchors), 1)
    mask_o = pool_id == list_o[:, 0:1]
    for h in range(1, fanout):
        mask_o = mask_o | (pool_id == list_o[:, h : h + 1])
    exp_o = jnp.where(mask_o, jnp.exp(logits_o), 0.0)
    exp_a = exp_all[:half]
    total_o = jnp.sum(exp_a, axis=1, keepdims=True) + jnp.sum(exp_o, axis=1, keepdims=True)
    grad_a = inverse_temp * (exp_a / total_o - target_own[:half])
    grad_o = inverse_temp * (exp_o / total_o)

    zeros = jnp.zeros((docs - half, anchors), jnp.float32)
    coef = jnp.concatenate(
        [
            (grad_c + jnp.concatenate([grad_a, zeros], axis=0)) * oth_scale,
            jnp.concatenate([grad_o * pool_scale, zeros], axis=0),
        ],
        axis=1,
    ).astype(jnp.bfloat16)
    inner = jnp.concatenate(
        [inner_c[:docs], jnp.concatenate([inner_o, zeros], axis=0)], axis=1
    )
    doc_grad = dot_nn(coef, oth_ref[...])
    doc_grad_ref[...] = doc_grad
    scale = own_scale[:docs]
    unit_dots = jnp.sum(coef.astype(jnp.float32) * inner, axis=1, keepdims=True) * scale
    pooled = pooled_ref[...].astype(jnp.float32)
    per_doc = (doc_grad - pooled * (scale * unit_dots)) * (scale / counts_ref[...])
    gain = gain_ref[...]
    gained = per_doc * gain
    gained_ref[...] = gained
    gain_grad_ref[...] = jnp.sum(per_doc * doc_sums_ref[...], axis=0, keepdims=True) / gain

    gained_b = gained.astype(jnp.bfloat16)
    tok_doc = 0.0
    for (low, high), state_ref in zip(spans(gained_b.shape[1]), state_refs):
        tok_doc = tok_doc + dot_nt(gained_b[:, low:high], state_ref[...])
    tokens = tok_doc.shape[1]
    rank = up_ref.shape[0]
    doc_id = lax.broadcasted_iota(jnp.int32, (docs, tokens), 0)
    tok_dots = jnp.sum(
        jnp.where(doc_id == labels_ref[...], tok_doc, 0.0), axis=0, keepdims=True
    )
    up_gained = dot_nt(up_ref[...].astype(jnp.float32), gained, highest)
    small_ref[...] = jnp.zeros_like(small_ref)
    small_ref[:rank, :tokens] = up_states_ref[...]
    small_ref[:rank, tokens : tokens + docs] = up_gained
    small_ref[rank : rank + 1, :tokens] = tok_dots


def body(
    hidden,
    document_labels,
    frozen_weight,
    adapter_down,
    adapter_up,
    norm_gain_vector,
    negative_owner,
    negative_pool_row,
):
    tokens = hidden[0]
    token_count, width = tokens.shape
    cols = adapter_up.shape[1]
    rank = adapter_up.shape[0]
    dp = lax.axis_size("dp")
    side = lax.axis_index("pair")
    shard = lax.axis_index("dp")
    anchors = negative_owner.shape[1]
    per_shard = anchors // dp
    docs = 2 * per_shard

    order = [0] + list(range(1, dp, 2)) + list(range(dp - 2 + dp % 2, 0, -2))
    hops = [(order[i], order[(i + 1) % dp]) for i in range(dp)]
    back_hops = [(b, a) for a, b in hops]

    def place_of(index):
        return jnp.where(index % 2 == 1, (index + 1) // 2, (dp - index // 2) % dp)

    def shard_at(position):
        return jnp.where(
            position == 0, 0, jnp.where(position <= dp // 2, 2 * position - 1, 2 * (dp - position))
        )

    place = place_of(shard)

    block_shard = shard_at((place - jnp.arange(dp, dtype=jnp.int32)) % dp)
    owner_block = (place - place_of(negative_owner[0])) % dp
    rel_list = (owner_block * docs + per_shard + negative_pool_row[0]).reshape(dp, per_shard, -1)
    list_c = rel_list[block_shard].reshape(anchors, -1).T
    pool_col = owner_block * per_shard + negative_pool_row[0]
    list_o = swap(
        lax.dynamic_slice_in_dim(pool_col, shard * per_shard, per_shard, 0), "pair"
    )

    group = lax.axis_index("groups")
    quarter = frozen_weight.shape[0] // 4
    shard_rows = frozen_weight.shape[0]
    parts = spans(cols)
    quarters = [
        (group * 2 + side),
        ((1 - group) * 2 + side),
        (group * 2 + 1 - side),
        ((1 - group) * 2 + 1 - side),
    ]
    moving = []
    for low, high in parts:
        corner = quarters[0] * quarter
        if moving:
            corner = after(corner, moving[0])
        moving.append(lax.dynamic_slice(frozen_weight, (corner, low), (quarter, high - low)))
    lora_mid = dot_nn(tokens, adapter_down).astype(jnp.bfloat16)
    own_cols = lax.dynamic_slice_in_dim(tokens, lax.axis_index("mp") * cols, cols, 1)
    own_tokens = lax.dynamic_slice_in_dim(tokens, shard * shard_rows, shard_rows, 1)
    states = [None] * chunk_count
    ringed = []
    for step in range(1, dp):
        for h in range(chunk_count):
            ringed.append(lax.ppermute(ringed[-chunk_count] if step > 1 else moving[h], "dp", hops))
    event = 0
    for step in range(1, dp):
        origin = shard_at((place - step) % dp)
        step_tokens = jnp.concatenate(
            [
                lax.dynamic_slice_in_dim(tokens, origin * shard_rows + q * quarter, quarter, 1)
                for q in quarters
            ],
            axis=1,
        )
        for h, (low, high) in enumerate(parts):
            moved = ringed[event]
            if step == 1:
                own_first, mid_first = own_tokens, lora_mid
                states[h] = (
                    own_cols[:, low:high].astype(jnp.float32)
                    + dot_nn(own_first, frozen_weight[:, low:high])
                    + dot_nn(mid_first, adapter_up[:, low:high])
                )
                states[h] = lax.optimization_barrier(states[h])
            across = swap(moved, "groups")
            lhs = step_tokens
            late = across
            if step == dp - 1 and h == chunk_count - 1:
                late = after(across, *states)
            rows = [moved, across, swap(moved, "pair"), swap(late, "pair")]
            states[h] = lax.optimization_barrier(
                states[h] + dot_nn(lhs, jnp.concatenate(rows, axis=0))
            )
            event += 1
    states_b = [x.astype(jnp.bfloat16) for x in states]
    squares = sum(jnp.sum(x * x, axis=1) for x in states)

    gain = norm_gain_vector.astype(jnp.float32)
    labels = document_labels[0, 0]
    member = labels[None, :] == jnp.arange(docs, dtype=jnp.int32)[:, None]
    member_f = member.astype(jnp.float32)
    counts = jnp.sum(member_f, axis=1)
    if lax.axis_size("mp") == 2:
        squares = [squares, swap(squares, "mp")]
    else:
        squares = [lax.psum(squares, "mp")]
    doc_sums, pooled, inv_rms = call(
        functools.partial(pool_kernel, len(squares), chunk_count, width),
        (
            jax.ShapeDtypeStruct((docs, cols), jnp.float32),
            jax.ShapeDtypeStruct((docs, cols), jnp.bfloat16),
            jax.ShapeDtypeStruct((1, token_count), jnp.float32),
        ),
        [x[None] for x in squares] + states + [labels[None], gain[None], counts[:, None]],
    )
    inv_rms = inv_rms[0]

    own_blocks = [pooled] * dp
    for j in range(1, dp):
        if j <= dp // 2:
            own_blocks[j] = lax.ppermute(own_blocks[j - 1], "dp", hops)
        else:
            own_blocks[dp + dp // 2 - j] = lax.ppermute(
                own_blocks[(dp + dp // 2 - j + 1) % dp], "dp", back_hops
            )
    other_blocks = [swap(block, "pair") for block in own_blocks]
    rows = dp * docs
    sums, sorted_oth = call(
        functools.partial(gram_kernel, dp),
        (
            jax.ShapeDtypeStruct((rows + per_shard + 8, anchors), jnp.float32),
            jax.ShapeDtypeStruct((rows, cols), jnp.bfloat16),
        ),
        own_blocks + other_blocks,
        [pltpu.VMEM((rows, cols), jnp.bfloat16)],
        vmem=16 if dp <= 4 else 48,
    )
    up_parts = [adapter_up[:, low:high] for low, high in parts]
    up_states = sum(dot_nt(u, x) for u, x in zip(up_parts, states_b))
    if lax.axis_size("mp") == 2:
        sums = [sums, swap(sums, "mp")]
    else:
        sums = [lax.psum(sums, "mp")]
    losses, doc_grad, small, gained, gain_grad = call(
        functools.partial(loss_kernel, dp, len(sums), chunk_count),
        (
            jax.ShapeDtypeStruct((1, anchors), jnp.float32),
            jax.ShapeDtypeStruct((docs, cols), jnp.float32),
            jax.ShapeDtypeStruct((rank + 8, token_count + 128), jnp.float32),
            jax.ShapeDtypeStruct((docs, cols), jnp.float32),
            jax.ShapeDtypeStruct((1, cols), jnp.float32),
        ),
        sums
        + [
            list_c,
            list_o,
            pooled,
            sorted_oth,
            counts[:, None],
            gain[None],
            doc_sums,
            adapter_up,
            up_states,
            labels[None],
        ]
        + states_b,
        vmem=16 if dp <= 4 else 48,
    )
    losses = losses[:, :per_shard]
    small = sum_over(small, "mp")
    alpha = inv_rms * inv_rms * inv_rms * small[rank, :token_count] / width
    up_states = small[:rank, :token_count]
    up_gained = small[:rank, token_count : token_count + docs]
    mid_grad = (
        inv_rms * dot_nn(up_gained, member_f, highest) - alpha * up_states
    ).astype(jnp.bfloat16)
    mid_t = lora_mid.astype(jnp.float32).T
    a_grad = dot_nn(mid_grad, own_cols)
    mid_alpha = (mid_t * alpha).astype(jnp.bfloat16)
    b_grad = dot_nn(dot_nt(mid_t * inv_rms, member_f, highest), gained, highest) - jnp.concatenate(
        [dot_nn(mid_alpha, x) for x in states_b], axis=1
    )

    grads = jnp.concatenate([a_grad, b_grad, gain_grad], axis=0)
    half = cols // 2
    kept = lax.dynamic_slice_in_dim(grads, side * half, half, 1)
    sent = lax.dynamic_slice_in_dim(grads, (1 - side) * half, half, 1)
    kept = kept + swap(sent, "pair")
    kept = kept.astype(jnp.bfloat16)
    level = [kept] + [partner(kept, "dp", j) for j in range(1, dp)]
    level = [x.astype(jnp.float32) for x in level]
    while len(level) > 1:
        level = [level[i] + level[i + 1] for i in range(0, len(level), 2)]
    total = level[0]
    received = swap(total, "pair")
    grads = jnp.concatenate(
        [jnp.where(side == 0, total, received), jnp.where(side == 0, received, total)], axis=1
    )
    return (
        losses,
        doc_grad[None, None],
        grads[:rank].T,
        grads[rank : 2 * rank],
        grads[2 * rank],
    )


def solution(mesh):
    in_specs = (
        P("pair", ("groups", "dp"), None),
        P("pair", ("groups", "dp"), None),
        P("dp", "mp"),
        P(),
        P(None, "mp"),
        P("mp"),
        P("pair", "groups", None),
        P("pair", "groups", None),
    )
    out_specs = (
        P("pair", ("groups", "dp")),
        P("pair", ("groups", "dp"), None, "mp"),
        P(("groups", "mp"), None),
        P("groups", "mp"),
        P(("groups", "mp")),
    )
    return jax.shard_map(body, mesh=mesh, in_specs=in_specs, out_specs=out_specs, check_vma=False)
```

```python
import functools

import jax
import jax.numpy as jnp
from jax import lax
from jax.experimental import pallas as pl
from jax.experimental.pallas import tpu as pltpu
from jax.sharding import PartitionSpec as P

inverse_temp = 50.0
highest = lax.Precision.HIGHEST
chunk_count = 2


def dot_nt(a, b, precision=None):
    return lax.dot_general(
        a, b, (((1,), (1,)), ((), ())), precision=precision, preferred_element_type=jnp.float32
    )


def dot_nn(a, b, precision=None):
    return jnp.dot(a, b, precision=precision, preferred_element_type=jnp.float32)


def swap(x, axis):
    return lax.ppermute(x, axis, [(0, 1), (1, 0)])


def partner(x, axis, flip):
    return lax.ppermute(x, axis, [(i, i ^ flip) for i in range(lax.axis_size(axis))])


def sum_over(x, axis):
    if lax.axis_size(axis) == 2:
        return x + swap(x, axis)
    return lax.psum(x, axis)


def widths(cols):
    tiles = cols // 128
    base, more = divmod(tiles, chunk_count)
    return [128 * (base + (i >= chunk_count - more)) for i in range(chunk_count)]


def spans(cols):
    out, at = [], 0
    for width in widths(cols):
        out.append((at, at + width))
        at += width
    return out


def after(x, *deps):
    return lax.optimization_barrier((x, *deps))[0]


def call(kernel, outs, args, scratch=(), flops=1 << 24, vmem=16):
    size = sum(a.size * a.dtype.itemsize for a in args)
    return pl.pallas_call(
        kernel,
        out_shape=outs,
        scratch_shapes=list(scratch),
        compiler_params=pltpu.CompilerParams(vmem_limit_bytes=vmem << 20),
        cost_estimate=pl.CostEstimate(flops=flops, bytes_accessed=size, transcendentals=0),
    )(*args)


def as_row(column):
    size = column.shape[0]
    eye = lax.broadcasted_iota(jnp.int32, (size, size), 0) == lax.broadcasted_iota(
        jnp.int32, (size, size), 1
    )
    return jnp.sum(jnp.where(eye, column, 0.0), axis=0, keepdims=True)


def as_column(row):
    size = row.shape[1]
    eye = lax.broadcasted_iota(jnp.int32, (size, size), 0) == lax.broadcasted_iota(
        jnp.int32, (size, size), 1
    )
    return jnp.sum(jnp.where(eye, row, 0.0), axis=1, keepdims=True)


def gram_kernel(blocks, *refs):
    own, oth = refs[:blocks], refs[blocks : 2 * blocks]
    out_ref, sorted_ref, own_ref = refs[2 * blocks :]
    docs = own[0].shape[0]
    half = docs // 2
    anchors = blocks * half
    for j in range(blocks):
        own_ref[j * docs : (j + 1) * docs] = own[j][...]
        sorted_ref[j * half : (j + 1) * half] = oth[j][:half]
        sorted_ref[anchors + j * half : anchors + (j + 1) * half] = oth[j][half:]
    rows = blocks * docs
    out_ref[:rows] = dot_nt(own_ref[...], sorted_ref[:anchors])
    out_ref[rows : rows + half] = dot_nt(own[0][:half], sorted_ref[anchors:])
    own_f = own_ref[...].astype(jnp.float32)
    oth_f = sorted_ref[...].astype(jnp.float32)
    own_sq = as_row(jnp.sum(own_f * own_f, axis=1, keepdims=True))
    oth_sq = as_row(jnp.sum(oth_f * oth_f, axis=1, keepdims=True))
    tail = jnp.concatenate(
        [
            own_sq[:, :anchors],
            own_sq[:, anchors:],
            oth_sq[:, :anchors],
            oth_sq[:, anchors:],
            jnp.zeros((4, anchors), jnp.float32),
        ],
        axis=0,
    )
    out_ref[rows + half :] = tail


def pool_kernel(squares_count, chunks, width, *refs):
    squares = refs[0][...]
    for ref in refs[1:squares_count]:
        squares = squares + ref[...]
    state_refs = refs[squares_count : squares_count + chunks]
    labels_ref, gain_ref, counts_ref, sums_ref, pooled_ref, inv_rms_ref = refs[
        squares_count + chunks :
    ]
    inv_rms = lax.rsqrt(squares / width + 1e-05)
    inv_rms_ref[...] = inv_rms
    scale = as_column(inv_rms)
    docs, tokens = counts_ref.shape[0], squares.shape[1]
    doc_id = lax.broadcasted_iota(jnp.int32, (docs, tokens), 0)
    member = jnp.where(doc_id == labels_ref[...], 1.0, 0.0).astype(jnp.bfloat16)
    counts = counts_ref[...]
    for (low, high), state_ref in zip(spans(gain_ref.shape[1]), state_refs):
        tile = 256 if (high - low) % 256 == 0 else 128
        for at in range(0, high - low, tile):
            part = slice(low + at, low + at + tile)
            states = state_ref[:, at : at + tile].astype(jnp.float32)
            normed = (states * scale * gain_ref[:, part]).astype(jnp.bfloat16)
            sums = dot_nn(member, normed)
            sums_ref[:, part] = sums
            pooled_ref[:, part] = (sums / counts).astype(jnp.bfloat16)


def loss_kernel(blocks, sums_count, chunks, *refs):
    sums_refs = refs[:sums_count]
    list_c, list_o, pooled_ref, oth_ref, counts_ref, gain_ref, doc_sums_ref, up_ref = refs[
        sums_count : sums_count + 8
    ]
    up_states_ref, labels_ref = refs[sums_count + 8 : sums_count + 10]
    state_refs = refs[sums_count + 10 : sums_count + 10 + chunks]
    losses_ref, doc_grad_ref, small_ref, gained_ref, gain_grad_ref = refs[
        sums_count + 10 + chunks :
    ]
    docs = pooled_ref.shape[0]
    half = docs // 2
    anchors = blocks * half
    rows = blocks * docs
    fanout = list_o.shape[1]
    sums = sums_refs[0][...]
    if sums_count == 2:
        sums = sums + sums_refs[1][...]
    inner_c = sums[:rows]
    inner_o = sums[rows : rows + half]
    scales = lax.rsqrt(sums[rows + half :] + 1e-06)
    own_scale = as_column(jnp.concatenate([scales[0:1], scales[1:2]], axis=1))
    oth_scale = scales[2:3]
    pool_scale = scales[3:4]

    row_id = lax.broadcasted_iota(jnp.int32, (rows, anchors), 0)
    col_id = lax.broadcasted_iota(jnp.int32, (rows, anchors), 1)
    mask_c = (row_id % docs) < half
    for h in range(fanout):
        mask_c = mask_c | (row_id == list_c[h : h + 1, :])
    target_c = row_id == (col_id // half) * docs + col_id % half
    logits_c = inverse_temp * (inner_c * own_scale * oth_scale)
    exp_all = jnp.exp(logits_c)
    exp_c = jnp.where(mask_c, exp_all, 0.0)
    total_c = jnp.sum(exp_c, axis=0, keepdims=True)
    losses_ref[...] = jnp.log(total_c) - jnp.sum(
        jnp.where(target_c, logits_c, 0.0), axis=0, keepdims=True
    )
    target_own = target_c[:docs].astype(jnp.float32)
    grad_c = inverse_temp * (exp_c[:docs] / total_c - target_own)

    logits_o = inverse_temp * (inner_o * own_scale[:half] * pool_scale)
    pool_id = lax.broadcasted_iota(jnp.int32, (half, anchors), 1)
    mask_o = pool_id == list_o[:, 0:1]
    for h in range(1, fanout):
        mask_o = mask_o | (pool_id == list_o[:, h : h + 1])
    exp_o = jnp.where(mask_o, jnp.exp(logits_o), 0.0)
    exp_a = exp_all[:half]
    total_o = jnp.sum(exp_a, axis=1, keepdims=True) + jnp.sum(exp_o, axis=1, keepdims=True)
    grad_a = inverse_temp * (exp_a / total_o - target_own[:half])
    grad_o = inverse_temp * (exp_o / total_o)

    zeros = jnp.zeros((docs - half, anchors), jnp.float32)
    coef = jnp.concatenate(
        [
            (grad_c + jnp.concatenate([grad_a, zeros], axis=0)) * oth_scale,
            jnp.concatenate([grad_o * pool_scale, zeros], axis=0),
        ],
        axis=1,
    ).astype(jnp.bfloat16)
    inner = jnp.concatenate(
        [inner_c[:docs], jnp.concatenate([inner_o, zeros], axis=0)], axis=1
    )
    doc_grad = dot_nn(coef, oth_ref[...])
    doc_grad_ref[...] = doc_grad
    scale = own_scale[:docs]
    unit_dots = jnp.sum(coef.astype(jnp.float32) * inner, axis=1, keepdims=True) * scale
    pooled = pooled_ref[...].astype(jnp.float32)
    per_doc = (doc_grad - pooled * (scale * unit_dots)) * (scale / counts_ref[...])
    gain = gain_ref[...]
    gained = per_doc * gain
    gained_ref[...] = gained
    gain_grad_ref[...] = jnp.sum(per_doc * doc_sums_ref[...], axis=0, keepdims=True) / gain

    gained_b = gained.astype(jnp.bfloat16)
    tok_doc = 0.0
    for (low, high), state_ref in zip(spans(gained_b.shape[1]), state_refs):
        tok_doc = tok_doc + dot_nt(gained_b[:, low:high], state_ref[...])
    tokens = tok_doc.shape[1]
    rank = up_ref.shape[0]
    doc_id = lax.broadcasted_iota(jnp.int32, (docs, tokens), 0)
    tok_dots = jnp.sum(
        jnp.where(doc_id == labels_ref[...], tok_doc, 0.0), axis=0, keepdims=True
    )
    up_gained = dot_nt(up_ref[...].astype(jnp.float32), gained, highest)
    small_ref[...] = jnp.zeros_like(small_ref)
    small_ref[:rank, :tokens] = up_states_ref[...]
    small_ref[:rank, tokens : tokens + docs] = up_gained
    small_ref[rank : rank + 1, :tokens] = tok_dots


def body(
    hidden,
    document_labels,
    frozen_weight,
    adapter_down,
    adapter_up,
    norm_gain_vector,
    negative_owner,
    negative_pool_row,
):
    tokens = hidden[0]
    token_count, width = tokens.shape
    cols = adapter_up.shape[1]
    rank = adapter_up.shape[0]
    dp = lax.axis_size("dp")
    side = lax.axis_index("pair")
    shard = lax.axis_index("dp")
    anchors = negative_owner.shape[1]
    per_shard = anchors // dp
    docs = 2 * per_shard

    order = [0] + list(range(1, dp, 2)) + list(range(dp - 2 + dp % 2, 0, -2))
    hops = [(order[i], order[(i + 1) % dp]) for i in range(dp)]
    back_hops = [(b, a) for a, b in hops]

    def place_of(index):
        return jnp.where(index % 2 == 1, (index + 1) // 2, (dp - index // 2) % dp)

    def shard_at(position):
        return jnp.where(
            position == 0, 0, jnp.where(position <= dp // 2, 2 * position - 1, 2 * (dp - position))
        )

    place = place_of(shard)

    block_shard = shard_at((place - jnp.arange(dp, dtype=jnp.int32)) % dp)
    owner_block = (place - place_of(negative_owner[0])) % dp
    rel_list = (owner_block * docs + per_shard + negative_pool_row[0]).reshape(dp, per_shard, -1)
    list_c = rel_list[block_shard].reshape(anchors, -1).T
    pool_col = owner_block * per_shard + negative_pool_row[0]
    list_o = swap(
        lax.dynamic_slice_in_dim(pool_col, shard * per_shard, per_shard, 0), "pair"
    )

    group = lax.axis_index("groups")
    quarter = frozen_weight.shape[0] // 4
    shard_rows = frozen_weight.shape[0]
    parts = spans(cols)
    quarters = [
        (group * 2 + side),
        ((1 - group) * 2 + side),
        (group * 2 + 1 - side),
        ((1 - group) * 2 + 1 - side),
    ]
    moving = []
    for low, high in parts:
        corner = quarters[0] * quarter
        if moving:
            corner = after(corner, moving[0])
        moving.append(lax.dynamic_slice(frozen_weight, (corner, low), (quarter, high - low)))
    lora_mid = dot_nn(tokens, adapter_down).astype(jnp.bfloat16)
    own_cols = lax.dynamic_slice_in_dim(tokens, lax.axis_index("mp") * cols, cols, 1)
    own_tokens = lax.dynamic_slice_in_dim(tokens, shard * shard_rows, shard_rows, 1)
    states = [None] * chunk_count
    ringed = []
    for step in range(1, dp):
        for h in range(chunk_count):
            ringed.append(lax.ppermute(ringed[-chunk_count] if step > 1 else moving[h], "dp", hops))
    event = 0
    for step in range(1, dp):
        origin = shard_at((place - step) % dp)
        step_tokens = jnp.concatenate(
            [
                lax.dynamic_slice_in_dim(tokens, origin * shard_rows + q * quarter, quarter, 1)
                for q in quarters
            ],
            axis=1,
        )
        for h, (low, high) in enumerate(parts):
            moved = ringed[event]
            if step == 1:
                own_first, mid_first = own_tokens, lora_mid
                states[h] = (
                    own_cols[:, low:high].astype(jnp.float32)
                    + dot_nn(own_first, frozen_weight[:, low:high])
                    + dot_nn(mid_first, adapter_up[:, low:high])
                )
                states[h] = lax.optimization_barrier(states[h])
            across = swap(moved, "groups")
            lhs = step_tokens
            late = across
            if step == dp - 1 and h == chunk_count - 1:
                late = after(across, *states)
            rows = [moved, across, swap(moved, "pair"), swap(late, "pair")]
            states[h] = lax.optimization_barrier(
                states[h] + dot_nn(lhs, jnp.concatenate(rows, axis=0))
            )
            event += 1
    states_b = [x.astype(jnp.bfloat16) for x in states]
    squares = sum(jnp.sum(x * x, axis=1) for x in states)

    gain = norm_gain_vector.astype(jnp.float32)
    labels = document_labels[0, 0]
    member = labels[None, :] == jnp.arange(docs, dtype=jnp.int32)[:, None]
    member_f = member.astype(jnp.float32)
    counts = jnp.sum(member_f, axis=1)
    if lax.axis_size("mp") == 2:
        squares = [squares, swap(squares, "mp")]
    else:
        squares = [lax.psum(squares, "mp")]
    doc_sums, pooled, inv_rms = call(
        functools.partial(pool_kernel, len(squares), chunk_count, width),
        (
            jax.ShapeDtypeStruct((docs, cols), jnp.float32),
            jax.ShapeDtypeStruct((docs, cols), jnp.bfloat16),
            jax.ShapeDtypeStruct((1, token_count), jnp.float32),
        ),
        [x[None] for x in squares] + states_b + [labels[None], gain[None], counts[:, None]],
    )
    inv_rms = inv_rms[0]

    own_blocks = [pooled] * dp
    for j in range(1, dp):
        if j <= dp // 2:
            own_blocks[j] = lax.ppermute(own_blocks[j - 1], "dp", hops)
        else:
            own_blocks[dp + dp // 2 - j] = lax.ppermute(
                own_blocks[(dp + dp // 2 - j + 1) % dp], "dp", back_hops
            )
    other_blocks = [swap(block, "pair") for block in own_blocks]
    rows = dp * docs
    sums, sorted_oth = call(
        functools.partial(gram_kernel, dp),
        (
            jax.ShapeDtypeStruct((rows + per_shard + 8, anchors), jnp.float32),
            jax.ShapeDtypeStruct((rows, cols), jnp.bfloat16),
        ),
        own_blocks + other_blocks,
        [pltpu.VMEM((rows, cols), jnp.bfloat16)],
        vmem=16 if dp <= 4 else 48,
    )
    up_parts = [adapter_up[:, low:high] for low, high in parts]
    up_states = sum(dot_nt(u, x) for u, x in zip(up_parts, states_b))
    if lax.axis_size("mp") == 2:
        sums = [sums, swap(sums, "mp")]
    else:
        sums = [lax.psum(sums, "mp")]
    losses, doc_grad, small, gained, gain_grad = call(
        functools.partial(loss_kernel, dp, len(sums), chunk_count),
        (
            jax.ShapeDtypeStruct((1, anchors), jnp.float32),
            jax.ShapeDtypeStruct((docs, cols), jnp.float32),
            jax.ShapeDtypeStruct((rank + 8, token_count + 128), jnp.float32),
            jax.ShapeDtypeStruct((docs, cols), jnp.float32),
            jax.ShapeDtypeStruct((1, cols), jnp.float32),
        ),
        sums
        + [
            list_c,
            list_o,
            pooled,
            sorted_oth,
            counts[:, None],
            gain[None],
            doc_sums,
            adapter_up,
            up_states,
            labels[None],
        ]
        + states_b,
        vmem=16 if dp <= 4 else 48,
    )
    losses = losses[:, :per_shard]
    small = sum_over(small, "mp")
    alpha = inv_rms * inv_rms * inv_rms * small[rank, :token_count] / width
    up_states = small[:rank, :token_count]
    up_gained = small[:rank, token_count : token_count + docs]
    mid_grad = (
        inv_rms * dot_nn(up_gained, member_f, highest) - alpha * up_states
    ).astype(jnp.bfloat16)
    mid_t = lora_mid.astype(jnp.float32).T
    a_grad = dot_nn(mid_grad, own_cols)
    mid_alpha = (mid_t * alpha).astype(jnp.bfloat16)
    b_grad = dot_nn(dot_nt(mid_t * inv_rms, member_f, highest), gained, highest) - jnp.concatenate(
        [dot_nn(mid_alpha, x) for x in states_b], axis=1
    )

    grads = jnp.concatenate([a_grad, b_grad, gain_grad], axis=0)
    half = cols // 2
    kept = lax.dynamic_slice_in_dim(grads, side * half, half, 1)
    sent = lax.dynamic_slice_in_dim(grads, (1 - side) * half, half, 1)
    kept = kept + swap(sent, "pair")
    kept = kept.astype(jnp.bfloat16)
    level = [kept] + [partner(kept, "dp", j) for j in range(1, dp)]
    level = [x.astype(jnp.float32) for x in level]
    while len(level) > 1:
        level = [level[i] + level[i + 1] for i in range(0, len(level), 2)]
    total = level[0]
    received = swap(total, "pair")
    grads = jnp.concatenate(
        [jnp.where(side == 0, total, received), jnp.where(side == 0, received, total)], axis=1
    )
    return (
        losses,
        doc_grad[None, None],
        grads[:rank].T,
        grads[rank : 2 * rank],
        grads[2 * rank],
    )


def solution(mesh):
    in_specs = (
        P("pair", ("groups", "dp"), None),
        P("pair", ("groups", "dp"), None),
        P("dp", "mp"),
        P(),
        P(None, "mp"),
        P("mp"),
        P("pair", "groups", None),
        P("pair", "groups", None),
    )
    out_specs = (
        P("pair", ("groups", "dp")),
        P("pair", ("groups", "dp"), None, "mp"),
        P(("groups", "mp"), None),
        P("groups", "mp"),
        P(("groups", "mp")),
    )
    return jax.shard_map(body, mesh=mesh, in_specs=in_specs, out_specs=out_specs, check_vma=False)
```

```python
import functools

import jax
import jax.numpy as jnp
from jax import lax
from jax.experimental import pallas as pl
from jax.experimental.pallas import tpu as pltpu
from jax.sharding import PartitionSpec as P

inverse_temp = 50.0
highest = lax.Precision.HIGHEST
chunk_count = 2


def dot_nt(a, b, precision=None):
    return lax.dot_general(
        a, b, (((1,), (1,)), ((), ())), precision=precision, preferred_element_type=jnp.float32
    )


def dot_nn(a, b, precision=None):
    return jnp.dot(a, b, precision=precision, preferred_element_type=jnp.float32)


def swap(x, axis):
    return lax.ppermute(x, axis, [(0, 1), (1, 0)])


def partner(x, axis, flip):
    return lax.ppermute(x, axis, [(i, i ^ flip) for i in range(lax.axis_size(axis))])


def sum_over(x, axis):
    if lax.axis_size(axis) == 2:
        return x + swap(x, axis)
    return lax.psum(x, axis)


def widths(cols):
    tiles = cols // 128
    base, more = divmod(tiles, chunk_count)
    return [128 * (base + (i >= chunk_count - more)) for i in range(chunk_count)]


def spans(cols):
    out, at = [], 0
    for width in widths(cols):
        out.append((at, at + width))
        at += width
    return out


def after(x, *deps):
    return lax.optimization_barrier((x, *deps))[0]


def call(kernel, outs, args, scratch=(), flops=1 << 24, vmem=16):
    size = sum(a.size * a.dtype.itemsize for a in args)
    return pl.pallas_call(
        kernel,
        out_shape=outs,
        scratch_shapes=list(scratch),
        compiler_params=pltpu.CompilerParams(vmem_limit_bytes=vmem << 20),
        cost_estimate=pl.CostEstimate(flops=flops, bytes_accessed=size, transcendentals=0),
    )(*args)


def as_row(column):
    size = column.shape[0]
    eye = lax.broadcasted_iota(jnp.int32, (size, size), 0) == lax.broadcasted_iota(
        jnp.int32, (size, size), 1
    )
    return jnp.sum(jnp.where(eye, column, 0.0), axis=0, keepdims=True)


def as_column(row):
    size = row.shape[1]
    eye = lax.broadcasted_iota(jnp.int32, (size, size), 0) == lax.broadcasted_iota(
        jnp.int32, (size, size), 1
    )
    return jnp.sum(jnp.where(eye, row, 0.0), axis=1, keepdims=True)


def gram_kernel(blocks, *refs):
    own, oth = refs[:blocks], refs[blocks : 2 * blocks]
    list_ref, out_ref, sorted_ref, own_ref = refs[2 * blocks :]
    docs = own[0].shape[0]
    half = docs // 2
    anchors = blocks * half
    for blocks_of, ref in ((own, own_ref), (oth, sorted_ref)):
        for j in range(blocks):
            ref[j * half : (j + 1) * half] = blocks_of[j][:half]
            ref[anchors + j * half : anchors + (j + 1) * half] = blocks_of[j][half:]
    out_ref[:anchors] = dot_nt(own_ref[:anchors], sorted_ref[:anchors])
    out_ref[anchors : anchors + half] = dot_nt(own_ref[:half], sorted_ref[anchors:])
    pool = dot_nt(own_ref[anchors:], sorted_ref[:anchors])
    pool_id = lax.broadcasted_iota(jnp.int32, pool.shape, 0)
    fanout = list_ref.shape[0]
    rows = []
    for ref in (own_ref, sorted_ref):
        x = ref[...].astype(jnp.float32)
        squares = as_row(jnp.sum(x * x, axis=1, keepdims=True))
        rows += [squares[:, :anchors], squares[:, anchors:]]
    for h in range(fanout):
        listed = pool_id == list_ref[h : h + 1, :]
        rows.append(jnp.sum(jnp.where(listed, pool, 0.0), axis=0, keepdims=True))
    rows.append(jnp.zeros((out_ref.shape[0] - anchors - half - len(rows), anchors), jnp.float32))
    out_ref[anchors + half :] = jnp.concatenate([x for x in rows if x.shape[0]], axis=0)


def pool_kernel(squares_count, chunks, width, *refs):
    squares = refs[0][...]
    for ref in refs[1:squares_count]:
        squares = squares + ref[...]
    state_refs = refs[squares_count : squares_count + chunks]
    labels_ref, gain_ref, counts_ref, sums_ref, pooled_ref, inv_rms_ref = refs[
        squares_count + chunks :
    ]
    inv_rms = lax.rsqrt(squares / width + 1e-05)
    inv_rms_ref[...] = inv_rms
    scale = as_column(inv_rms)
    docs, tokens = counts_ref.shape[0], squares.shape[1]
    doc_id = lax.broadcasted_iota(jnp.int32, (docs, tokens), 0)
    member = jnp.where(doc_id == labels_ref[...], 1.0, 0.0).astype(jnp.bfloat16)
    counts = counts_ref[...]
    for (low, high), state_ref in zip(spans(gain_ref.shape[1]), state_refs):
        tile = 256 if (high - low) % 256 == 0 else 128
        for at in range(0, high - low, tile):
            part = slice(low + at, low + at + tile)
            states = state_ref[:, at : at + tile].astype(jnp.float32)
            normed = (states * scale * gain_ref[:, part]).astype(jnp.bfloat16)
            sums = dot_nn(member, normed)
            sums_ref[:, part] = sums
            pooled_ref[:, part] = (sums / counts).astype(jnp.bfloat16)


def loss_kernel(blocks, sums_count, chunks, *refs):
    sums_refs = refs[:sums_count]
    list_c, list_o, pooled_ref, oth_ref, counts_ref, gain_ref, doc_sums_ref, up_ref = refs[
        sums_count : sums_count + 8
    ]
    up_states_ref, labels_ref = refs[sums_count + 8 : sums_count + 10]
    state_refs = refs[sums_count + 10 : sums_count + 10 + chunks]
    losses_ref, doc_grad_ref, small_ref, gained_ref, gain_grad_ref = refs[
        sums_count + 10 + chunks :
    ]
    docs = pooled_ref.shape[0]
    half = docs // 2
    anchors = blocks * half
    fanout = list_o.shape[1]
    sums = sums_refs[0][...]
    if sums_count == 2:
        sums = sums + sums_refs[1][...]
    inner_a = sums[:anchors]
    inner_o = sums[anchors : anchors + half]
    last = sums[anchors + half :]
    scales = lax.rsqrt(last[:4] + 1e-06)
    own_scale = as_column(scales[0:1])
    own_pool_scale = as_column(scales[1:2])
    oth_scale = scales[2:3]
    pool_scale = scales[3:4]

    row_id = lax.broadcasted_iota(jnp.int32, (anchors, anchors), 0)
    col_id = lax.broadcasted_iota(jnp.int32, (anchors, anchors), 1)
    target = row_id == col_id
    logits_a = inverse_temp * (inner_a * own_scale * oth_scale)
    exp_a = jnp.exp(logits_a)
    total_c = jnp.sum(exp_a, axis=0, keepdims=True)
    listed, exp_n = [], []
    for h in range(fanout):
        listed.append(row_id == list_c[h : h + 1, :])
        scale_n = jnp.sum(jnp.where(listed[h], own_pool_scale, 0.0), axis=0, keepdims=True)
        exp_n.append(jnp.exp(inverse_temp * (last[4 + h : 5 + h] * scale_n * oth_scale)))
        total_c = total_c + exp_n[h]
    losses_ref[...] = jnp.log(total_c) - jnp.sum(
        jnp.where(target, logits_a, 0.0), axis=0, keepdims=True
    )
    target_own = target[:half].astype(jnp.float32)
    grad_c = inverse_temp * (exp_a[:half] / total_c - target_own)
    grad_p = jnp.zeros((half, anchors), jnp.float32)
    inner_p = jnp.zeros((half, anchors), jnp.float32)
    for h in range(fanout):
        mine = listed[h][:half]
        grad_p = grad_p + jnp.where(mine, inverse_temp * (exp_n[h] / total_c), 0.0)
        inner_p = inner_p + jnp.where(mine, last[4 + h : 5 + h], 0.0)

    logits_o = inverse_temp * (inner_o * own_scale[:half] * pool_scale)
    pool_id = col_id[:half]
    mask_o = pool_id == list_o[:, 0:1]
    for h in range(1, fanout):
        mask_o = mask_o | (pool_id == list_o[:, h : h + 1])
    exp_o = jnp.where(mask_o, jnp.exp(logits_o), 0.0)
    total_o = jnp.sum(exp_a[:half], axis=1, keepdims=True) + jnp.sum(exp_o, axis=1, keepdims=True)
    grad_a = inverse_temp * (exp_a[:half] / total_o - target_own)
    grad_o = inverse_temp * (exp_o / total_o)

    zeros = jnp.zeros((docs - half, anchors), jnp.float32)
    coef = jnp.concatenate(
        [
            jnp.concatenate([grad_c + grad_a, grad_p], axis=0) * oth_scale,
            jnp.concatenate([grad_o * pool_scale, zeros], axis=0),
        ],
        axis=1,
    ).astype(jnp.bfloat16)
    inner = jnp.concatenate(
        [
            jnp.concatenate([inner_a[:half], inner_p], axis=0),
            jnp.concatenate([inner_o, zeros], axis=0),
        ],
        axis=1,
    )
    doc_grad = dot_nn(coef, oth_ref[...])
    doc_grad_ref[...] = doc_grad
    scale = jnp.concatenate([own_scale[:half], own_pool_scale[:half]], axis=0)
    unit_dots = jnp.sum(coef.astype(jnp.float32) * inner, axis=1, keepdims=True) * scale
    pooled = pooled_ref[...].astype(jnp.float32)
    per_doc = (doc_grad - pooled * (scale * unit_dots)) * (scale / counts_ref[...])
    gain = gain_ref[...]
    gained = per_doc * gain
    gained_ref[...] = gained
    gain_grad_ref[...] = jnp.sum(per_doc * doc_sums_ref[...], axis=0, keepdims=True) / gain

    gained_b = gained.astype(jnp.bfloat16)
    tok_doc = 0.0
    for (low, high), state_ref in zip(spans(gained_b.shape[1]), state_refs):
        tok_doc = tok_doc + dot_nt(gained_b[:, low:high], state_ref[...])
    tokens = tok_doc.shape[1]
    rank = up_ref.shape[0]
    doc_id = lax.broadcasted_iota(jnp.int32, (docs, tokens), 0)
    tok_dots = jnp.sum(
        jnp.where(doc_id == labels_ref[...], tok_doc, 0.0), axis=0, keepdims=True
    )
    up_gained = dot_nt(up_ref[...].astype(jnp.float32), gained, highest)
    small_ref[...] = jnp.zeros_like(small_ref)
    small_ref[:rank, :tokens] = up_states_ref[...]
    small_ref[:rank, tokens : tokens + docs] = up_gained
    small_ref[rank : rank + 1, :tokens] = tok_dots


def body(
    hidden,
    document_labels,
    frozen_weight,
    adapter_down,
    adapter_up,
    norm_gain_vector,
    negative_owner,
    negative_pool_row,
):
    tokens = hidden[0]
    token_count, width = tokens.shape
    cols = adapter_up.shape[1]
    rank = adapter_up.shape[0]
    dp = lax.axis_size("dp")
    side = lax.axis_index("pair")
    shard = lax.axis_index("dp")
    anchors = negative_owner.shape[1]
    per_shard = anchors // dp
    docs = 2 * per_shard

    order = [0] + list(range(1, dp, 2)) + list(range(dp - 2 + dp % 2, 0, -2))
    hops = [(order[i], order[(i + 1) % dp]) for i in range(dp)]
    back_hops = [(b, a) for a, b in hops]

    def place_of(index):
        return jnp.where(index % 2 == 1, (index + 1) // 2, (dp - index // 2) % dp)

    def shard_at(position):
        return jnp.where(
            position == 0, 0, jnp.where(position <= dp // 2, 2 * position - 1, 2 * (dp - position))
        )

    place = place_of(shard)

    block_shard = shard_at((place - jnp.arange(dp, dtype=jnp.int32)) % dp)
    owner_block = (place - place_of(negative_owner[0])) % dp
    pool_place = owner_block * per_shard + negative_pool_row[0]
    list_c = pool_place.reshape(dp, per_shard, -1)[block_shard].reshape(anchors, -1).T
    list_o = swap(
        lax.dynamic_slice_in_dim(pool_place, shard * per_shard, per_shard, 0), "pair"
    )

    group = lax.axis_index("groups")
    quarter = frozen_weight.shape[0] // 4
    shard_rows = frozen_weight.shape[0]
    parts = spans(cols)
    quarters = [
        (group * 2 + side),
        ((1 - group) * 2 + side),
        (group * 2 + 1 - side),
        ((1 - group) * 2 + 1 - side),
    ]
    moving = []
    for low, high in parts:
        corner = quarters[0] * quarter
        if moving:
            corner = after(corner, moving[0])
        moving.append(lax.dynamic_slice(frozen_weight, (corner, low), (quarter, high - low)))
    lora_mid = dot_nn(tokens, adapter_down).astype(jnp.bfloat16)
    own_cols = lax.dynamic_slice_in_dim(tokens, lax.axis_index("mp") * cols, cols, 1)
    own_tokens = lax.dynamic_slice_in_dim(tokens, shard * shard_rows, shard_rows, 1)
    states = [None] * chunk_count
    ringed = []
    for step in range(1, dp):
        for h in range(chunk_count):
            ringed.append(lax.ppermute(ringed[-chunk_count] if step > 1 else moving[h], "dp", hops))
    event = 0
    for step in range(1, dp):
        origin = shard_at((place - step) % dp)
        step_tokens = jnp.concatenate(
            [
                lax.dynamic_slice_in_dim(tokens, origin * shard_rows + q * quarter, quarter, 1)
                for q in quarters
            ],
            axis=1,
        )
        for h, (low, high) in enumerate(parts):
            moved = ringed[event]
            if step == 1:
                own_first, mid_first = own_tokens, lora_mid
                states[h] = (
                    own_cols[:, low:high].astype(jnp.float32)
                    + dot_nn(own_first, frozen_weight[:, low:high])
                    + dot_nn(mid_first, adapter_up[:, low:high])
                )
                states[h] = lax.optimization_barrier(states[h])
            across = swap(moved, "groups")
            lhs = step_tokens
            late = across
            if step == dp - 1 and h == chunk_count - 1:
                late = after(across, *states)
            rows = [moved, across, swap(moved, "pair"), swap(late, "pair")]
            states[h] = lax.optimization_barrier(
                states[h] + dot_nn(lhs, jnp.concatenate(rows, axis=0))
            )
            event += 1
    states_b = [x.astype(jnp.bfloat16) for x in states]
    squares = sum(jnp.sum(x * x, axis=1) for x in states)

    gain = norm_gain_vector.astype(jnp.float32)
    labels = document_labels[0, 0]
    member = labels[None, :] == jnp.arange(docs, dtype=jnp.int32)[:, None]
    member_f = member.astype(jnp.float32)
    counts = jnp.sum(member_f, axis=1)
    if lax.axis_size("mp") == 2:
        squares = [squares, swap(squares, "mp")]
    else:
        squares = [lax.psum(squares, "mp")]
    doc_sums, pooled, inv_rms = call(
        functools.partial(pool_kernel, len(squares), chunk_count, width),
        (
            jax.ShapeDtypeStruct((docs, cols), jnp.float32),
            jax.ShapeDtypeStruct((docs, cols), jnp.bfloat16),
            jax.ShapeDtypeStruct((1, token_count), jnp.float32),
        ),
        [x[None] for x in squares] + states_b + [labels[None], gain[None], counts[:, None]],
    )
    inv_rms = inv_rms[0]

    own_blocks = [pooled] * dp
    for j in range(1, dp):
        if j <= dp // 2:
            own_blocks[j] = lax.ppermute(own_blocks[j - 1], "dp", hops)
        else:
            own_blocks[dp + dp // 2 - j] = lax.ppermute(
                own_blocks[(dp + dp // 2 - j + 1) % dp], "dp", back_hops
            )
    other_blocks = [swap(block, "pair") for block in own_blocks]
    rows = dp * docs
    last_rows = -(-(4 + list_c.shape[0]) // 8) * 8
    sums, sorted_oth = call(
        functools.partial(gram_kernel, dp),
        (
            jax.ShapeDtypeStruct((anchors + per_shard + last_rows, anchors), jnp.float32),
            jax.ShapeDtypeStruct((rows, cols), jnp.bfloat16),
        ),
        own_blocks + other_blocks + [list_c],
        [pltpu.VMEM((rows, cols), jnp.bfloat16)],
        vmem=16 if dp <= 4 else 48,
    )
    up_parts = [adapter_up[:, low:high] for low, high in parts]
    up_states = sum(dot_nt(u, x) for u, x in zip(up_parts, states_b))
    if lax.axis_size("mp") == 2:
        sums = [sums, swap(sums, "mp")]
    else:
        sums = [lax.psum(sums, "mp")]
    losses, doc_grad, small, gained, gain_grad = call(
        functools.partial(loss_kernel, dp, len(sums), chunk_count),
        (
            jax.ShapeDtypeStruct((1, anchors), jnp.float32),
            jax.ShapeDtypeStruct((docs, cols), jnp.float32),
            jax.ShapeDtypeStruct((rank + 8, token_count + 128), jnp.float32),
            jax.ShapeDtypeStruct((docs, cols), jnp.float32),
            jax.ShapeDtypeStruct((1, cols), jnp.float32),
        ),
        sums
        + [
            list_c,
            list_o,
            pooled,
            sorted_oth,
            counts[:, None],
            gain[None],
            doc_sums,
            adapter_up,
            up_states,
            labels[None],
        ]
        + states_b,
        vmem=16 if dp <= 4 else 48,
    )
    losses = losses[:, :per_shard]
    small = sum_over(small, "mp")
    alpha = inv_rms * inv_rms * inv_rms * small[rank, :token_count] / width
    up_states = small[:rank, :token_count]
    up_gained = small[:rank, token_count : token_count + docs]
    mid_grad = (
        inv_rms * dot_nn(up_gained, member_f, highest) - alpha * up_states
    ).astype(jnp.bfloat16)
    mid_t = lora_mid.astype(jnp.float32).T
    a_grad = dot_nn(mid_grad, own_cols)
    mid_alpha = (mid_t * alpha).astype(jnp.bfloat16)
    b_grad = dot_nn(dot_nt(mid_t * inv_rms, member_f, highest), gained, highest) - jnp.concatenate(
        [dot_nn(mid_alpha, x) for x in states_b], axis=1
    )

    grads = jnp.concatenate([a_grad, b_grad, gain_grad], axis=0)
    half = cols // 2
    kept = lax.dynamic_slice_in_dim(grads, side * half, half, 1)
    sent = lax.dynamic_slice_in_dim(grads, (1 - side) * half, half, 1)
    kept = kept + swap(sent, "pair")
    kept = kept.astype(jnp.bfloat16)
    level = [kept] + [partner(kept, "dp", j) for j in range(1, dp)]
    level = [x.astype(jnp.float32) for x in level]
    while len(level) > 1:
        level = [level[i] + level[i + 1] for i in range(0, len(level), 2)]
    total = level[0]
    received = swap(total, "pair")
    grads = jnp.concatenate(
        [jnp.where(side == 0, total, received), jnp.where(side == 0, received, total)], axis=1
    )
    return (
        losses,
        doc_grad[None, None],
        grads[:rank].T,
        grads[rank : 2 * rank],
        grads[2 * rank],
    )


def solution(mesh):
    in_specs = (
        P("pair", ("groups", "dp"), None),
        P("pair", ("groups", "dp"), None),
        P("dp", "mp"),
        P(),
        P(None, "mp"),
        P("mp"),
        P("pair", "groups", None),
        P("pair", "groups", None),
    )
    out_specs = (
        P("pair", ("groups", "dp")),
        P("pair", ("groups", "dp"), None, "mp"),
        P(("groups", "mp"), None),
        P("groups", "mp"),
        P(("groups", "mp")),
    )
    return jax.shard_map(body, mesh=mesh, in_specs=in_specs, out_specs=out_specs, check_vma=False)
```

```python
import functools

import jax
import jax.numpy as jnp
from jax import lax
from jax.experimental import pallas as pl
from jax.experimental.pallas import tpu as pltpu
from jax.sharding import PartitionSpec as P

inverse_temp = 50.0
highest = lax.Precision.HIGHEST
chunk_count = 2


def dot_nt(a, b, precision=None):
    return lax.dot_general(
        a, b, (((1,), (1,)), ((), ())), precision=precision, preferred_element_type=jnp.float32
    )


def dot_nn(a, b, precision=None):
    return jnp.dot(a, b, precision=precision, preferred_element_type=jnp.float32)


def swap(x, axis):
    return lax.ppermute(x, axis, [(0, 1), (1, 0)])


def partner(x, axis, flip):
    return lax.ppermute(x, axis, [(i, i ^ flip) for i in range(lax.axis_size(axis))])


def sum_over(x, axis):
    if lax.axis_size(axis) == 2:
        return x + swap(x, axis)
    return lax.psum(x, axis)


def widths(cols):
    tiles = cols // 128
    base, more = divmod(tiles, chunk_count)
    return [128 * (base + (i >= chunk_count - more)) for i in range(chunk_count)]


def spans(cols):
    out, at = [], 0
    for width in widths(cols):
        out.append((at, at + width))
        at += width
    return out


def after(x, *deps):
    return lax.optimization_barrier((x, *deps))[0]


def call(kernel, outs, args, scratch=(), flops=1 << 24, vmem=16):
    size = sum(a.size * a.dtype.itemsize for a in args)
    return pl.pallas_call(
        kernel,
        out_shape=outs,
        scratch_shapes=list(scratch),
        compiler_params=pltpu.CompilerParams(vmem_limit_bytes=vmem << 20),
        cost_estimate=pl.CostEstimate(flops=flops, bytes_accessed=size, transcendentals=0),
    )(*args)


def as_row(column):
    size = column.shape[0]
    eye = lax.broadcasted_iota(jnp.int32, (size, size), 0) == lax.broadcasted_iota(
        jnp.int32, (size, size), 1
    )
    return jnp.sum(jnp.where(eye, column, 0.0), axis=0, keepdims=True)


def as_column(row):
    size = row.shape[1]
    eye = lax.broadcasted_iota(jnp.int32, (size, size), 0) == lax.broadcasted_iota(
        jnp.int32, (size, size), 1
    )
    return jnp.sum(jnp.where(eye, row, 0.0), axis=1, keepdims=True)


def gram_kernel(blocks, *refs):
    own, oth = refs[:blocks], refs[blocks : 2 * blocks]
    list_ref, out_ref, sorted_ref, own_ref = refs[2 * blocks :]
    docs = own[0].shape[0]
    half = docs // 2
    anchors = blocks * half
    for blocks_of, ref in ((own, own_ref), (oth, sorted_ref)):
        for j in range(blocks):
            ref[j * half : (j + 1) * half] = blocks_of[j][:half]
            ref[anchors + j * half : anchors + (j + 1) * half] = blocks_of[j][half:]
    out_ref[:anchors] = dot_nt(own_ref[:anchors], sorted_ref[:anchors])
    out_ref[anchors : anchors + half] = dot_nt(own_ref[:half], sorted_ref[anchors:])
    pool = dot_nt(own_ref[anchors:], sorted_ref[:anchors])
    pool_id = lax.broadcasted_iota(jnp.int32, pool.shape, 0)
    fanout = list_ref.shape[0]
    rows = []
    for ref in (own_ref, sorted_ref):
        x = ref[...].astype(jnp.float32)
        squares = as_row(jnp.sum(x * x, axis=1, keepdims=True))
        rows += [squares[:, :anchors], squares[:, anchors:]]
    for h in range(fanout):
        listed = pool_id == list_ref[h : h + 1, :]
        rows.append(jnp.sum(jnp.where(listed, pool, 0.0), axis=0, keepdims=True))
    rows.append(jnp.zeros((out_ref.shape[0] - anchors - half - len(rows), anchors), jnp.float32))
    out_ref[anchors + half :] = jnp.concatenate([x for x in rows if x.shape[0]], axis=0)


def finish_kernel(acc_ref, tokens_ref, *refs):
    rows, (states_ref, squares_ref) = refs[:-2], refs[-2:]
    width = acc_ref.shape[1]
    tile = 256 if width % 256 == 0 else 128
    tokens = tokens_ref[...]
    lanes = jnp.zeros((acc_ref.shape[0], 128), jnp.float32)
    for low in range(0, width, tile):
        part = slice(low, low + tile)
        block = jnp.concatenate([row[:, part] for row in rows], axis=0)
        x = acc_ref[:, part] + dot_nn(tokens, block)
        states_ref[:, part] = x.astype(jnp.bfloat16)
        for at in range(0, tile, 128):
            y = x[:, at : at + 128]
            lanes = lanes + y * y
    squares_ref[...] = dot_nt(jnp.ones((8, 128), jnp.float32), lanes, highest)[:1]


def pool_kernel(squares_count, chunks, width, *refs):
    squares = refs[0][...]
    for ref in refs[1:squares_count]:
        squares = squares + ref[...]
    state_refs = refs[squares_count : squares_count + chunks]
    labels_ref, gain_ref, counts_ref, sums_ref, pooled_ref, inv_rms_ref = refs[
        squares_count + chunks :
    ]
    inv_rms = lax.rsqrt(squares / width + 1e-05)
    inv_rms_ref[...] = inv_rms
    scale = as_column(inv_rms)
    docs, tokens = counts_ref.shape[0], squares.shape[1]
    doc_id = lax.broadcasted_iota(jnp.int32, (docs, tokens), 0)
    member = jnp.where(doc_id == labels_ref[...], 1.0, 0.0).astype(jnp.bfloat16)
    counts = counts_ref[...]
    for (low, high), state_ref in zip(spans(gain_ref.shape[1]), state_refs):
        tile = 256 if (high - low) % 256 == 0 else 128
        for at in range(0, high - low, tile):
            part = slice(low + at, low + at + tile)
            states = state_ref[:, at : at + tile].astype(jnp.float32)
            normed = (states * scale * gain_ref[:, part]).astype(jnp.bfloat16)
            sums = dot_nn(member, normed)
            sums_ref[:, part] = sums
            pooled_ref[:, part] = (sums / counts).astype(jnp.bfloat16)


def loss_kernel(blocks, sums_count, chunks, *refs):
    sums_refs = refs[:sums_count]
    list_c, list_o, pooled_ref, oth_ref, counts_ref, gain_ref, doc_sums_ref, up_ref = refs[
        sums_count : sums_count + 8
    ]
    up_states_ref, labels_ref = refs[sums_count + 8 : sums_count + 10]
    state_refs = refs[sums_count + 10 : sums_count + 10 + chunks]
    losses_ref, doc_grad_ref, small_ref, gained_ref, gain_grad_ref = refs[
        sums_count + 10 + chunks :
    ]
    docs = pooled_ref.shape[0]
    half = docs // 2
    anchors = blocks * half
    fanout = list_o.shape[1]
    sums = sums_refs[0][...]
    if sums_count == 2:
        sums = sums + sums_refs[1][...]
    inner_a = sums[:anchors]
    inner_o = sums[anchors : anchors + half]
    last = sums[anchors + half :]
    scales = lax.rsqrt(last[:4] + 1e-06)
    own_scale = as_column(scales[0:1])
    own_pool_scale = as_column(scales[1:2])
    oth_scale = scales[2:3]
    pool_scale = scales[3:4]

    row_id = lax.broadcasted_iota(jnp.int32, (anchors, anchors), 0)
    col_id = lax.broadcasted_iota(jnp.int32, (anchors, anchors), 1)
    target = row_id == col_id
    logits_a = inverse_temp * (inner_a * own_scale * oth_scale)
    exp_a = jnp.exp(logits_a)
    total_c = jnp.sum(exp_a, axis=0, keepdims=True)
    listed, exp_n = [], []
    for h in range(fanout):
        listed.append(row_id == list_c[h : h + 1, :])
        scale_n = jnp.sum(jnp.where(listed[h], own_pool_scale, 0.0), axis=0, keepdims=True)
        exp_n.append(jnp.exp(inverse_temp * (last[4 + h : 5 + h] * scale_n * oth_scale)))
        total_c = total_c + exp_n[h]
    losses_ref[...] = jnp.log(total_c) - jnp.sum(
        jnp.where(target, logits_a, 0.0), axis=0, keepdims=True
    )
    target_own = target[:half].astype(jnp.float32)
    grad_c = inverse_temp * (exp_a[:half] / total_c - target_own)
    grad_p = jnp.zeros((half, anchors), jnp.float32)
    inner_p = jnp.zeros((half, anchors), jnp.float32)
    for h in range(fanout):
        mine = listed[h][:half]
        grad_p = grad_p + jnp.where(mine, inverse_temp * (exp_n[h] / total_c), 0.0)
        inner_p = inner_p + jnp.where(mine, last[4 + h : 5 + h], 0.0)

    logits_o = inverse_temp * (inner_o * own_scale[:half] * pool_scale)
    pool_id = col_id[:half]
    mask_o = pool_id == list_o[:, 0:1]
    for h in range(1, fanout):
        mask_o = mask_o | (pool_id == list_o[:, h : h + 1])
    exp_o = jnp.where(mask_o, jnp.exp(logits_o), 0.0)
    total_o = jnp.sum(exp_a[:half], axis=1, keepdims=True) + jnp.sum(exp_o, axis=1, keepdims=True)
    grad_a = inverse_temp * (exp_a[:half] / total_o - target_own)
    grad_o = inverse_temp * (exp_o / total_o)

    zeros = jnp.zeros((docs - half, anchors), jnp.float32)
    coef = jnp.concatenate(
        [
            jnp.concatenate([grad_c + grad_a, grad_p], axis=0) * oth_scale,
            jnp.concatenate([grad_o * pool_scale, zeros], axis=0),
        ],
        axis=1,
    ).astype(jnp.bfloat16)
    inner = jnp.concatenate(
        [
            jnp.concatenate([inner_a[:half], inner_p], axis=0),
            jnp.concatenate([inner_o, zeros], axis=0),
        ],
        axis=1,
    )
    doc_grad = dot_nn(coef, oth_ref[...])
    doc_grad_ref[...] = doc_grad
    scale = jnp.concatenate([own_scale[:half], own_pool_scale[:half]], axis=0)
    unit_dots = jnp.sum(coef.astype(jnp.float32) * inner, axis=1, keepdims=True) * scale
    pooled = pooled_ref[...].astype(jnp.float32)
    per_doc = (doc_grad - pooled * (scale * unit_dots)) * (scale / counts_ref[...])
    gain = gain_ref[...]
    gained = per_doc * gain
    gained_ref[...] = gained
    gain_grad_ref[...] = jnp.sum(per_doc * doc_sums_ref[...], axis=0, keepdims=True) / gain

    gained_b = gained.astype(jnp.bfloat16)
    tok_doc = 0.0
    for (low, high), state_ref in zip(spans(gained_b.shape[1]), state_refs):
        tok_doc = tok_doc + dot_nt(gained_b[:, low:high], state_ref[...])
    tokens = tok_doc.shape[1]
    rank = up_ref.shape[0]
    doc_id = lax.broadcasted_iota(jnp.int32, (docs, tokens), 0)
    tok_dots = jnp.sum(
        jnp.where(doc_id == labels_ref[...], tok_doc, 0.0), axis=0, keepdims=True
    )
    up_gained = dot_nt(up_ref[...].astype(jnp.float32), gained, highest)
    small_ref[...] = jnp.zeros_like(small_ref)
    small_ref[:rank, :tokens] = up_states_ref[...]
    small_ref[:rank, tokens : tokens + docs] = up_gained
    small_ref[rank : rank + 1, :tokens] = tok_dots


def body(
    hidden,
    document_labels,
    frozen_weight,
    adapter_down,
    adapter_up,
    norm_gain_vector,
    negative_owner,
    negative_pool_row,
):
    tokens = hidden[0]
    token_count, width = tokens.shape
    cols = adapter_up.shape[1]
    rank = adapter_up.shape[0]
    dp = lax.axis_size("dp")
    side = lax.axis_index("pair")
    shard = lax.axis_index("dp")
    anchors = negative_owner.shape[1]
    per_shard = anchors // dp
    docs = 2 * per_shard

    order = [0] + list(range(1, dp, 2)) + list(range(dp - 2 + dp % 2, 0, -2))
    hops = [(order[i], order[(i + 1) % dp]) for i in range(dp)]
    back_hops = [(b, a) for a, b in hops]

    def place_of(index):
        return jnp.where(index % 2 == 1, (index + 1) // 2, (dp - index // 2) % dp)

    def shard_at(position):
        return jnp.where(
            position == 0, 0, jnp.where(position <= dp // 2, 2 * position - 1, 2 * (dp - position))
        )

    place = place_of(shard)

    block_shard = shard_at((place - jnp.arange(dp, dtype=jnp.int32)) % dp)
    owner_block = (place - place_of(negative_owner[0])) % dp
    pool_place = owner_block * per_shard + negative_pool_row[0]
    list_c = pool_place.reshape(dp, per_shard, -1)[block_shard].reshape(anchors, -1).T
    list_o = swap(
        lax.dynamic_slice_in_dim(pool_place, shard * per_shard, per_shard, 0), "pair"
    )

    group = lax.axis_index("groups")
    quarter = frozen_weight.shape[0] // 4
    shard_rows = frozen_weight.shape[0]
    parts = spans(cols)
    quarters = [
        (group * 2 + side),
        ((1 - group) * 2 + side),
        (group * 2 + 1 - side),
        ((1 - group) * 2 + 1 - side),
    ]
    moving = []
    for low, high in parts:
        corner = quarters[0] * quarter
        if moving:
            corner = after(corner, moving[0])
        moving.append(lax.dynamic_slice(frozen_weight, (corner, low), (quarter, high - low)))
    lora_mid = dot_nn(tokens, adapter_down).astype(jnp.bfloat16)
    own_cols = lax.dynamic_slice_in_dim(tokens, lax.axis_index("mp") * cols, cols, 1)
    own_tokens = lax.dynamic_slice_in_dim(tokens, shard * shard_rows, shard_rows, 1)
    states = [None] * chunk_count
    ringed = []
    for step in range(1, dp):
        for h in range(chunk_count):
            ringed.append(lax.ppermute(ringed[-chunk_count] if step > 1 else moving[h], "dp", hops))
    event = 0
    for step in range(1, dp):
        origin = shard_at((place - step) % dp)
        step_tokens = jnp.concatenate(
            [
                lax.dynamic_slice_in_dim(tokens, origin * shard_rows + q * quarter, quarter, 1)
                for q in quarters
            ],
            axis=1,
        )
        for h, (low, high) in enumerate(parts):
            moved = ringed[event]
            if step == 1:
                own_first, mid_first = own_tokens, lora_mid
                states[h] = (
                    own_cols[:, low:high].astype(jnp.float32)
                    + dot_nn(own_first, frozen_weight[:, low:high])
                    + dot_nn(mid_first, adapter_up[:, low:high])
                )
                states[h] = lax.optimization_barrier(states[h])
            across = swap(moved, "groups")
            lhs = step_tokens
            late = across
            if step == dp - 1 and h == chunk_count - 1:
                late = after(across, *states[:h])
            rows = [moved, across, swap(moved, "pair"), swap(late, "pair")]
            if event < len(ringed) - 1:
                product = dot_nn(lhs, jnp.concatenate(rows, axis=0))
                states[h] = lax.optimization_barrier(states[h] + product)
            else:
                last_states, last_squares = call(
                    finish_kernel,
                    (
                        jax.ShapeDtypeStruct((token_count, high - low), jnp.bfloat16),
                        jax.ShapeDtypeStruct((1, token_count), jnp.float32),
                    ),
                    [states[h], lhs, *rows],
                    flops=1<<24,
                )
            event += 1
    states = states[:-1]
    states_b = [x.astype(jnp.bfloat16) for x in states] + [last_states]
    squares = sum(jnp.sum(x * x, axis=1) for x in states)[None] + last_squares

    gain = norm_gain_vector.astype(jnp.float32)
    labels = document_labels[0, 0]
    member = labels[None, :] == jnp.arange(docs, dtype=jnp.int32)[:, None]
    member_f = member.astype(jnp.float32)
    counts = jnp.sum(member_f, axis=1)
    if lax.axis_size("mp") == 2:
        squares = [squares, swap(squares, "mp")]
    else:
        squares = [lax.psum(squares, "mp")]
    doc_sums, pooled, inv_rms = call(
        functools.partial(pool_kernel, len(squares), chunk_count, width),
        (
            jax.ShapeDtypeStruct((docs, cols), jnp.float32),
            jax.ShapeDtypeStruct((docs, cols), jnp.bfloat16),
            jax.ShapeDtypeStruct((1, token_count), jnp.float32),
        ),
        squares + states_b + [labels[None], gain[None], counts[:, None]],
    )
    inv_rms = inv_rms[0]

    own_blocks = [pooled] * dp
    for j in range(1, dp):
        if j <= dp // 2:
            own_blocks[j] = lax.ppermute(own_blocks[j - 1], "dp", hops)
        else:
            own_blocks[dp + dp // 2 - j] = lax.ppermute(
                own_blocks[(dp + dp // 2 - j + 1) % dp], "dp", back_hops
            )
    other_blocks = [swap(block, "pair") for block in own_blocks]
    rows = dp * docs
    last_rows = -(-(4 + list_c.shape[0]) // 8) * 8
    sums, sorted_oth = call(
        functools.partial(gram_kernel, dp),
        (
            jax.ShapeDtypeStruct((anchors + per_shard + last_rows, anchors), jnp.float32),
            jax.ShapeDtypeStruct((rows, cols), jnp.bfloat16),
        ),
        own_blocks + other_blocks + [list_c],
        [pltpu.VMEM((rows, cols), jnp.bfloat16)],
        vmem=16 if dp <= 4 else 48,
    )
    up_parts = [adapter_up[:, low:high] for low, high in parts]
    up_states = sum(dot_nt(u, x) for u, x in zip(up_parts, states_b))
    if lax.axis_size("mp") == 2:
        sums = [sums, swap(sums, "mp")]
    else:
        sums = [lax.psum(sums, "mp")]
    losses, doc_grad, small, gained, gain_grad = call(
        functools.partial(loss_kernel, dp, len(sums), chunk_count),
        (
            jax.ShapeDtypeStruct((1, anchors), jnp.float32),
            jax.ShapeDtypeStruct((docs, cols), jnp.float32),
            jax.ShapeDtypeStruct((rank + 8, token_count + 128), jnp.float32),
            jax.ShapeDtypeStruct((docs, cols), jnp.float32),
            jax.ShapeDtypeStruct((1, cols), jnp.float32),
        ),
        sums
        + [
            list_c,
            list_o,
            pooled,
            sorted_oth,
            counts[:, None],
            gain[None],
            doc_sums,
            adapter_up,
            up_states,
            labels[None],
        ]
        + states_b,
        vmem=16 if dp <= 4 else 48,
    )
    losses = losses[:, :per_shard]
    small = sum_over(small, "mp")
    alpha = inv_rms * inv_rms * inv_rms * small[rank, :token_count] / width
    up_states = small[:rank, :token_count]
    up_gained = small[:rank, token_count : token_count + docs]
    mid_grad = (
        inv_rms * dot_nn(up_gained, member_f, highest) - alpha * up_states
    ).astype(jnp.bfloat16)
    mid_t = lora_mid.astype(jnp.float32).T
    a_grad = dot_nn(mid_grad, own_cols)
    mid_alpha = (mid_t * alpha).astype(jnp.bfloat16)
    b_grad = dot_nn(dot_nt(mid_t * inv_rms, member_f, highest), gained, highest) - jnp.concatenate(
        [dot_nn(mid_alpha, x) for x in states_b], axis=1
    )

    grads = jnp.concatenate([a_grad, b_grad, gain_grad], axis=0)
    half = cols // 2
    kept = lax.dynamic_slice_in_dim(grads, side * half, half, 1)
    sent = lax.dynamic_slice_in_dim(grads, (1 - side) * half, half, 1)
    kept = kept + swap(sent, "pair")
    kept = kept.astype(jnp.bfloat16)
    level = [kept] + [partner(kept, "dp", j) for j in range(1, dp)]
    level = [x.astype(jnp.float32) for x in level]
    while len(level) > 1:
        level = [level[i] + level[i + 1] for i in range(0, len(level), 2)]
    total = level[0]
    received = swap(total, "pair")
    grads = jnp.concatenate(
        [jnp.where(side == 0, total, received), jnp.where(side == 0, received, total)], axis=1
    )
    return (
        losses,
        doc_grad[None, None],
        grads[:rank].T,
        grads[rank : 2 * rank],
        grads[2 * rank],
    )


def solution(mesh):
    in_specs = (
        P("pair", ("groups", "dp"), None),
        P("pair", ("groups", "dp"), None),
        P("dp", "mp"),
        P(),
        P(None, "mp"),
        P("mp"),
        P("pair", "groups", None),
        P("pair", "groups", None),
    )
    out_specs = (
        P("pair", ("groups", "dp")),
        P("pair", ("groups", "dp"), None, "mp"),
        P(("groups", "mp"), None),
        P("groups", "mp"),
        P(("groups", "mp")),
    )
    return jax.shard_map(body, mesh=mesh, in_specs=in_specs, out_specs=out_specs, check_vma=False)
```

```python
import functools

import jax
import jax.numpy as jnp
from jax import lax
from jax.experimental import pallas as pl
from jax.experimental.pallas import tpu as pltpu
from jax.sharding import PartitionSpec as P

inverse_temp = 50.0
highest = lax.Precision.HIGHEST
chunk_count = 2


def dot_nt(a, b, precision=None):
    return lax.dot_general(
        a, b, (((1,), (1,)), ((), ())), precision=precision, preferred_element_type=jnp.float32
    )


def dot_nn(a, b, precision=None):
    return jnp.dot(a, b, precision=precision, preferred_element_type=jnp.float32)


def swap(x, axis):
    return lax.ppermute(x, axis, [(0, 1), (1, 0)])


def partner(x, axis, flip):
    return lax.ppermute(x, axis, [(i, i ^ flip) for i in range(lax.axis_size(axis))])


def sum_over(x, axis):
    if lax.axis_size(axis) == 2:
        return x + swap(x, axis)
    return lax.psum(x, axis)


def widths(cols):
    tiles = cols // 128
    base, more = divmod(tiles, chunk_count)
    return [128 * (base + (i >= chunk_count - more)) for i in range(chunk_count)]


def spans(cols):
    out, at = [], 0
    for width in widths(cols):
        out.append((at, at + width))
        at += width
    return out


def after(x, *deps):
    return lax.optimization_barrier((x, *deps))[0]


def call(kernel, outs, args, scratch=(), flops=1 << 24, vmem=16, scalar=None):
    size = sum(a.size * a.dtype.itemsize for a in args)
    return pl.pallas_call(
        kernel,
        out_shape=outs,
        scratch_shapes=list(scratch),
        in_specs=[
            pl.BlockSpec(memory_space=pltpu.SMEM if i == scalar else pltpu.VMEM)
            for i in range(len(args))
        ],
        compiler_params=pltpu.CompilerParams(vmem_limit_bytes=vmem << 20),
        cost_estimate=pl.CostEstimate(flops=flops, bytes_accessed=size, transcendentals=0),
    )(*args)


def as_row(column):
    size = column.shape[0]
    eye = lax.broadcasted_iota(jnp.int32, (size, size), 0) == lax.broadcasted_iota(
        jnp.int32, (size, size), 1
    )
    return jnp.sum(jnp.where(eye, column, 0.0), axis=0, keepdims=True)


def as_column(row):
    size = row.shape[1]
    eye = lax.broadcasted_iota(jnp.int32, (size, size), 0) == lax.broadcasted_iota(
        jnp.int32, (size, size), 1
    )
    return jnp.sum(jnp.where(eye, row, 0.0), axis=1, keepdims=True)


def gram_kernel(blocks, *refs):
    own, oth = refs[:blocks], refs[blocks : 2 * blocks]
    list_ref, out_ref, sorted_ref, own_ref = refs[2 * blocks :]
    docs = own[0].shape[0]
    half = docs // 2
    anchors = blocks * half
    for blocks_of, ref in ((own, own_ref), (oth, sorted_ref)):
        for j in range(blocks):
            ref[j * half : (j + 1) * half] = blocks_of[j][:half]
            ref[anchors + j * half : anchors + (j + 1) * half] = blocks_of[j][half:]
    out_ref[:anchors] = dot_nt(own_ref[:anchors], sorted_ref[:anchors])
    out_ref[anchors : anchors + half] = dot_nt(own_ref[:half], sorted_ref[anchors:])
    pool = dot_nt(own_ref[anchors:], sorted_ref[:anchors])
    pool_id = lax.broadcasted_iota(jnp.int32, pool.shape, 0)
    fanout = list_ref.shape[0]
    rows = []
    for ref in (own_ref, sorted_ref):
        x = ref[...].astype(jnp.float32)
        squares = as_row(jnp.sum(x * x, axis=1, keepdims=True))
        rows += [squares[:, :anchors], squares[:, anchors:]]
    for h in range(fanout):
        listed = pool_id == list_ref[h : h + 1, :]
        rows.append(jnp.sum(jnp.where(listed, pool, 0.0), axis=0, keepdims=True))
    rows.append(jnp.zeros((out_ref.shape[0] - anchors - half - len(rows), anchors), jnp.float32))
    out_ref[anchors + half :] = jnp.concatenate([x for x in rows if x.shape[0]], axis=0)


def finish_kernel(acc_ref, tokens_ref, *refs):
    rows, (states_ref, squares_ref) = refs[:-2], refs[-2:]
    width = acc_ref.shape[1]
    tile = 256 if width % 256 == 0 else 128
    tokens = tokens_ref[...]
    lanes = jnp.zeros((acc_ref.shape[0], 128), jnp.float32)
    for low in range(0, width, tile):
        part = slice(low, low + tile)
        block = jnp.concatenate([row[:, part] for row in rows], axis=0)
        x = acc_ref[:, part] + dot_nn(tokens, block)
        states_ref[:, part] = x.astype(jnp.bfloat16)
        for at in range(0, tile, 128):
            y = x[:, at : at + 128]
            lanes = lanes + y * y
    squares_ref[...] = dot_nt(jnp.ones((8, 128), jnp.float32), lanes, highest)[:1]


def pool_kernel(squares_count, chunks, width, *refs):
    squares = refs[0][...]
    for ref in refs[1:squares_count]:
        squares = squares + ref[...]
    state_refs = refs[squares_count : squares_count + chunks]
    labels_ref, gain_ref, counts_ref, sums_ref, pooled_ref, inv_rms_ref = refs[
        squares_count + chunks :
    ]
    inv_rms = lax.rsqrt(squares / width + 1e-05)
    inv_rms_ref[...] = inv_rms
    scale = as_column(inv_rms)
    docs, tokens = counts_ref.shape[0], squares.shape[1]
    doc_id = lax.broadcasted_iota(jnp.int32, (docs, tokens), 0)
    member = jnp.where(doc_id == labels_ref[...], 1.0, 0.0).astype(jnp.bfloat16)
    counts = counts_ref[...]
    for (low, high), state_ref in zip(spans(gain_ref.shape[1]), state_refs):
        tile = 256 if (high - low) % 256 == 0 else 128
        for at in range(0, high - low, tile):
            part = slice(low + at, low + at + tile)
            states = state_ref[:, at : at + tile].astype(jnp.float32)
            normed = (states * scale * gain_ref[:, part]).astype(jnp.bfloat16)
            sums = dot_nn(member, normed)
            sums_ref[:, part] = sums
            pooled_ref[:, part] = (sums / counts).astype(jnp.bfloat16)


def loss_kernel(blocks, sums_count, chunks, *refs):
    sums_refs = refs[:sums_count]
    list_c, list_o, pooled_ref, oth_ref, counts_ref, gain_ref, doc_sums_ref, up_ref = refs[
        sums_count : sums_count + 8
    ]
    up_states_ref, labels_ref = refs[sums_count + 8 : sums_count + 10]
    state_refs = refs[sums_count + 10 : sums_count + 10 + chunks]
    losses_ref, doc_grad_ref, small_ref, gained_ref, gain_grad_ref = refs[
        sums_count + 10 + chunks :
    ]
    docs = pooled_ref.shape[0]
    half = docs // 2
    anchors = blocks * half
    fanout = list_o.shape[1]
    sums = sums_refs[0][...]
    if sums_count == 2:
        sums = sums + sums_refs[1][...]
    inner_a = sums[:anchors]
    inner_o = sums[anchors : anchors + half]
    last = sums[anchors + half :]
    scales = lax.rsqrt(last[:4] + 1e-06)
    own_scale = as_column(scales[0:1])
    own_pool_scale = as_column(scales[1:2])
    oth_scale = scales[2:3]
    pool_scale = scales[3:4]

    row_id = lax.broadcasted_iota(jnp.int32, (anchors, anchors), 0)
    col_id = lax.broadcasted_iota(jnp.int32, (anchors, anchors), 1)
    target = row_id == col_id
    logits_a = inverse_temp * (inner_a * own_scale * oth_scale)
    exp_a = jnp.exp(logits_a)
    total_c = jnp.sum(exp_a, axis=0, keepdims=True)
    listed, exp_n = [], []
    for h in range(fanout):
        listed.append(row_id == list_c[h : h + 1, :])
        scale_n = jnp.sum(jnp.where(listed[h], own_pool_scale, 0.0), axis=0, keepdims=True)
        exp_n.append(jnp.exp(inverse_temp * (last[4 + h : 5 + h] * scale_n * oth_scale)))
        total_c = total_c + exp_n[h]
    losses_ref[...] = jnp.log(total_c) - jnp.sum(
        jnp.where(target, logits_a, 0.0), axis=0, keepdims=True
    )
    target_own = target[:half].astype(jnp.float32)
    grad_c = inverse_temp * (exp_a[:half] / total_c - target_own)
    grad_p = jnp.zeros((half, anchors), jnp.float32)
    inner_p = jnp.zeros((half, anchors), jnp.float32)
    for h in range(fanout):
        mine = listed[h][:half]
        grad_p = grad_p + jnp.where(mine, inverse_temp * (exp_n[h] / total_c), 0.0)
        inner_p = inner_p + jnp.where(mine, last[4 + h : 5 + h], 0.0)

    logits_o = inverse_temp * (inner_o * own_scale[:half] * pool_scale)
    pool_id = col_id[:half]
    mask_o = pool_id == list_o[:, 0:1]
    for h in range(1, fanout):
        mask_o = mask_o | (pool_id == list_o[:, h : h + 1])
    exp_o = jnp.where(mask_o, jnp.exp(logits_o), 0.0)
    total_o = jnp.sum(exp_a[:half], axis=1, keepdims=True) + jnp.sum(exp_o, axis=1, keepdims=True)
    grad_a = inverse_temp * (exp_a[:half] / total_o - target_own)
    grad_o = inverse_temp * (exp_o / total_o)

    zeros = jnp.zeros((docs - half, anchors), jnp.float32)
    coef = jnp.concatenate(
        [
            jnp.concatenate([grad_c + grad_a, grad_p], axis=0) * oth_scale,
            jnp.concatenate([grad_o * pool_scale, zeros], axis=0),
        ],
        axis=1,
    ).astype(jnp.bfloat16)
    inner = jnp.concatenate(
        [
            jnp.concatenate([inner_a[:half], inner_p], axis=0),
            jnp.concatenate([inner_o, zeros], axis=0),
        ],
        axis=1,
    )
    doc_grad = dot_nn(coef, oth_ref[...])
    doc_grad_ref[...] = doc_grad
    scale = jnp.concatenate([own_scale[:half], own_pool_scale[:half]], axis=0)
    unit_dots = jnp.sum(coef.astype(jnp.float32) * inner, axis=1, keepdims=True) * scale
    pooled = pooled_ref[...].astype(jnp.float32)
    per_doc = (doc_grad - pooled * (scale * unit_dots)) * (scale / counts_ref[...])
    gain = gain_ref[...]
    gained = per_doc * gain
    gained_ref[...] = gained
    gain_grad_ref[...] = jnp.sum(per_doc * doc_sums_ref[...], axis=0, keepdims=True) / gain

    gained_b = gained.astype(jnp.bfloat16)
    tok_doc = 0.0
    for (low, high), state_ref in zip(spans(gained_b.shape[1]), state_refs):
        tok_doc = tok_doc + dot_nt(gained_b[:, low:high], state_ref[...])
    tokens = tok_doc.shape[1]
    rank = up_ref.shape[0]
    doc_id = lax.broadcasted_iota(jnp.int32, (docs, tokens), 0)
    tok_dots = jnp.sum(
        jnp.where(doc_id == labels_ref[...], tok_doc, 0.0), axis=0, keepdims=True
    )
    up_gained = dot_nt(up_ref[...].astype(jnp.float32), gained, highest)
    small_ref[...] = jnp.zeros_like(small_ref)
    small_ref[:rank, :tokens] = up_states_ref[...]
    small_ref[:rank, tokens : tokens + docs] = up_gained
    small_ref[rank : rank + 1, :tokens] = tok_dots


def grads_kernel(small_count, chunks, rank, width, *refs):
    small = refs[0][...]
    for ref in refs[1:small_count]:
        small = small + ref[...]
    side_ref, inv_rms_ref, mid_ref, labels_ref, own_cols_ref, gained_ref, gain_grad_ref = refs[
        small_count : small_count + 7
    ]
    state_refs = refs[small_count + 7 : small_count + 7 + chunks]
    kept_ref, sent_ref, grads_ref = refs[small_count + 7 + chunks :]
    tokens = inv_rms_ref.shape[1]
    docs = gained_ref.shape[0]
    doc_id = lax.broadcasted_iota(jnp.int32, (docs, tokens), 0)
    member = jnp.where(doc_id == labels_ref[...], 1.0, 0.0)
    inv_rms = inv_rms_ref[...]
    alpha = inv_rms * inv_rms * inv_rms * small[rank : rank + 1, :tokens] / width
    up_states = small[:rank, :tokens]
    up_gained = small[:rank, tokens : tokens + docs]
    mid_grad = (inv_rms * dot_nn(up_gained, member, highest) - alpha * up_states).astype(
        jnp.bfloat16
    )
    mid = mid_ref[...]
    mid_alpha = (mid * alpha).astype(jnp.bfloat16)
    mid_docs = dot_nt(mid * inv_rms, member, highest)
    grads_ref[:rank] = dot_nn(mid_grad, own_cols_ref[...])
    from_docs = dot_nn(mid_docs, gained_ref[...], highest)
    for (low, high), state_ref in zip(spans(own_cols_ref.shape[1]), state_refs):
        grads_ref[rank : 2 * rank, low:high] = from_docs[:, low:high] - dot_nn(
            mid_alpha, state_ref[...]
        )
    grads_ref[2 * rank :] = jnp.concatenate(
        [gain_grad_ref[...], jnp.zeros((7, own_cols_ref.shape[1]), jnp.float32)], axis=0
    )
    half = kept_ref.shape[1]
    side = side_ref[0]

    @pl.when(side == 0)
    def _():
        kept_ref[...] = grads_ref[:, :half]
        sent_ref[...] = grads_ref[:, half:]

    @pl.when(side != 0)
    def _():
        kept_ref[...] = grads_ref[:, half:]
        sent_ref[...] = grads_ref[:, :half]


def body(
    hidden,
    document_labels,
    frozen_weight,
    adapter_down,
    adapter_up,
    norm_gain_vector,
    negative_owner,
    negative_pool_row,
):
    tokens = hidden[0]
    token_count, width = tokens.shape
    cols = adapter_up.shape[1]
    rank = adapter_up.shape[0]
    dp = lax.axis_size("dp")
    side = lax.axis_index("pair")
    shard = lax.axis_index("dp")
    anchors = negative_owner.shape[1]
    per_shard = anchors // dp
    docs = 2 * per_shard

    order = [0] + list(range(1, dp, 2)) + list(range(dp - 2 + dp % 2, 0, -2))
    hops = [(order[i], order[(i + 1) % dp]) for i in range(dp)]
    back_hops = [(b, a) for a, b in hops]

    def place_of(index):
        return jnp.where(index % 2 == 1, (index + 1) // 2, (dp - index // 2) % dp)

    def shard_at(position):
        return jnp.where(
            position == 0, 0, jnp.where(position <= dp // 2, 2 * position - 1, 2 * (dp - position))
        )

    place = place_of(shard)

    block_shard = shard_at((place - jnp.arange(dp, dtype=jnp.int32)) % dp)
    owner_block = (place - place_of(negative_owner[0])) % dp
    pool_place = owner_block * per_shard + negative_pool_row[0]
    list_c = pool_place.reshape(dp, per_shard, -1)[block_shard].reshape(anchors, -1).T
    list_o = swap(
        lax.dynamic_slice_in_dim(pool_place, shard * per_shard, per_shard, 0), "pair"
    )

    group = lax.axis_index("groups")
    quarter = frozen_weight.shape[0] // 4
    shard_rows = frozen_weight.shape[0]
    parts = spans(cols)
    quarters = [
        (group * 2 + side),
        ((1 - group) * 2 + side),
        (group * 2 + 1 - side),
        ((1 - group) * 2 + 1 - side),
    ]
    moving = []
    for low, high in parts:
        corner = quarters[0] * quarter
        if moving:
            corner = after(corner, moving[0])
        moving.append(lax.dynamic_slice(frozen_weight, (corner, low), (quarter, high - low)))
    lora_mid = dot_nn(tokens, adapter_down).astype(jnp.bfloat16)
    own_cols = lax.dynamic_slice_in_dim(tokens, lax.axis_index("mp") * cols, cols, 1)
    own_tokens = lax.dynamic_slice_in_dim(tokens, shard * shard_rows, shard_rows, 1)
    states = [None] * chunk_count
    ringed = []
    for step in range(1, dp):
        for h in range(chunk_count):
            ringed.append(lax.ppermute(ringed[-chunk_count] if step > 1 else moving[h], "dp", hops))
    event = 0
    for step in range(1, dp):
        origin = shard_at((place - step) % dp)
        step_tokens = jnp.concatenate(
            [
                lax.dynamic_slice_in_dim(tokens, origin * shard_rows + q * quarter, quarter, 1)
                for q in quarters
            ],
            axis=1,
        )
        for h, (low, high) in enumerate(parts):
            moved = ringed[event]
            if step == 1:
                own_first, mid_first = own_tokens, lora_mid
                if h > 0:
                    own_first = after(own_first, ringed[0])
                states[h] = (
                    own_cols[:, low:high].astype(jnp.float32)
                    + dot_nn(own_first, frozen_weight[:, low:high])
                    + dot_nn(mid_first, adapter_up[:, low:high])
                )
                states[h] = lax.optimization_barrier(states[h])
            across = swap(moved, "groups")
            lhs = step_tokens
            late = across
            if step == dp - 1 and h == chunk_count - 1:
                late = after(across, *states[:h])
            rows = [moved, across, swap(moved, "pair"), swap(late, "pair")]
            if event < len(ringed) - 1:
                product = dot_nn(lhs, jnp.concatenate(rows, axis=0))
                states[h] = lax.optimization_barrier(states[h] + product)
            else:
                last_states, last_squares = call(
                    finish_kernel,
                    (
                        jax.ShapeDtypeStruct((token_count, high - low), jnp.bfloat16),
                        jax.ShapeDtypeStruct((1, token_count), jnp.float32),
                    ),
                    [states[h], lhs, *rows],
                    flops=1<<24,
                )
            event += 1
    states = states[:-1]
    states_b = [x.astype(jnp.bfloat16) for x in states] + [last_states]
    squares = sum(jnp.sum(x * x, axis=1) for x in states)[None] + last_squares

    gain = norm_gain_vector.astype(jnp.float32)
    labels = document_labels[0, 0]
    member = labels[None, :] == jnp.arange(docs, dtype=jnp.int32)[:, None]
    member_f = member.astype(jnp.float32)
    counts = jnp.sum(member_f, axis=1)
    if lax.axis_size("mp") == 2:
        squares = [squares, swap(squares, "mp")]
    else:
        squares = [lax.psum(squares, "mp")]
    doc_sums, pooled, inv_rms = call(
        functools.partial(pool_kernel, len(squares), chunk_count, width),
        (
            jax.ShapeDtypeStruct((docs, cols), jnp.float32),
            jax.ShapeDtypeStruct((docs, cols), jnp.bfloat16),
            jax.ShapeDtypeStruct((1, token_count), jnp.float32),
        ),
        squares + states_b + [labels[None], gain[None], counts[:, None]],
    )

    own_blocks = [pooled] * dp
    for j in range(1, dp):
        if j <= dp // 2:
            own_blocks[j] = lax.ppermute(own_blocks[j - 1], "dp", hops)
        else:
            own_blocks[dp + dp // 2 - j] = lax.ppermute(
                own_blocks[(dp + dp // 2 - j + 1) % dp], "dp", back_hops
            )
    other_blocks = [swap(block, "pair") for block in own_blocks]
    rows = dp * docs
    last_rows = -(-(4 + list_c.shape[0]) // 8) * 8
    sums, sorted_oth = call(
        functools.partial(gram_kernel, dp),
        (
            jax.ShapeDtypeStruct((anchors + per_shard + last_rows, anchors), jnp.float32),
            jax.ShapeDtypeStruct((rows, cols), jnp.bfloat16),
        ),
        own_blocks + other_blocks + [list_c],
        [pltpu.VMEM((rows, cols), jnp.bfloat16)],
        vmem=16 if dp <= 4 else 48,
    )
    up_parts = [adapter_up[:, low:high] for low, high in parts]
    up_states = sum(dot_nt(u, x) for u, x in zip(up_parts, states_b))
    if lax.axis_size("mp") == 2:
        sums = [sums, swap(sums, "mp")]
    else:
        sums = [lax.psum(sums, "mp")]
    losses, doc_grad, small, gained, gain_grad = call(
        functools.partial(loss_kernel, dp, len(sums), chunk_count),
        (
            jax.ShapeDtypeStruct((1, anchors), jnp.float32),
            jax.ShapeDtypeStruct((docs, cols), jnp.float32),
            jax.ShapeDtypeStruct((rank + 8, token_count + 128), jnp.float32),
            jax.ShapeDtypeStruct((docs, cols), jnp.float32),
            jax.ShapeDtypeStruct((1, cols), jnp.float32),
        ),
        sums
        + [
            list_c,
            list_o,
            pooled,
            sorted_oth,
            counts[:, None],
            gain[None],
            doc_sums,
            adapter_up,
            up_states,
            labels[None],
        ]
        + states_b,
        vmem=16 if dp <= 4 else 48,
    )
    losses = losses[:, :per_shard]
    if lax.axis_size("mp") == 2:
        small = [small, swap(small, "mp")]
    else:
        small = [lax.psum(small, "mp")]
    half = cols // 2
    kept, sent = call(
        functools.partial(grads_kernel, len(small), chunk_count, rank, width),
        (jax.ShapeDtypeStruct((2 * rank + 8, half), jnp.float32),) * 2,
        small
        + [
            side[None],
            inv_rms,
            lora_mid.astype(jnp.float32).T,
            labels[None],
            own_cols,
            gained,
            gain_grad,
        ]
        + states_b,
        [pltpu.VMEM((2 * rank + 8, cols), jnp.float32)],
        scalar=len(small),
    )
    kept = kept + swap(sent, "pair")
    kept = kept.astype(jnp.bfloat16)
    level = [kept] + [partner(kept, "dp", j) for j in range(1, dp)]
    level = [x.astype(jnp.float32) for x in level]
    while len(level) > 1:
        level = [level[i] + level[i + 1] for i in range(0, len(level), 2)]
    total = level[0]
    received = swap(total, "pair")
    grads = jnp.concatenate(
        [jnp.where(side == 0, total, received), jnp.where(side == 0, received, total)], axis=1
    )
    return (
        losses,
        doc_grad[None, None],
        grads[:rank].T,
        grads[rank : 2 * rank],
        grads[2 * rank],
    )


def solution(mesh):
    in_specs = (
        P("pair", ("groups", "dp"), None),
        P("pair", ("groups", "dp"), None),
        P("dp", "mp"),
        P(),
        P(None, "mp"),
        P("mp"),
        P("pair", "groups", None),
        P("pair", "groups", None),
    )
    out_specs = (
        P("pair", ("groups", "dp")),
        P("pair", ("groups", "dp"), None, "mp"),
        P(("groups", "mp"), None),
        P("groups", "mp"),
        P(("groups", "mp")),
    )
    return jax.shard_map(body, mesh=mesh, in_specs=in_specs, out_specs=out_specs, check_vma=False)
```

```python
import functools

import jax
import jax.numpy as jnp
from jax import lax
from jax.experimental import pallas as pl
from jax.experimental.pallas import tpu as pltpu
from jax.sharding import PartitionSpec as P

inverse_temp = 50.0
highest = lax.Precision.HIGHEST
chunk_count = 2


def dot_nt(a, b, precision=None):
    return lax.dot_general(
        a, b, (((1,), (1,)), ((), ())), precision=precision, preferred_element_type=jnp.float32
    )


def dot_nn(a, b, precision=None):
    return jnp.dot(a, b, precision=precision, preferred_element_type=jnp.float32)


def swap(x, axis):
    return lax.ppermute(x, axis, [(0, 1), (1, 0)])


def partner(x, axis, flip):
    return lax.ppermute(x, axis, [(i, i ^ flip) for i in range(lax.axis_size(axis))])


def sum_over(x, axis):
    if lax.axis_size(axis) == 2:
        return x + swap(x, axis)
    return lax.psum(x, axis)


def widths(cols):
    tiles = cols // 128
    base, more = divmod(tiles, chunk_count)
    return [128 * (base + (i >= chunk_count - more)) for i in range(chunk_count)]


def spans(cols):
    out, at = [], 0
    for width in widths(cols):
        out.append((at, at + width))
        at += width
    return out


def after(x, *deps):
    return lax.optimization_barrier((x, *deps))[0]


def call(kernel, outs, args, scratch=(), flops=1 << 24, vmem=16, scalar=None):
    size = sum(a.size * a.dtype.itemsize for a in args)
    return pl.pallas_call(
        kernel,
        out_shape=outs,
        scratch_shapes=list(scratch),
        in_specs=[
            pl.BlockSpec(memory_space=pltpu.SMEM if i == scalar else pltpu.VMEM)
            for i in range(len(args))
        ],
        compiler_params=pltpu.CompilerParams(vmem_limit_bytes=vmem << 20),
        cost_estimate=pl.CostEstimate(flops=flops, bytes_accessed=size, transcendentals=0),
    )(*args)


def as_row(column):
    size = column.shape[0]
    eye = lax.broadcasted_iota(jnp.int32, (size, size), 0) == lax.broadcasted_iota(
        jnp.int32, (size, size), 1
    )
    return jnp.sum(jnp.where(eye, column, 0.0), axis=0, keepdims=True)


def as_column(row):
    size = row.shape[1]
    eye = lax.broadcasted_iota(jnp.int32, (size, size), 0) == lax.broadcasted_iota(
        jnp.int32, (size, size), 1
    )
    return jnp.sum(jnp.where(eye, row, 0.0), axis=1, keepdims=True)


def gram_kernel(blocks, *refs):
    own, oth = refs[:blocks], refs[blocks : 2 * blocks]
    list_ref, out_ref, sorted_ref, own_ref = refs[2 * blocks :]
    docs = own[0].shape[0]
    half = docs // 2
    anchors = blocks * half
    for blocks_of, ref in ((own, own_ref), (oth, sorted_ref)):
        for j in range(blocks):
            ref[j * half : (j + 1) * half] = blocks_of[j][:half]
            ref[anchors + j * half : anchors + (j + 1) * half] = blocks_of[j][half:]
    out_ref[:anchors] = dot_nt(own_ref[:anchors], sorted_ref[:anchors])
    out_ref[anchors : anchors + half] = dot_nt(own_ref[:half], sorted_ref[anchors:])
    pool = dot_nt(own_ref[anchors:], sorted_ref[:anchors])
    pool_id = lax.broadcasted_iota(jnp.int32, pool.shape, 0)
    fanout = list_ref.shape[0]
    rows = []
    for ref in (own_ref, sorted_ref):
        x = ref[...].astype(jnp.float32)
        squares = as_row(jnp.sum(x * x, axis=1, keepdims=True))
        rows += [squares[:, :anchors], squares[:, anchors:]]
    for h in range(fanout):
        listed = pool_id == list_ref[h : h + 1, :]
        rows.append(jnp.sum(jnp.where(listed, pool, 0.0), axis=0, keepdims=True))
    rows.append(jnp.zeros((out_ref.shape[0] - anchors - half - len(rows), anchors), jnp.float32))
    out_ref[anchors + half :] = jnp.concatenate([x for x in rows if x.shape[0]], axis=0)


def finish_kernel(acc_ref, tokens_ref, *refs):
    rows, (states_ref, squares_ref) = refs[:-2], refs[-2:]
    width = acc_ref.shape[1]
    tile = 256 if width % 256 == 0 else 128
    tokens = tokens_ref[...]
    lanes = jnp.zeros((acc_ref.shape[0], 128), jnp.float32)
    for low in range(0, width, tile):
        part = slice(low, low + tile)
        block = jnp.concatenate([row[:, part] for row in rows], axis=0)
        x = acc_ref[:, part] + dot_nn(tokens, block)
        states_ref[:, part] = x.astype(jnp.bfloat16)
        for at in range(0, tile, 128):
            y = x[:, at : at + 128]
            lanes = lanes + y * y
    squares_ref[...] = dot_nt(jnp.ones((8, 128), jnp.float32), lanes, highest)[:1]


def pool_kernel(squares_count, chunks, width, *refs):
    squares = refs[0][...]
    for ref in refs[1:squares_count]:
        squares = squares + ref[...]
    state_refs = refs[squares_count : squares_count + chunks]
    labels_ref, gain_ref, counts_ref, sums_ref, pooled_ref, inv_rms_ref = refs[
        squares_count + chunks :
    ]
    inv_rms = lax.rsqrt(squares / width + 1e-05)
    inv_rms_ref[...] = inv_rms
    scale = as_column(inv_rms)
    docs, tokens = counts_ref.shape[0], squares.shape[1]
    doc_id = lax.broadcasted_iota(jnp.int32, (docs, tokens), 0)
    member = jnp.where(doc_id == labels_ref[...], 1.0, 0.0).astype(jnp.bfloat16)
    counts = counts_ref[...]
    for (low, high), state_ref in zip(spans(gain_ref.shape[1]), state_refs):
        tile = 256 if (high - low) % 256 == 0 else 128
        for at in range(0, high - low, tile):
            part = slice(low + at, low + at + tile)
            states = state_ref[:, at : at + tile].astype(jnp.float32)
            normed = (states * scale * gain_ref[:, part]).astype(jnp.bfloat16)
            sums = dot_nn(member, normed)
            sums_ref[:, part] = sums
            pooled_ref[:, part] = (sums / counts).astype(jnp.bfloat16)


def loss_kernel(blocks, sums_count, chunks, *refs):
    sums_refs = refs[:sums_count]
    list_c, list_o, pooled_ref, oth_ref, counts_ref, gain_ref, doc_sums_ref, up_ref = refs[
        sums_count : sums_count + 8
    ]
    up_states_ref, labels_ref = refs[sums_count + 8 : sums_count + 10]
    state_refs = refs[sums_count + 10 : sums_count + 10 + chunks]
    losses_ref, doc_grad_ref, small_ref, gained_ref, gain_grad_ref = refs[
        sums_count + 10 + chunks :
    ]
    docs = pooled_ref.shape[0]
    half = docs // 2
    anchors = blocks * half
    fanout = list_o.shape[1]
    sums = sums_refs[0][...]
    if sums_count == 2:
        sums = sums + sums_refs[1][...]
    inner_a = sums[:anchors]
    inner_o = sums[anchors : anchors + half]
    last = sums[anchors + half :]
    scales = lax.rsqrt(last[:4] + 1e-06)
    own_scale = as_column(scales[0:1])
    own_pool_scale = as_column(scales[1:2])
    oth_scale = scales[2:3]
    pool_scale = scales[3:4]

    row_id = lax.broadcasted_iota(jnp.int32, (anchors, anchors), 0)
    col_id = lax.broadcasted_iota(jnp.int32, (anchors, anchors), 1)
    target = row_id == col_id
    logits_a = inverse_temp * (inner_a * own_scale * oth_scale)
    exp_a = jnp.exp(logits_a)
    total_c = jnp.sum(exp_a, axis=0, keepdims=True)
    listed, exp_n = [], []
    for h in range(fanout):
        listed.append(row_id == list_c[h : h + 1, :])
        scale_n = jnp.sum(jnp.where(listed[h], own_pool_scale, 0.0), axis=0, keepdims=True)
        exp_n.append(jnp.exp(inverse_temp * (last[4 + h : 5 + h] * scale_n * oth_scale)))
        total_c = total_c + exp_n[h]
    losses_ref[...] = jnp.log(total_c) - jnp.sum(
        jnp.where(target, logits_a, 0.0), axis=0, keepdims=True
    )
    target_own = target[:half].astype(jnp.float32)
    grad_c = inverse_temp * (exp_a[:half] / total_c - target_own)
    grad_p = jnp.zeros((half, anchors), jnp.float32)
    inner_p = jnp.zeros((half, anchors), jnp.float32)
    for h in range(fanout):
        mine = listed[h][:half]
        grad_p = grad_p + jnp.where(mine, inverse_temp * (exp_n[h] / total_c), 0.0)
        inner_p = inner_p + jnp.where(mine, last[4 + h : 5 + h], 0.0)

    logits_o = inverse_temp * (inner_o * own_scale[:half] * pool_scale)
    pool_id = col_id[:half]
    mask_o = pool_id == list_o[:, 0:1]
    for h in range(1, fanout):
        mask_o = mask_o | (pool_id == list_o[:, h : h + 1])
    exp_o = jnp.where(mask_o, jnp.exp(logits_o), 0.0)
    total_o = jnp.sum(exp_a[:half], axis=1, keepdims=True) + jnp.sum(exp_o, axis=1, keepdims=True)
    grad_a = inverse_temp * (exp_a[:half] / total_o - target_own)
    grad_o = inverse_temp * (exp_o / total_o)

    zeros = jnp.zeros((docs - half, anchors), jnp.float32)
    coef = jnp.concatenate(
        [
            jnp.concatenate([grad_c + grad_a, grad_p], axis=0) * oth_scale,
            jnp.concatenate([grad_o * pool_scale, zeros], axis=0),
        ],
        axis=1,
    ).astype(jnp.bfloat16)
    inner = jnp.concatenate(
        [
            jnp.concatenate([inner_a[:half], inner_p], axis=0),
            jnp.concatenate([inner_o, zeros], axis=0),
        ],
        axis=1,
    )
    doc_grad = dot_nn(coef, oth_ref[...])
    doc_grad_ref[...] = doc_grad
    scale = jnp.concatenate([own_scale[:half], own_pool_scale[:half]], axis=0)
    unit_dots = jnp.sum(coef.astype(jnp.float32) * inner, axis=1, keepdims=True) * scale
    pooled = pooled_ref[...].astype(jnp.float32)
    per_doc = (doc_grad - pooled * (scale * unit_dots)) * (scale / counts_ref[...])
    gain = gain_ref[...]
    gained = per_doc * gain
    gained_ref[...] = gained
    gain_grad_ref[...] = jnp.sum(per_doc * doc_sums_ref[...], axis=0, keepdims=True) / gain

    gained_b = gained.astype(jnp.bfloat16)
    tok_doc = 0.0
    for (low, high), state_ref in zip(spans(gained_b.shape[1]), state_refs):
        tok_doc = tok_doc + dot_nt(gained_b[:, low:high], state_ref[...])
    tokens = tok_doc.shape[1]
    rank = up_ref.shape[0]
    doc_id = lax.broadcasted_iota(jnp.int32, (docs, tokens), 0)
    tok_dots = jnp.sum(
        jnp.where(doc_id == labels_ref[...], tok_doc, 0.0), axis=0, keepdims=True
    )
    up_gained = dot_nt(up_ref[...].astype(jnp.float32), gained, highest)
    small_ref[...] = jnp.zeros_like(small_ref)
    small_ref[:rank, :tokens] = up_states_ref[...]
    small_ref[:rank, tokens : tokens + docs] = up_gained
    small_ref[rank : rank + 1, :tokens] = tok_dots


def grads_kernel(small_count, chunks, rank, width, *refs):
    small = refs[0][...]
    for ref in refs[1:small_count]:
        small = small + ref[...]
    side_ref, inv_rms_ref, mid_ref, labels_ref, own_cols_ref, gained_ref, gain_grad_ref = refs[
        small_count : small_count + 7
    ]
    state_refs = refs[small_count + 7 : small_count + 7 + chunks]
    kept_ref, sent_ref, grads_ref = refs[small_count + 7 + chunks :]
    tokens = inv_rms_ref.shape[1]
    docs = gained_ref.shape[0]
    doc_id = lax.broadcasted_iota(jnp.int32, (docs, tokens), 0)
    member = jnp.where(doc_id == labels_ref[...], 1.0, 0.0)
    inv_rms = inv_rms_ref[...]
    alpha = inv_rms * inv_rms * inv_rms * small[rank : rank + 1, :tokens] / width
    up_states = small[:rank, :tokens]
    up_gained = small[:rank, tokens : tokens + docs]
    mid_grad = (inv_rms * dot_nn(up_gained, member, highest) - alpha * up_states).astype(
        jnp.bfloat16
    )
    mid = mid_ref[...]
    mid_alpha = (mid * alpha).astype(jnp.bfloat16)
    mid_docs = dot_nt(mid * inv_rms, member, highest)
    grads_ref[:rank] = dot_nn(mid_grad, own_cols_ref[...])
    from_docs = dot_nn(mid_docs, gained_ref[...], highest)
    for (low, high), state_ref in zip(spans(own_cols_ref.shape[1]), state_refs):
        grads_ref[rank : 2 * rank, low:high] = from_docs[:, low:high] - dot_nn(
            mid_alpha, state_ref[...]
        )
    grads_ref[2 * rank :] = jnp.concatenate(
        [gain_grad_ref[...], jnp.zeros((7, own_cols_ref.shape[1]), jnp.float32)], axis=0
    )
    half = kept_ref.shape[1]
    side = side_ref[0]

    @pl.when(side == 0)
    def _():
        kept_ref[...] = grads_ref[:, :half]
        sent_ref[...] = grads_ref[:, half:]

    @pl.when(side != 0)
    def _():
        kept_ref[...] = grads_ref[:, half:]
        sent_ref[...] = grads_ref[:, :half]


def body(
    hidden,
    document_labels,
    frozen_weight,
    adapter_down,
    adapter_up,
    norm_gain_vector,
    negative_owner,
    negative_pool_row,
):
    tokens = hidden[0]
    token_count, width = tokens.shape
    cols = adapter_up.shape[1]
    rank = adapter_up.shape[0]
    dp = lax.axis_size("dp")
    side = lax.axis_index("pair")
    shard = lax.axis_index("dp")
    anchors = negative_owner.shape[1]
    per_shard = anchors // dp
    docs = 2 * per_shard

    order = [0] + list(range(1, dp, 2)) + list(range(dp - 2 + dp % 2, 0, -2))
    hops = [(order[i], order[(i + 1) % dp]) for i in range(dp)]
    back_hops = [(b, a) for a, b in hops]

    def place_of(index):
        return jnp.where(index % 2 == 1, (index + 1) // 2, (dp - index // 2) % dp)

    def shard_at(position):
        return jnp.where(
            position == 0, 0, jnp.where(position <= dp // 2, 2 * position - 1, 2 * (dp - position))
        )

    place = place_of(shard)

    block_shard = shard_at((place - jnp.arange(dp, dtype=jnp.int32)) % dp)
    owner_block = (place - place_of(negative_owner[0])) % dp
    pool_place = owner_block * per_shard + negative_pool_row[0]
    list_c = pool_place.reshape(dp, per_shard, -1)[block_shard].reshape(anchors, -1).T
    list_o = swap(
        lax.dynamic_slice_in_dim(pool_place, shard * per_shard, per_shard, 0), "pair"
    )

    group = lax.axis_index("groups")
    quarter = frozen_weight.shape[0] // 4
    shard_rows = frozen_weight.shape[0]
    parts = spans(cols)
    quarters = [
        (group * 2 + side),
        ((1 - group) * 2 + side),
        (group * 2 + 1 - side),
        ((1 - group) * 2 + 1 - side),
    ]
    moving = []
    for low, high in parts:
        corner = quarters[0] * quarter
        if moving:
            corner = after(corner, moving[0])
        moving.append(lax.dynamic_slice(frozen_weight, (corner, low), (quarter, high - low)))
    lora_mid = dot_nn(tokens, adapter_down).astype(jnp.bfloat16)
    own_cols = lax.dynamic_slice_in_dim(tokens, lax.axis_index("mp") * cols, cols, 1)
    own_tokens = lax.dynamic_slice_in_dim(tokens, shard * shard_rows, shard_rows, 1)
    states = [None] * chunk_count
    ringed = []
    for step in range(1, dp):
        for h in range(chunk_count):
            ringed.append(lax.ppermute(ringed[-chunk_count] if step > 1 else moving[h], "dp", hops))
    event = 0
    for step in range(1, dp):
        origin = shard_at((place - step) % dp)
        step_tokens = jnp.concatenate(
            [
                lax.dynamic_slice_in_dim(tokens, origin * shard_rows + q * quarter, quarter, 1)
                for q in quarters
            ],
            axis=1,
        )
        for h, (low, high) in enumerate(parts):
            moved = ringed[event]
            if step == 1:
                own_first, mid_first = own_tokens, lora_mid
                if h > 0:
                    own_first = after(own_first, ringed[0])
                states[h] = (
                    own_cols[:, low:high].astype(jnp.float32)
                    + dot_nn(own_first, frozen_weight[:, low:high])
                    + dot_nn(mid_first, adapter_up[:, low:high])
                )
                states[h] = lax.optimization_barrier(states[h])
            across = swap(moved, "groups")
            lhs = step_tokens
            late = across
            if step == dp - 1 and h == chunk_count - 1:
                late = after(across, *states[:h])
            rows = [moved, across, swap(moved, "pair"), swap(late, "pair")]
            if event < len(ringed) - 1:
                product = dot_nn(lhs, jnp.concatenate(rows, axis=0))
                states[h] = lax.optimization_barrier(states[h] + product)
            else:
                last_states, last_squares = call(
                    finish_kernel,
                    (
                        jax.ShapeDtypeStruct((token_count, high - low), jnp.bfloat16),
                        jax.ShapeDtypeStruct((1, token_count), jnp.float32),
                    ),
                    [states[h], lhs, *rows],
                    flops=1<<24,
                )
            event += 1
    states = states[:-1]
    states_b = [x.astype(jnp.bfloat16) for x in states] + [last_states]
    squares = sum(jnp.sum(x * x, axis=1) for x in states)[None] + last_squares

    gain = norm_gain_vector.astype(jnp.float32)
    labels = document_labels[0, 0]
    member = labels[None, :] == jnp.arange(docs, dtype=jnp.int32)[:, None]
    member_f = member.astype(jnp.float32)
    counts = jnp.sum(member_f, axis=1)
    if lax.axis_size("mp") == 2:
        squares = [squares, swap(squares, "mp")]
    else:
        squares = [lax.psum(squares, "mp")]
    doc_sums, pooled, inv_rms = call(
        functools.partial(pool_kernel, len(squares), chunk_count, width),
        (
            jax.ShapeDtypeStruct((docs, cols), jnp.float32),
            jax.ShapeDtypeStruct((docs, cols), jnp.bfloat16),
            jax.ShapeDtypeStruct((1, token_count), jnp.float32),
        ),
        squares + states_b + [labels[None], gain[None], counts[:, None]],
    )

    first_other = swap(pooled, "pair")
    late_pooled = after(pooled, first_other, list_c)
    own_blocks = [pooled] * dp
    for j in range(1, dp):
        if j <= dp // 2:
            own_blocks[j] = lax.ppermute(own_blocks[j - 1], "dp", hops)
        else:
            at = dp + dp // 2 - j
            source = late_pooled if at == dp - 1 else own_blocks[at + 1]
            own_blocks[at] = lax.ppermute(source, "dp", back_hops)
    other_blocks = [first_other] + [swap(block, "pair") for block in own_blocks[1:]]
    rows = dp * docs
    last_rows = -(-(4 + list_c.shape[0]) // 8) * 8
    sums, sorted_oth = call(
        functools.partial(gram_kernel, dp),
        (
            jax.ShapeDtypeStruct((anchors + per_shard + last_rows, anchors), jnp.float32),
            jax.ShapeDtypeStruct((rows, cols), jnp.bfloat16),
        ),
        own_blocks + other_blocks + [list_c],
        [pltpu.VMEM((rows, cols), jnp.bfloat16)],
        vmem=16 if dp <= 4 else 48,
    )
    up_parts = [adapter_up[:, low:high] for low, high in parts]
    up_states = sum(dot_nt(u, x) for u, x in zip(up_parts, states_b))
    if lax.axis_size("mp") == 2:
        sums = [sums, swap(sums, "mp")]
    else:
        sums = [lax.psum(sums, "mp")]
    losses, doc_grad, small, gained, gain_grad = call(
        functools.partial(loss_kernel, dp, len(sums), chunk_count),
        (
            jax.ShapeDtypeStruct((1, anchors), jnp.float32),
            jax.ShapeDtypeStruct((docs, cols), jnp.float32),
            jax.ShapeDtypeStruct((rank + 8, token_count + 128), jnp.float32),
            jax.ShapeDtypeStruct((docs, cols), jnp.float32),
            jax.ShapeDtypeStruct((1, cols), jnp.float32),
        ),
        sums
        + [
            list_c,
            list_o,
            pooled,
            sorted_oth,
            counts[:, None],
            gain[None],
            doc_sums,
            adapter_up,
            up_states,
            labels[None],
        ]
        + states_b,
        vmem=16 if dp <= 4 else 48,
    )
    losses = losses[:, :per_shard]
    if lax.axis_size("mp") == 2:
        small = [small, swap(small, "mp")]
    else:
        small = [lax.psum(small, "mp")]
    half = cols // 2
    kept, sent = call(
        functools.partial(grads_kernel, len(small), chunk_count, rank, width),
        (jax.ShapeDtypeStruct((2 * rank + 8, half), jnp.float32),) * 2,
        small
        + [
            side[None],
            inv_rms,
            lora_mid.astype(jnp.float32).T,
            labels[None],
            own_cols,
            gained,
            gain_grad,
        ]
        + states_b,
        [pltpu.VMEM((2 * rank + 8, cols), jnp.float32)],
        scalar=len(small),
    )
    kept = kept + swap(sent, "pair")
    kept = kept.astype(jnp.bfloat16)
    level = [kept] + [partner(kept, "dp", j) for j in range(1, dp)]
    level = [x.astype(jnp.float32) for x in level]
    while len(level) > 1:
        level = [level[i] + level[i + 1] for i in range(0, len(level), 2)]
    total = level[0]
    received = swap(total, "pair")
    grads = jnp.concatenate(
        [jnp.where(side == 0, total, received), jnp.where(side == 0, received, total)], axis=1
    )
    return (
        losses,
        doc_grad[None, None],
        grads[:rank].T,
        grads[rank : 2 * rank],
        grads[2 * rank],
    )


def solution(mesh):
    in_specs = (
        P("pair", ("groups", "dp"), None),
        P("pair", ("groups", "dp"), None),
        P("dp", "mp"),
        P(),
        P(None, "mp"),
        P("mp"),
        P("pair", "groups", None),
        P("pair", "groups", None),
    )
    out_specs = (
        P("pair", ("groups", "dp")),
        P("pair", ("groups", "dp"), None, "mp"),
        P(("groups", "mp"), None),
        P("groups", "mp"),
        P(("groups", "mp")),
    )
    return jax.shard_map(body, mesh=mesh, in_specs=in_specs, out_specs=out_specs, check_vma=False)
```

```python
import functools

import jax
import jax.numpy as jnp
from jax import lax
from jax.experimental import pallas as pl
from jax.experimental.pallas import tpu as pltpu
from jax.sharding import PartitionSpec as P

inverse_temp = 50.0
highest = lax.Precision.HIGHEST
chunk_count = 2


def dot_nt(a, b, precision=None):
    return lax.dot_general(
        a, b, (((1,), (1,)), ((), ())), precision=precision, preferred_element_type=jnp.float32
    )


def dot_nn(a, b, precision=None):
    return jnp.dot(a, b, precision=precision, preferred_element_type=jnp.float32)


def swap(x, axis):
    return lax.ppermute(x, axis, [(0, 1), (1, 0)])


def partner(x, axis, flip):
    return lax.ppermute(x, axis, [(i, i ^ flip) for i in range(lax.axis_size(axis))])


def sum_over(x, axis):
    if lax.axis_size(axis) == 2:
        return x + swap(x, axis)
    return lax.psum(x, axis)


def widths(cols):
    tiles = cols // 128
    base, more = divmod(tiles, chunk_count)
    return [128 * (base + (i >= chunk_count - more)) for i in range(chunk_count)]


def spans(cols):
    out, at = [], 0
    for width in widths(cols):
        out.append((at, at + width))
        at += width
    return out


def after(x, *deps):
    return lax.optimization_barrier((x, *deps))[0]


def call(kernel, outs, args, scratch=(), flops=1 << 24, vmem=16, scalar=None):
    size = sum(a.size * a.dtype.itemsize for a in args)
    return pl.pallas_call(
        kernel,
        out_shape=outs,
        scratch_shapes=list(scratch),
        in_specs=[
            pl.BlockSpec(memory_space=pltpu.SMEM if i == scalar else pltpu.VMEM)
            for i in range(len(args))
        ],
        compiler_params=pltpu.CompilerParams(vmem_limit_bytes=vmem << 20),
        cost_estimate=pl.CostEstimate(flops=flops, bytes_accessed=size, transcendentals=0),
    )(*args)


def as_row(column):
    size = column.shape[0]
    eye = lax.broadcasted_iota(jnp.int32, (size, size), 0) == lax.broadcasted_iota(
        jnp.int32, (size, size), 1
    )
    return jnp.sum(jnp.where(eye, column, 0.0), axis=0, keepdims=True)


def as_column(row):
    size = row.shape[1]
    eye = lax.broadcasted_iota(jnp.int32, (size, size), 0) == lax.broadcasted_iota(
        jnp.int32, (size, size), 1
    )
    return jnp.sum(jnp.where(eye, row, 0.0), axis=1, keepdims=True)


def gram_kernel(blocks, *refs):
    own, oth = refs[:blocks], refs[blocks : 2 * blocks]
    list_ref, out_ref, sorted_ref, own_ref = refs[2 * blocks :]
    docs = own[0].shape[0]
    half = docs // 2
    anchors = blocks * half
    for blocks_of, ref in ((own, own_ref), (oth, sorted_ref)):
        for j in range(blocks):
            ref[j * half : (j + 1) * half] = blocks_of[j][:half]
            ref[anchors + j * half : anchors + (j + 1) * half] = blocks_of[j][half:]
    out_ref[:anchors] = dot_nt(own_ref[:anchors], sorted_ref[:anchors])
    out_ref[anchors : anchors + half] = dot_nt(own_ref[:half], sorted_ref[anchors:])
    pool = dot_nt(own_ref[anchors:], sorted_ref[:anchors])
    pool_id = lax.broadcasted_iota(jnp.int32, pool.shape, 0)
    fanout = list_ref.shape[0]
    rows = []
    for ref in (own_ref, sorted_ref):
        x = ref[...].astype(jnp.float32)
        squares = as_row(jnp.sum(x * x, axis=1, keepdims=True))
        rows += [squares[:, :anchors], squares[:, anchors:]]
    for h in range(fanout):
        listed = pool_id == list_ref[h : h + 1, :]
        rows.append(jnp.sum(jnp.where(listed, pool, 0.0), axis=0, keepdims=True))
    rows.append(jnp.zeros((out_ref.shape[0] - anchors - half - len(rows), anchors), jnp.float32))
    out_ref[anchors + half :] = jnp.concatenate([x for x in rows if x.shape[0]], axis=0)


def finish_kernel(acc_ref, tokens_ref, *refs):
    rows, (states_ref, squares_ref) = refs[:-2], refs[-2:]
    width = acc_ref.shape[1]
    tile = 256 if width % 256 == 0 else 128
    tokens = tokens_ref[...]
    lanes = jnp.zeros((acc_ref.shape[0], 128), jnp.float32)
    for low in range(0, width, tile):
        part = slice(low, low + tile)
        block = jnp.concatenate([row[:, part] for row in rows], axis=0)
        x = acc_ref[:, part] + dot_nn(tokens, block)
        states_ref[:, part] = x.astype(jnp.bfloat16)
        for at in range(0, tile, 128):
            y = x[:, at : at + 128]
            lanes = lanes + y * y
    squares_ref[...] = dot_nt(jnp.ones((8, 128), jnp.float32), lanes, highest)[:1]


def pool_kernel(squares_count, chunks, width, *refs):
    squares = refs[0][...]
    for ref in refs[1:squares_count]:
        squares = squares + ref[...]
    state_refs = refs[squares_count : squares_count + chunks]
    labels_ref, gain_ref, counts_ref, sums_ref, pooled_ref, inv_rms_ref = refs[
        squares_count + chunks :
    ]
    inv_rms = lax.rsqrt(squares / width + 1e-05)
    inv_rms_ref[...] = inv_rms
    scale = as_column(inv_rms)
    docs, tokens = counts_ref.shape[0], squares.shape[1]
    doc_id = lax.broadcasted_iota(jnp.int32, (docs, tokens), 0)
    member = jnp.where(doc_id == labels_ref[...], 1.0, 0.0).astype(jnp.bfloat16)
    counts = counts_ref[...]
    for (low, high), state_ref in zip(spans(gain_ref.shape[1]), state_refs):
        tile = 256 if (high - low) % 256 == 0 else 128
        for at in range(0, high - low, tile):
            part = slice(low + at, low + at + tile)
            states = state_ref[:, at : at + tile].astype(jnp.float32)
            normed = (states * scale * gain_ref[:, part]).astype(jnp.bfloat16)
            sums = dot_nn(member, normed)
            sums_ref[:, part] = sums
            pooled_ref[:, part] = (sums / counts).astype(jnp.bfloat16)


def loss_kernel(blocks, sums_count, chunks, *refs):
    sums_refs = refs[:sums_count]
    list_c, list_o, pooled_ref, oth_ref, counts_ref, gain_ref, doc_sums_ref, up_ref = refs[
        sums_count : sums_count + 8
    ]
    labels_ref = refs[sums_count + 8]
    state_refs = refs[sums_count + 9 : sums_count + 9 + chunks]
    losses_ref, doc_grad_ref, small_ref, gained_ref, gain_grad_ref = refs[
        sums_count + 9 + chunks :
    ]
    docs = pooled_ref.shape[0]
    half = docs // 2
    anchors = blocks * half
    fanout = list_o.shape[1]
    sums = sums_refs[0][...]
    if sums_count == 2:
        sums = sums + sums_refs[1][...]
    inner_a = sums[:anchors]
    inner_o = sums[anchors : anchors + half]
    last = sums[anchors + half :]
    scales = lax.rsqrt(last[:4] + 1e-06)
    own_scale = as_column(scales[0:1])
    own_pool_scale = as_column(scales[1:2])
    oth_scale = scales[2:3]
    pool_scale = scales[3:4]

    row_id = lax.broadcasted_iota(jnp.int32, (anchors, anchors), 0)
    col_id = lax.broadcasted_iota(jnp.int32, (anchors, anchors), 1)
    target = row_id == col_id
    logits_a = inverse_temp * (inner_a * own_scale * oth_scale)
    exp_a = jnp.exp(logits_a)
    total_c = jnp.sum(exp_a, axis=0, keepdims=True)
    listed, exp_n = [], []
    for h in range(fanout):
        listed.append(row_id == list_c[h : h + 1, :])
        scale_n = jnp.sum(jnp.where(listed[h], own_pool_scale, 0.0), axis=0, keepdims=True)
        exp_n.append(jnp.exp(inverse_temp * (last[4 + h : 5 + h] * scale_n * oth_scale)))
        total_c = total_c + exp_n[h]
    losses_ref[...] = jnp.log(total_c) - jnp.sum(
        jnp.where(target, logits_a, 0.0), axis=0, keepdims=True
    )
    target_own = target[:half].astype(jnp.float32)
    grad_c = inverse_temp * (exp_a[:half] / total_c - target_own)
    grad_p = jnp.zeros((half, anchors), jnp.float32)
    inner_p = jnp.zeros((half, anchors), jnp.float32)
    for h in range(fanout):
        mine = listed[h][:half]
        grad_p = grad_p + jnp.where(mine, inverse_temp * (exp_n[h] / total_c), 0.0)
        inner_p = inner_p + jnp.where(mine, last[4 + h : 5 + h], 0.0)

    logits_o = inverse_temp * (inner_o * own_scale[:half] * pool_scale)
    pool_id = col_id[:half]
    mask_o = pool_id == list_o[:, 0:1]
    for h in range(1, fanout):
        mask_o = mask_o | (pool_id == list_o[:, h : h + 1])
    exp_o = jnp.where(mask_o, jnp.exp(logits_o), 0.0)
    total_o = jnp.sum(exp_a[:half], axis=1, keepdims=True) + jnp.sum(exp_o, axis=1, keepdims=True)
    grad_a = inverse_temp * (exp_a[:half] / total_o - target_own)
    grad_o = inverse_temp * (exp_o / total_o)

    zeros = jnp.zeros((docs - half, anchors), jnp.float32)
    coef = jnp.concatenate(
        [
            jnp.concatenate([grad_c + grad_a, grad_p], axis=0) * oth_scale,
            jnp.concatenate([grad_o * pool_scale, zeros], axis=0),
        ],
        axis=1,
    ).astype(jnp.bfloat16)
    inner = jnp.concatenate(
        [
            jnp.concatenate([inner_a[:half], inner_p], axis=0),
            jnp.concatenate([inner_o, zeros], axis=0),
        ],
        axis=1,
    )
    doc_grad = dot_nn(coef, oth_ref[...])
    doc_grad_ref[...] = doc_grad
    scale = jnp.concatenate([own_scale[:half], own_pool_scale[:half]], axis=0)
    unit_dots = jnp.sum(coef.astype(jnp.float32) * inner, axis=1, keepdims=True) * scale
    pooled = pooled_ref[...].astype(jnp.float32)
    per_doc = (doc_grad - pooled * (scale * unit_dots)) * (scale / counts_ref[...])
    gain = gain_ref[...]
    gained = per_doc * gain
    gained_ref[...] = gained
    gain_grad_ref[...] = jnp.sum(per_doc * doc_sums_ref[...], axis=0, keepdims=True) / gain

    gained_b = gained.astype(jnp.bfloat16)
    tok_doc = 0.0
    for (low, high), state_ref in zip(spans(gained_b.shape[1]), state_refs):
        tok_doc = tok_doc + dot_nt(gained_b[:, low:high], state_ref[...])
    tokens = tok_doc.shape[1]
    rank = up_ref.shape[0]
    doc_id = lax.broadcasted_iota(jnp.int32, (docs, tokens), 0)
    tok_dots = jnp.sum(
        jnp.where(doc_id == labels_ref[...], tok_doc, 0.0), axis=0, keepdims=True
    )
    up_gained = dot_nt(up_ref[...].astype(jnp.float32), gained, highest)
    small_ref[...] = jnp.zeros_like(small_ref)
    small_ref[:rank, :docs] = up_gained
    for i in range(tokens // 128):
        small_ref[rank + i : rank + i + 1] = tok_dots[:, i * 128 : (i + 1) * 128]


def grads_kernel(small_count, chunks, rank, width, *refs):
    small = refs[0][...]
    for ref in refs[1:small_count]:
        small = small + ref[...]
    side_ref, inv_rms_ref, mid_ref, labels_ref, own_cols_ref, gained_ref, gain_grad_ref = refs[
        small_count : small_count + 7
    ]
    up_states_ref = refs[small_count + 7]
    state_refs = refs[small_count + 8 : small_count + 8 + chunks]
    kept_ref, sent_ref, grads_ref = refs[small_count + 8 + chunks :]
    tokens = inv_rms_ref.shape[1]
    docs = gained_ref.shape[0]
    doc_id = lax.broadcasted_iota(jnp.int32, (docs, tokens), 0)
    member = jnp.where(doc_id == labels_ref[...], 1.0, 0.0)
    inv_rms = inv_rms_ref[...]
    tok_dots = jnp.concatenate(
        [small[rank + i : rank + i + 1] for i in range(tokens // 128)], axis=1
    )
    alpha = inv_rms * inv_rms * inv_rms * tok_dots / width
    up_states = up_states_ref[...]
    up_gained = small[:rank, :docs]
    mid_grad = (inv_rms * dot_nn(up_gained, member, highest) - alpha * up_states).astype(
        jnp.bfloat16
    )
    mid = mid_ref[...]
    mid_alpha = (mid * alpha).astype(jnp.bfloat16)
    mid_docs = dot_nt(mid * inv_rms, member, highest)
    grads_ref[:rank] = dot_nn(mid_grad, own_cols_ref[...])
    from_docs = dot_nn(mid_docs, gained_ref[...], highest)
    for (low, high), state_ref in zip(spans(own_cols_ref.shape[1]), state_refs):
        grads_ref[rank : 2 * rank, low:high] = from_docs[:, low:high] - dot_nn(
            mid_alpha, state_ref[...]
        )
    grads_ref[2 * rank :] = jnp.concatenate(
        [gain_grad_ref[...], jnp.zeros((7, own_cols_ref.shape[1]), jnp.float32)], axis=0
    )
    half = kept_ref.shape[1]
    side = side_ref[0]

    @pl.when(side == 0)
    def _():
        kept_ref[...] = grads_ref[:, :half]
        sent_ref[...] = grads_ref[:, half:]

    @pl.when(side != 0)
    def _():
        kept_ref[...] = grads_ref[:, half:]
        sent_ref[...] = grads_ref[:, :half]


def body(
    hidden,
    document_labels,
    frozen_weight,
    adapter_down,
    adapter_up,
    norm_gain_vector,
    negative_owner,
    negative_pool_row,
):
    tokens = hidden[0]
    token_count, width = tokens.shape
    cols = adapter_up.shape[1]
    rank = adapter_up.shape[0]
    dp = lax.axis_size("dp")
    side = lax.axis_index("pair")
    shard = lax.axis_index("dp")
    anchors = negative_owner.shape[1]
    per_shard = anchors // dp
    docs = 2 * per_shard

    order = [0] + list(range(1, dp, 2)) + list(range(dp - 2 + dp % 2, 0, -2))
    hops = [(order[i], order[(i + 1) % dp]) for i in range(dp)]
    back_hops = [(b, a) for a, b in hops]

    def place_of(index):
        return jnp.where(index % 2 == 1, (index + 1) // 2, (dp - index // 2) % dp)

    def shard_at(position):
        return jnp.where(
            position == 0, 0, jnp.where(position <= dp // 2, 2 * position - 1, 2 * (dp - position))
        )

    place = place_of(shard)

    block_shard = shard_at((place - jnp.arange(dp, dtype=jnp.int32)) % dp)
    owner_block = (place - place_of(negative_owner[0])) % dp
    pool_place = owner_block * per_shard + negative_pool_row[0]
    list_c = pool_place.reshape(dp, per_shard, -1)[block_shard].reshape(anchors, -1).T
    list_o = swap(
        lax.dynamic_slice_in_dim(pool_place, shard * per_shard, per_shard, 0), "pair"
    )

    group = lax.axis_index("groups")
    quarter = frozen_weight.shape[0] // 4
    shard_rows = frozen_weight.shape[0]
    parts = spans(cols)
    quarters = [
        (group * 2 + side),
        ((1 - group) * 2 + side),
        (group * 2 + 1 - side),
        ((1 - group) * 2 + 1 - side),
    ]
    moving = []
    for low, high in parts:
        corner = quarters[0] * quarter
        if moving:
            corner = after(corner, moving[0])
        moving.append(lax.dynamic_slice(frozen_weight, (corner, low), (quarter, high - low)))
    lora_mid = dot_nn(tokens, adapter_down).astype(jnp.bfloat16)
    own_cols = lax.dynamic_slice_in_dim(tokens, lax.axis_index("mp") * cols, cols, 1)
    own_tokens = lax.dynamic_slice_in_dim(tokens, shard * shard_rows, shard_rows, 1)
    states = [None] * chunk_count
    ringed = []
    for step in range(1, dp):
        for h in range(chunk_count):
            ringed.append(lax.ppermute(ringed[-chunk_count] if step > 1 else moving[h], "dp", hops))
    event = 0
    for step in range(1, dp):
        origin = shard_at((place - step) % dp)
        step_tokens = jnp.concatenate(
            [
                lax.dynamic_slice_in_dim(tokens, origin * shard_rows + q * quarter, quarter, 1)
                for q in quarters
            ],
            axis=1,
        )
        for h, (low, high) in enumerate(parts):
            moved = ringed[event]
            if step == 1:
                own_first, mid_first = own_tokens, lora_mid
                if h > 0:
                    own_first = after(own_first, ringed[0])
                states[h] = (
                    own_cols[:, low:high].astype(jnp.float32)
                    + dot_nn(own_first, frozen_weight[:, low:high])
                    + dot_nn(mid_first, adapter_up[:, low:high])
                )
                states[h] = lax.optimization_barrier(states[h])
            across = swap(moved, "groups")
            lhs = step_tokens
            late = across
            if step == dp - 1 and h == chunk_count - 1:
                late = after(across, *states[:h])
            rows = [moved, across, swap(moved, "pair"), swap(late, "pair")]
            if event < len(ringed) - 1:
                product = dot_nn(lhs, jnp.concatenate(rows, axis=0))
                states[h] = lax.optimization_barrier(states[h] + product)
            else:
                last_states, last_squares = call(
                    finish_kernel,
                    (
                        jax.ShapeDtypeStruct((token_count, high - low), jnp.bfloat16),
                        jax.ShapeDtypeStruct((1, token_count), jnp.float32),
                    ),
                    [states[h], lhs, *rows],
                    flops=1<<24,
                )
            event += 1
    states = states[:-1]
    states_b = [x.astype(jnp.bfloat16) for x in states] + [last_states]
    squares = sum(jnp.sum(x * x, axis=1) for x in states)[None] + last_squares

    gain = norm_gain_vector.astype(jnp.float32)
    labels = document_labels[0, 0]
    member = labels[None, :] == jnp.arange(docs, dtype=jnp.int32)[:, None]
    member_f = member.astype(jnp.float32)
    counts = jnp.sum(member_f, axis=1)
    if lax.axis_size("mp") == 2:
        squares = [squares, swap(squares, "mp")]
    else:
        squares = [lax.psum(squares, "mp")]
    doc_sums, pooled, inv_rms = call(
        functools.partial(pool_kernel, len(squares), chunk_count, width),
        (
            jax.ShapeDtypeStruct((docs, cols), jnp.float32),
            jax.ShapeDtypeStruct((docs, cols), jnp.bfloat16),
            jax.ShapeDtypeStruct((1, token_count), jnp.float32),
        ),
        squares + states_b + [labels[None], gain[None], counts[:, None]],
    )

    up_parts = [adapter_up[:, low:high] for low, high in parts]
    up_states = sum(dot_nt(u, x) for u, x in zip(up_parts, states_b))
    up_states = sum_over(up_states, "mp")
    first_other = swap(pooled, "pair")
    late_pooled = after(pooled, first_other, list_c)
    own_blocks = [pooled] * dp
    for j in range(1, dp):
        if j <= dp // 2:
            own_blocks[j] = lax.ppermute(own_blocks[j - 1], "dp", hops)
        else:
            at = dp + dp // 2 - j
            source = late_pooled if at == dp - 1 else own_blocks[at + 1]
            own_blocks[at] = lax.ppermute(source, "dp", back_hops)
    other_blocks = [first_other] + [swap(block, "pair") for block in own_blocks[1:]]
    rows = dp * docs
    last_rows = -(-(4 + list_c.shape[0]) // 8) * 8
    sums, sorted_oth = call(
        functools.partial(gram_kernel, dp),
        (
            jax.ShapeDtypeStruct((anchors + per_shard + last_rows, anchors), jnp.float32),
            jax.ShapeDtypeStruct((rows, cols), jnp.bfloat16),
        ),
        own_blocks + other_blocks + [list_c],
        [pltpu.VMEM((rows, cols), jnp.bfloat16)],
        vmem=16 if dp <= 4 else 48,
    )
    if lax.axis_size("mp") == 2:
        sums = [sums, swap(sums, "mp")]
    else:
        sums = [lax.psum(sums, "mp")]
    losses, doc_grad, small, gained, gain_grad = call(
        functools.partial(loss_kernel, dp, len(sums), chunk_count),
        (
            jax.ShapeDtypeStruct((1, anchors), jnp.float32),
            jax.ShapeDtypeStruct((docs, cols), jnp.float32),
            jax.ShapeDtypeStruct((rank + -(-token_count // 1024) * 8, 128), jnp.float32),
            jax.ShapeDtypeStruct((docs, cols), jnp.float32),
            jax.ShapeDtypeStruct((1, cols), jnp.float32),
        ),
        sums
        + [
            list_c,
            list_o,
            pooled,
            sorted_oth,
            counts[:, None],
            gain[None],
            doc_sums,
            adapter_up,
            labels[None],
        ]
        + states_b,
        vmem=16 if dp <= 4 else 48,
    )
    losses = losses[:, :per_shard]
    if lax.axis_size("mp") == 2:
        small = [small, swap(small, "mp")]
    else:
        small = [lax.psum(small, "mp")]
    half = cols // 2
    kept, sent = call(
        functools.partial(grads_kernel, len(small), chunk_count, rank, width),
        (jax.ShapeDtypeStruct((2 * rank + 8, half), jnp.float32),) * 2,
        small
        + [
            side[None],
            inv_rms,
            lora_mid.astype(jnp.float32).T,
            labels[None],
            own_cols,
            gained,
            gain_grad,
            up_states,
        ]
        + states_b,
        [pltpu.VMEM((2 * rank + 8, cols), jnp.float32)],
        scalar=len(small),
    )
    kept = kept + swap(sent, "pair")
    kept = kept.astype(jnp.bfloat16)
    level = [kept] + [partner(kept, "dp", j) for j in range(1, dp)]
    level = [x.astype(jnp.float32) for x in level]
    while len(level) > 1:
        level = [level[i] + level[i + 1] for i in range(0, len(level), 2)]
    total = level[0]
    received = swap(total, "pair")
    grads = jnp.concatenate(
        [jnp.where(side == 0, total, received), jnp.where(side == 0, received, total)], axis=1
    )
    return (
        losses,
        doc_grad[None, None],
        grads[:rank].T,
        grads[rank : 2 * rank],
        grads[2 * rank],
    )


def solution(mesh):
    in_specs = (
        P("pair", ("groups", "dp"), None),
        P("pair", ("groups", "dp"), None),
        P("dp", "mp"),
        P(),
        P(None, "mp"),
        P("mp"),
        P("pair", "groups", None),
        P("pair", "groups", None),
    )
    out_specs = (
        P("pair", ("groups", "dp")),
        P("pair", ("groups", "dp"), None, "mp"),
        P(("groups", "mp"), None),
        P("groups", "mp"),
        P(("groups", "mp")),
    )
    return jax.shard_map(body, mesh=mesh, in_specs=in_specs, out_specs=out_specs, check_vma=False)
```
